32 devices in a mesh: dp: 16 (over z, y, core), tensor: 2 (over x).
Axes of the slice: x: 2, y: 2, z: 4, core: 2. Of those that a mesh axis runs over, the one named last changes fastest.
Arguments:
- tokens: bfloat16 [8192, 1152], P(('dp', 'tensor')), may hold values from -6 to 6
- condition: bfloat16 [32, 1152], P(('dp', 'tensor')), may hold values from -6 to 6
- grid_shape: int32 [32, 2], P('dp'), may hold values from 8 to 16, as said below
- w_ada: bfloat16 [1152, 6912], replicated, may hold values from -0.1875 to 0.1875
- b_ada: bfloat16 [6912], replicated, may hold values from -3 to 3
- w_qkv: bfloat16 [1152, 3, 1152], P(None, None, 'tensor'), may hold values from -0.1875 to 0.1875
- w_out: bfloat16 [1152, 1152], P('tensor'), may hold values from -1 to 1
- w_gate_up: bfloat16 [1152, 2, 3072], P(None, None, 'tensor'), may hold values from -0.1875 to 0.1875
- w_down: bfloat16 [3072, 1152], P('tensor'), may hold values from -0.21875 to 0.21875
- cotangent: bfloat16 [8192, 1152], P(('dp', 'tensor')), may hold values from -6 to 6
Outputs:
- layer_out: bfloat16 [8192, 1152], P(('dp', 'tensor'))
- d_tokens: float32 [8192, 1152], P(('dp', 'tensor'))
- d_condition: float32 [32, 1152], P(('dp', 'tensor'))
- grad_ada: float32 [1152, 6912], P(None, ('dp', 'tensor'))
- grad_ada_bias: float32 [6912], P(('dp', 'tensor'))
- grad_qkv: float32 [1152, 3, 1152], P('dp', None, 'tensor')
- grad_out: float32 [1152, 1152], P('tensor', 'dp')
- grad_gate_up: float32 [1152, 2, 3072], P('dp', None, 'tensor')
- grad_down: float32 [3072, 1152], P('tensor', 'dp')
The draws below stay inside these ranges and needn't reach their ends.
Inputs may be any that keep to these rules, and one draw needn't show every extreme that they name: `grid_shape`: each image's patch grid has half of 16 to 16 rows and as many columns, drawn independently; in every draw some image is 16 by 16. An image's valid tokens are the first rows times columns of its 256 slots, row by row.
All inputs are finite; a program needn't handle non-finite values.
Results may differ from the reference program's by a relative error of at most 0.029.
The reference program's roundings to bfloat16 on the way count: a program that leaves them out, or rounds other values in their place, can miss the bound.
Values may be sent and summed in bfloat16 or wider, within the bound.
A program may use at most 192 MiB of HBM per device.

```python
from functools import partial
import jax
import jax.numpy as jnp
from jax import lax

D = 1152
HEADS = 16
HD = 72
FF = 3072
SIDE = 16
LEN = 256
IMAGES = 32
TOKENS = 8192


def draw_grid_shape(key, part):
    key_sides, key_full = jax.random.split(key)
    sides = jax.random.randint(key_sides, (IMAGES, 2), SIDE // 2, SIDE + 1)
    full_image = jax.random.randint(key_full, (), 0, IMAGES)
    image_rows = jnp.arange(IMAGES)[:, None]
    return jnp.where(image_rows == full_image, SIDE, sides).astype(jnp.int32)


def strengthened(drawn, stream_key, source, target, blocks, factor):
    def block_of(axis_at):
        return (jnp.arange(drawn.shape[axis_at]) // (drawn.shape[axis_at] // blocks)).reshape((-1,) + (1,) * (drawn.ndim - 1 - axis_at))

    near = jax.random.permutation(stream_key, blocks)[block_of(target)]
    second = (block_of(target) + blocks // 2) % blocks
    return jnp.where((block_of(source) == near) | (block_of(source) == second), factor * drawn, drawn)


def steps_of(key, shape, shards, low, top_value):
    gain, own = 1.0, jax.random.fold_in(key, 6)
    for dim, parts in shards:
        draws = jnp.exp(jax.random.uniform(jax.random.fold_in(own, dim), (parts,), jnp.float32, low / len(shards), top_value / len(shards)))
        gain = gain * jnp.repeat(draws, shape[dim] // parts).reshape([-1 if axis == dim else 1 for axis in range(len(shape))])
    return gain


def gaussian(own_key, shape, scale, bound, pieces=(), held_as=jnp.bfloat16):
    gain = steps_of(own_key, shape, pieces, -0.22, 0.18) if pieces else 1.0
    entries = jax.random.normal(own_key, shape, jnp.float32) * scale * gain
    return jnp.minimum(jnp.maximum(entries, -bound), bound).astype(held_as)


def noise_with(rng, shape, width, most, shards, heavy, kind=jnp.bfloat16):
    array = width * jax.random.normal(rng, shape, jnp.float32)
    if shards:
        array = array * steps_of(rng, shape, shards, -0.22, 0.18)
    return jnp.clip(strengthened(array, jax.random.fold_in(rng, 3), *heavy), -most, most).astype(kind)


def setup_inputs(seed: int = 0) -> dict:
    keys = jax.random.split(jax.random.key(seed), 11)
    return {
        "tokens": gaussian(keys[0], (TOKENS, D), 1.0, 6.0, ((0, 32),)),
        "condition": gaussian(keys[1], (IMAGES, D), 1.0, 6.0, ((0, 32),)),
        "grid_shape": draw_grid_shape(jax.random.fold_in(keys[10], 71), 0),
        "w_ada": gaussian(keys[3], (D, 6 * D), D ** -0.5, 0.1875),
        "b_ada": gaussian(keys[4], (6 * D,), 0.5, 3.0),
        "w_qkv": gaussian(keys[5], (D, 3, D), D ** -0.5, 0.1875, ((2, 2),)),
        "w_out": gaussian(keys[6], (D, D), (D // 32) ** -0.5, 1.0, ((0, 2),)),
        "w_gate_up": gaussian(keys[7], (D, 2, FF), D ** -0.5, 0.1875, ((2, 2),)),
        "w_down": gaussian(keys[8], (FF, D), (FF // 4) ** -0.5, 0.21875, ((0, 2),)),
        "cotangent": noise_with(keys[9], (TOKENS, D), 1.0, 6.0, ((0, 32),), (0, 1, 32, 2.75)),
    }


@jax.custom_vjp
def low(v):
    return lax.optimization_barrier(v.astype(jnp.bfloat16)).astype(jnp.float32)

@jax.custom_vjp
def low_back(v):
    return v

def low_keep(v):
    return (low(v), None)

def low_pass(kept, grad):
    return (grad,)

def back_keep(v):
    return (v, None)

def back_low(kept, grad):
    return (low(grad),)
low.defvjp(low_keep, low_pass)
low_back.defvjp(back_keep, back_low)
highest = lax.Precision.HIGHEST

def layer_norm(values):
    centered = values - lax.optimization_barrier(jnp.mean(values, axis=-1, keepdims=True))
    variance = lax.optimization_barrier(jnp.mean(centered * centered, axis=-1, keepdims=True))
    return centered * lax.rsqrt(variance + 1e-06)

def rotate_half(values):
    quarter = values.shape[-1] // 4
    part_one = values[..., :quarter]
    part_two = values[..., quarter:2 * quarter]
    part_three = values[..., 2 * quarter:3 * quarter]
    part_four = values[..., 3 * quarter:]
    return jnp.concatenate([-part_two, part_one, -part_four, part_three], axis=-1)

def rope_tables(grid_shape, length, head_dim):
    position = jnp.arange(length, dtype=jnp.int32)[None, :]
    widths = grid_shape[:, 1:2]
    rows_at = position // widths
    cols_at = position % widths
    key_valid = position < grid_shape[:, 0:1] * widths
    quarter = head_dim // 4
    frequency = 10000.0 ** (-jnp.arange(quarter, dtype=jnp.float32) / quarter)
    row_angle = rows_at.astype(jnp.float32)[..., None] * frequency
    col_angle = cols_at.astype(jnp.float32)[..., None] * frequency
    angles = jnp.concatenate([row_angle, row_angle, col_angle, col_angle], axis=-1)
    angles = angles.reshape(-1, 1, head_dim)
    return (jnp.cos(angles), jnp.sin(angles), key_valid)

def apply_rope(values, cosine, sine_table):
    return values * cosine + rotate_half(values) * sine_table

def group_attention(block):
    queries, key_rows, value_rows, cosine, sine_table, key_valid = block
    images = key_valid.shape[0]
    scaled = low(apply_rope(queries, cosine, sine_table) * HD ** (-0.5))
    rotated = low(apply_rope(key_rows, cosine, sine_table))
    values_low = low(value_rows)
    scaled = scaled.reshape(images, LEN, HEADS, HD)
    rotated = rotated.reshape(images, LEN, HEADS, HD)
    values_low = values_low.reshape(images, LEN, HEADS, HD)
    scores = low_back(jnp.einsum('gqhe,gkhe->ghqk', scaled, rotated, precision=highest))
    scores = jnp.where(key_valid[:, None, None, :], scores, -1e+30)
    row_top = lax.optimization_barrier(jnp.max(scores, axis=-1, keepdims=True))
    exp_scores = jnp.exp(scores - row_top)
    attn_probs = exp_scores / lax.optimization_barrier(jnp.sum(exp_scores, axis=-1, keepdims=True))
    mixed_out = jnp.einsum('ghqk,gkhe->gqhe', low(attn_probs), values_low, precision=highest)
    return low(low_back(mixed_out)).reshape(images * LEN, HEADS * HD)

def forward(tokens, condition, w_ada, b_ada, w_qkv, w_out, w_gate_up, w_down, cosine, sine_table, key_valid):
    images = condition.shape[0]
    silu_cond = low(condition * jax.nn.sigmoid(condition))
    modulation = low_back(jnp.dot(silu_cond, w_ada, precision=highest) + b_ada)
    modulation = modulation.reshape(images, 6, 1, D)
    shift_one = modulation[:, 0]
    scale_one = modulation[:, 1]
    gate_one = modulation[:, 2]
    shift_two = modulation[:, 3]
    scale_two = modulation[:, 4]
    gate_two = modulation[:, 5]
    stacked = tokens.reshape(images, LEN, D)
    norm_one = layer_norm(stacked)
    hidden_one = low(norm_one * (1.0 + scale_one) + shift_one).reshape(-1, D)
    qkv_all = low_back(jnp.dot(hidden_one, w_qkv.reshape(D, 3 * D), precision=highest))
    qkv_all = qkv_all.reshape(-1, 3, HEADS, HD)
    group_rows = 16 * LEN
    group_count = qkv_all.shape[0] // group_rows
    blocks = (qkv_all[:, 0].reshape(group_count, group_rows, HEADS, HD), qkv_all[:, 1].reshape(group_count, group_rows, HEADS, HD), qkv_all[:, 2].reshape(group_count, group_rows, HEADS, HD), cosine.reshape(group_count, group_rows, 1, HD), sine_table.reshape(group_count, group_rows, 1, HD), key_valid.reshape(group_count, 16, LEN))
    heads_out = lax.map(jax.checkpoint(group_attention), blocks).reshape(-1, D)
    attn_branch = low_back(jnp.dot(heads_out, w_out, precision=highest)).reshape(images, LEN, D)
    middle = stacked + gate_one * attn_branch
    norm_two = layer_norm(middle)
    hidden_two = low(norm_two * (1.0 + scale_two) + shift_two).reshape(-1, D)
    gate_up = low_back(jnp.dot(hidden_two, w_gate_up.reshape(D, 2 * FF), precision=highest))
    gate_up = gate_up.reshape(-1, 2, FF)
    gate_pre = gate_up[:, 0]
    up_pre = gate_up[:, 1]
    inner_act = low(gate_pre * jax.nn.sigmoid(gate_pre) * up_pre)
    branch = low_back(jnp.dot(inner_act, w_down, precision=highest)).reshape(images, LEN, D)
    return (middle + gate_two * branch).reshape(-1, D)

def reference(tokens, condition, grid_shape, w_ada, b_ada, w_qkv, w_out, w_gate_up, w_down, cotangent):
    cosine, sine_table, key_valid = rope_tables(grid_shape, LEN, HD)
    bound_forward = partial(forward, cosine=cosine, sine_table=sine_table, key_valid=key_valid)
    result, pullback = jax.vjp(bound_forward, tokens.astype(jnp.float32), condition.astype(jnp.float32), w_ada.astype(jnp.float32), b_ada.astype(jnp.float32), w_qkv.astype(jnp.float32), w_out.astype(jnp.float32), w_gate_up.astype(jnp.float32), w_down.astype(jnp.float32))
    gradients = pullback(cotangent.astype(jnp.float32))
    return (result.astype(jnp.bfloat16), gradients[0], gradients[1], gradients[2], gradients[3], gradients[4], gradients[5], gradients[6], gradients[7])
```

```python
import jax
import jax.numpy as jnp
from jax import lax
from jax.sharding import PartitionSpec as P

HD = 72
LEN = 256


epsilon = 1e-06


def layer_norm(values):
    centered = values - jnp.mean(values, axis=-1, keepdims=True)
    variance = jnp.mean(centered * centered, axis=-1, keepdims=True)
    inverse = lax.rsqrt(variance + epsilon)
    return (centered * inverse, inverse)


def norm_back(upstream, normed, inverse):
    mean_grad = jnp.mean(upstream, axis=-1, keepdims=True)
    mean_cross = jnp.mean(upstream * normed, axis=-1, keepdims=True)
    return inverse * (upstream - mean_grad - normed * mean_cross)


def rotate_half(values):
    quarter = values.shape[-1] // 4
    part_one = values[..., :quarter]
    part_two = values[..., quarter : 2 * quarter]
    part_three = values[..., 2 * quarter : 3 * quarter]
    part_four = values[..., 3 * quarter :]
    return jnp.concatenate([-part_two, part_one, -part_four, part_three], axis=-1)


def rope_tables(grid_shape, length, head_dim):
    position = jnp.arange(length, dtype=jnp.int32)[None, :]
    widths = grid_shape[:, 1:2]
    rows_at = position // widths
    cols_at = position % widths
    key_valid = position < grid_shape[:, 0:1] * widths
    quarter = head_dim // 4
    frequency = 10000.0 ** (-jnp.arange(quarter, dtype=jnp.float32) / quarter)
    row_angle = rows_at.astype(jnp.float32)[..., None] * frequency
    col_angle = cols_at.astype(jnp.float32)[..., None] * frequency
    angles = jnp.concatenate([row_angle, row_angle, col_angle, col_angle], axis=-1)
    angles = angles[:, :, None, :]
    return (jnp.cos(angles), jnp.sin(angles), key_valid)


def apply_rope(values, cosine, sine_table):
    return values * cosine + rotate_half(values) * sine_table


def rope_back(upstream, cosine, sine_table):
    return upstream * cosine - rotate_half(upstream * sine_table)


def contract_rows(left_side, right_side):
    return lax.dot_general(
        left_side, right_side, (((0,), (0,)), ((), ())), preferred_element_type=jnp.float32
    )


def contract_cols(left_side, right_side):
    return lax.dot_general(
        left_side, right_side, (((1,), (1,)), ((), ())), preferred_element_type=jnp.float32
    )


def swap(values):
    return lax.ppermute(values, "tensor", [(0, 1), (1, 0)])


def gather_pair(values):
    return jnp.concatenate([values, swap(values)], axis=0)


def scatter_pair(partial):
    rows = partial.shape[0] // 2
    arrived = swap(partial[rows:].astype(jnp.bfloat16))
    return partial[:rows] + arrived.astype(jnp.float32)


def sum_over_images(partial):
    count = lax.axis_size("dp")
    me = lax.axis_index("dp")
    held = partial.reshape(count, partial.shape[0] // count, partial.shape[1])
    stride = 1
    left = count
    while left > 1:
        bit = (me // stride) % 2
        pairs = held.reshape(left // 2, 2, *held.shape[1:])
        keep = lax.dynamic_index_in_dim(pairs, bit, 1, keepdims=False)
        give = lax.dynamic_index_in_dim(pairs, 1 - bit, 1, keepdims=False)
        came = lax.ppermute(
            give.astype(jnp.bfloat16), "dp", [(i, i ^ stride) for i in range(count)]
        )
        held = keep.astype(jnp.float32) + came.astype(jnp.float32)
        left //= 2
        stride *= 2
        if left > 1:
            held = held.astype(jnp.bfloat16)
    return held[0]


def body(tokens, condition, grid_shape, w_ada, b_ada, w_qkv, w_out, w_gate_up, w_down, cotangent):
    model_width = tokens.shape[1]
    images = condition.shape[0]
    local_rows = tokens.shape[0]
    head_cols = w_out.shape[0]
    heads_local = head_cols // HD
    inner_width = w_down.shape[0]
    qkv_flat = w_qkv.reshape(model_width, 3 * head_cols)
    gate_up_flat = w_gate_up.reshape(model_width, 2 * inner_width)
    score_scale = HD ** (-0.5)
    cond_float = condition.astype(jnp.float32)
    cond_sigmoid = jax.nn.sigmoid(cond_float)
    silu_cond = (cond_float * cond_sigmoid).astype(jnp.bfloat16)
    modulation = jnp.dot(silu_cond, w_ada, preferred_element_type=jnp.float32) + b_ada.astype(
        jnp.float32
    )
    mod_parts = modulation.reshape(images, 6, 1, model_width)
    shift_one = mod_parts[:, 0]
    scale_one = mod_parts[:, 1]
    gate_one = mod_parts[:, 2]
    shift_two = mod_parts[:, 3]
    scale_two = mod_parts[:, 4]
    gate_two = mod_parts[:, 5]
    stacked = tokens.astype(jnp.float32).reshape(images, LEN, model_width)
    norm_one, inverse_one = layer_norm(stacked)
    hidden_one = (
        (norm_one * (1.0 + scale_one) + shift_one)
        .astype(jnp.bfloat16)
        .reshape(local_rows, model_width)
    )
    gathered_one = gather_pair(hidden_one)
    total_rows = gathered_one.shape[0]
    all_images = total_rows // LEN
    qkv_all = jnp.dot(gathered_one, qkv_flat, preferred_element_type=jnp.float32)
    qkv_all = qkv_all.reshape(all_images, LEN, 3, heads_local, HD)
    mine = lax.axis_index("tensor")
    grid_shape = jnp.where(mine == 0, grid_shape, grid_shape[::-1])
    cosine, sine_table, key_valid = rope_tables(grid_shape, LEN, HD)
    query_low = (apply_rope(qkv_all[:, :, 0], cosine, sine_table) * score_scale).astype(
        jnp.bfloat16
    )
    key_low = apply_rope(qkv_all[:, :, 1], cosine, sine_table).astype(jnp.bfloat16)
    value_low = qkv_all[:, :, 2].astype(jnp.bfloat16)
    key_mask = key_valid[:, None, None, :]
    scores = jnp.einsum("gqhe,gkhe->ghqk", query_low, key_low, preferred_element_type=jnp.float32)
    scores = jnp.where(key_mask, scores, -1e30)
    row_top = jnp.max(scores, axis=-1, keepdims=True)
    exp_scores = jnp.exp(scores - row_top)
    row_total = jnp.sum(exp_scores, axis=-1, keepdims=True)
    attn_probs = exp_scores / row_total
    log_total = row_top + jnp.log(row_total)
    heads_low = jnp.einsum(
        "ghqk,gkhe->gqhe",
        attn_probs.astype(jnp.bfloat16),
        value_low,
        preferred_element_type=jnp.float32,
    )
    heads_low = heads_low.astype(jnp.bfloat16).reshape(total_rows, head_cols)
    rows_in = heads_low
    attn_branch = scatter_pair(jnp.dot(rows_in, w_out, preferred_element_type=jnp.float32))
    attn_branch = attn_branch.reshape(images, LEN, model_width)
    middle = stacked + gate_one * attn_branch
    norm_two, inverse_two = layer_norm(middle)
    hidden_two = (
        (norm_two * (1.0 + scale_two) + shift_two)
        .astype(jnp.bfloat16)
        .reshape(local_rows, model_width)
    )
    gathered_two = gather_pair(hidden_two)
    gate_up_pre = jnp.dot(gathered_two, gate_up_flat, preferred_element_type=jnp.float32)
    gate_up_pre = gate_up_pre.reshape(total_rows, 2, inner_width)
    gate_pre = gate_up_pre[:, 0]
    up_pre = gate_up_pre[:, 1]
    gate_sigmoid = jax.nn.sigmoid(gate_pre)
    gate_act = gate_pre * gate_sigmoid
    inner_low = (gate_act * up_pre).astype(jnp.bfloat16)
    rows_in = inner_low
    mlp_branch = scatter_pair(jnp.dot(rows_in, w_down, preferred_element_type=jnp.float32))
    mlp_branch = mlp_branch.reshape(images, LEN, model_width)
    layer_out = (
        (middle + gate_two * mlp_branch).astype(jnp.bfloat16).reshape(local_rows, model_width)
    )
    upstream = cotangent.astype(jnp.float32).reshape(images, LEN, model_width)
    d_gate_two = jnp.sum(upstream * mlp_branch, axis=1)
    d_mlp = (gate_two * upstream).astype(jnp.bfloat16).reshape(local_rows, model_width)
    shard_rows = gather_pair(d_mlp)
    grad_down = sum_over_images(contract_rows(shard_rows, inner_low)).T
    grad_inner = contract_cols(shard_rows, w_down)
    d_gate_pre = grad_inner * up_pre * gate_sigmoid * (1.0 + gate_pre * (1.0 - gate_sigmoid))
    d_up_pre = grad_inner * gate_act
    d_gate_up = (
        jnp.stack([d_gate_pre, d_up_pre], axis=1)
        .astype(jnp.bfloat16)
        .reshape(total_rows, 2 * inner_width)
    )
    grad_gate_up = sum_over_images(contract_rows(gathered_two, d_gate_up)).reshape(
        -1, 2, inner_width
    )
    rows_in = d_gate_up
    d_hidden_two = scatter_pair(contract_cols(rows_in, gate_up_flat))
    d_hidden_two = d_hidden_two.reshape(images, LEN, model_width)
    d_shift_two = jnp.sum(d_hidden_two, axis=1)
    d_scale_two = jnp.sum(d_hidden_two * norm_two, axis=1)
    d_middle = upstream + norm_back(d_hidden_two * (1.0 + scale_two), norm_two, inverse_two)
    d_gate_one = jnp.sum(d_middle * attn_branch, axis=1)
    d_attn = (gate_one * d_middle).astype(jnp.bfloat16).reshape(local_rows, model_width)
    shard_rows = gather_pair(d_attn)
    grad_out = sum_over_images(contract_rows(shard_rows, heads_low)).T
    grad_heads = contract_cols(shard_rows, w_out)
    d_heads_low = grad_heads.astype(jnp.bfloat16).reshape(all_images, LEN, heads_local, HD)
    scores_again = jnp.einsum(
        "gqhe,gkhe->ghqk", query_low, key_low, preferred_element_type=jnp.float32
    )
    scores_again = jnp.where(key_mask, scores_again, -1e30)
    probs_again = jnp.exp(scores_again - log_total)
    d_probs = jnp.einsum(
        "gqhe,gkhe->ghqk", d_heads_low, value_low, preferred_element_type=jnp.float32
    )
    d_value = jnp.einsum(
        "ghqk,gqhe->gkhe",
        probs_again.astype(jnp.bfloat16),
        d_heads_low,
        preferred_element_type=jnp.float32,
    )
    row_inner = jnp.sum(probs_again * d_probs, axis=-1, keepdims=True)
    d_scores = (probs_again * (d_probs - row_inner)).astype(jnp.bfloat16)
    d_query = jnp.einsum("ghqk,gkhe->gqhe", d_scores, key_low, preferred_element_type=jnp.float32)
    d_key = jnp.einsum("ghqk,gqhe->gkhe", d_scores, query_low, preferred_element_type=jnp.float32)
    d_query = rope_back(d_query, cosine, sine_table) * score_scale
    d_key = rope_back(d_key, cosine, sine_table)
    d_qkv = (
        jnp.stack([d_query, d_key, d_value], axis=2)
        .astype(jnp.bfloat16)
        .reshape(total_rows, 3 * head_cols)
    )
    grad_qkv = sum_over_images(contract_rows(gathered_one, d_qkv)).reshape(-1, 3, head_cols)
    rows_in = d_qkv
    d_hidden_one = scatter_pair(contract_cols(rows_in, qkv_flat))
    d_hidden_one = d_hidden_one.reshape(images, LEN, model_width)
    d_shift_one = jnp.sum(d_hidden_one, axis=1)
    d_scale_one = jnp.sum(d_hidden_one * norm_one, axis=1)
    d_tokens = d_middle + norm_back(d_hidden_one * (1.0 + scale_one), norm_one, inverse_one)
    d_tokens = d_tokens.reshape(local_rows, model_width)
    d_mod = jnp.stack(
        [d_shift_one, d_scale_one, d_gate_one, d_shift_two, d_scale_two, d_gate_two], axis=1
    )
    d_mod = d_mod.reshape(images, 6 * model_width).astype(jnp.bfloat16)
    d_condition = (
        contract_cols(d_mod, w_ada) * cond_sigmoid * (1.0 + cond_float * (1.0 - cond_sigmoid))
    )
    devices_all = lax.axis_size("dp") * lax.axis_size("tensor")
    own_cols = 6 * model_width // devices_all
    packed = jnp.concatenate(
        [
            d_mod.reshape(devices_all, own_cols),
            jnp.broadcast_to(silu_cond, (devices_all, model_width)),
        ],
        axis=1,
    )
    packed = jnp.pad(packed, ((0, 0), (0, -packed.shape[1] % 128)))
    packed = lax.all_to_all(
        packed.reshape(devices_all, -1, 128), ("dp", "tensor"), 0, 0, tiled=True
    ).reshape(devices_all, -1)
    columns = packed[:, :own_cols]
    silu_rows = packed[:, own_cols : own_cols + model_width]
    weight_part = contract_rows(silu_rows, columns)
    bias_part = jnp.sum(columns.astype(jnp.float32), axis=0)
    return (
        layer_out,
        d_tokens,
        d_condition,
        weight_part,
        bias_part,
        grad_qkv,
        grad_out,
        grad_gate_up,
        grad_down,
    )


def solution(mesh):
    placed = (
        P(("dp", "tensor"), None),
        P(("dp", "tensor"), None),
        P("dp", None),
        P(),
        P(),
        P(None, None, "tensor"),
        P("tensor", None),
        P(None, None, "tensor"),
        P("tensor", None),
        P(("dp", "tensor"), None),
    )
    return jax.shard_map(
        body,
        mesh=mesh,
        in_specs=placed,
        out_specs=(
            P(("dp", "tensor"), None),
            P(("dp", "tensor"), None),
            P(("dp", "tensor"), None),
            P(None, ("dp", "tensor")),
            P(("dp", "tensor")),
            P("dp", None, "tensor"),
            P("tensor", "dp"),
            P("dp", None, "tensor"),
            P("tensor", "dp"),
        ),
        check_vma=False,
    )
```

```python
import functools

import jax
import jax.numpy as jnp
from jax import lax
from jax.experimental import pallas as pl
from jax.experimental.pallas import tpu as pltpu
from jax.sharding import PartitionSpec as P

HD = 72
LEN = 256
EPSILON = 1e-06
MESH = pl.DeviceIdType.MESH
F32 = jnp.float32
BF16 = jnp.bfloat16
ROWS = 32
STRIP = 384
TILE = 256


def dot(left, right, left_dim, right_dim):
    return lax.dot_general(
        left, right, (((left_dim,), (right_dim,)), ((), ())), preferred_element_type=F32
    )


def normed(values):
    centered = values - jnp.mean(values, axis=-1, keepdims=True)
    variance = jnp.mean(centered * centered, axis=-1, keepdims=True)
    inverse = lax.rsqrt(variance + EPSILON)
    return centered * inverse, inverse


def norm_back(upstream, norm, inverse):
    mean_grad = jnp.mean(upstream, axis=-1, keepdims=True)
    mean_cross = jnp.mean(upstream * norm, axis=-1, keepdims=True)
    return inverse * (upstream - mean_grad - norm * mean_cross)


def rotate_rows(values):
    quarter = HD // 4
    a, b = values[:quarter], values[quarter : 2 * quarter]
    c, d = values[2 * quarter : 3 * quarter], values[3 * quarter :]
    return jnp.concatenate([-b, a, -d, c], axis=0)


def fold(values):
    return jnp.sum(values.reshape(values.shape[0] // 8, 8, values.shape[1]), axis=0)


def block_kernel(
    tok, cot, mod, cos_t, sin_t, valid,
    wqkv_hbm, wout_hbm, wg_hbm, wu_hbm, wdown_hbm,
    out, dtok, dmod, gqkv, gout, ggu, gdown,
    wqkv, wout, wg, wu, wdown,
    h1, h2, dml, dat,
    q_s, k_s, v_s, p_s, qkv_f, a_f, a_t,
    hid, dgate, dup, dqkv,
    attn, x1, dx1, own,
    send_a, send_b, send_c, send_d, recv_a, recv_b, recv_c, recv_d,
    flip, g_f, stage, sums,
    wsem, ssem, rsem, gsem,
):
    width = tok.shape[1]
    heads = q_s.shape[0] // 2
    head_cols = heads * HD
    inner = wdown.shape[0]
    side = lax.axis_index("tensor")
    mate = {"tensor": 1 - side}
    scale = HD ** (-0.5)

    loads = [
        pltpu.make_async_copy(src, dst, wsem.at[i])
        for i, (src, dst) in enumerate(
            ((wqkv_hbm, wqkv), (wout_hbm, wout), (wg_hbm, wg), (wu_hbm, wu), (wdown_hbm, wdown))
        )
    ]
    for load in loads:
        load.start()

    barrier = pltpu.get_barrier_semaphore()
    pl.semaphore_signal(barrier, inc=1, device_id=mate, device_id_type=MESH)
    pl.semaphore_wait(barrier, 1)

    def give(src, dst, slot):
        return pltpu.make_async_remote_copy(
            src_ref=src, dst_ref=dst, send_sem=ssem.at[slot], recv_sem=rsem.at[slot],
            device_id=mate, device_id_type=MESH,
        )

    def gather(buf, slot):
        half = LEN // 2
        return [
            give(buf.at[0, pl.ds(c * half, half)], buf.at[1, pl.ds(c * half, half)], slot + c)
            for c in range(2)
        ]

    strips = width // STRIP

    def scatter(send, recv, slot):
        return [
            give(
                send.at[:, pl.ds(c * STRIP, STRIP)], recv.at[:, pl.ds(c * STRIP, STRIP)], slot + c
            )
            for c in range(strips)
        ]

    go_h1, go_dml, go_h2, go_dat = (gather(b, 2 * i) for i, b in enumerate((h1, dml, h2, dat)))
    go_a, go_b, go_c, go_d = (
        scatter(s, r, 8 + strips * i)
        for i, (s, r) in enumerate(
            ((send_a, recv_a), (send_b, recv_b), (send_c, recv_c), (send_d, recv_d))
        )
    )

    def rows_loop(step, copies=None):
        half = LEN // 2
        count = half // ROWS
        for c in range(2):
            def one(i, carry, c=c):
                step(pl.ds(pl.multiple_of(c * half + i * ROWS, ROWS), ROWS))
                return carry
            lax.fori_loop(0, count, one, 0)
            if copies is not None:
                copies[c].start()

    shift_one, scale_one, gate_one = mod[0:1], mod[1:2], mod[2:3]
    shift_two, scale_two, gate_two = mod[3:4], mod[4:5], mod[5:6]

    def first_norm(rows):
        norm, _ = normed(tok[rows, :].astype(F32))
        h1[0, rows, :] = (norm * (1.0 + scale_one) + shift_one).astype(BF16)

    rows_loop(first_norm, go_h1)

    def mlp_grad(rows):
        dml[0, rows, :] = (gate_two * cot[rows, :].astype(F32)).astype(BF16)

    rows_loop(mlp_grad, go_dml)
    sums[...] = jnp.zeros_like(sums)

    def heads_forward(image):
        for part in range(3):
            qkv_f[part * head_cols : (part + 1) * head_cols, :] = dot(
                wqkv[part * head_cols : (part + 1) * head_cols, :], h1[image], 1, 1
            )
        cosine, sine = cos_t[image], sin_t[image]
        ok = valid[image][:, :1] > 0.0

        def head(h, carry):
            at = image * heads + h
            rows = pl.ds(pl.multiple_of(h * HD, 8), HD)
            query = qkv_f[rows, :]
            key = qkv_f[pl.ds(pl.multiple_of(head_cols + h * HD, 8), HD), :]
            value = qkv_f[pl.ds(pl.multiple_of(2 * head_cols + h * HD, 8), HD), :].astype(BF16)
            query = ((query * cosine + rotate_rows(query) * sine) * scale).astype(BF16)
            key = (key * cosine + rotate_rows(key) * sine).astype(BF16)
            q_s[at], k_s[at], v_s[at] = query, key, value
            scores = dot(key, query, 0, 0)
            scores = jnp.where(ok, scores, -1e30)
            top = jnp.max(scores, axis=0, keepdims=True)
            exps = jnp.exp(scores - top)
            probs = exps * (1.0 / jnp.sum(exps, axis=0, keepdims=True))
            p_s[at] = probs
            a_f[rows, :] = dot(value, probs.astype(BF16), 1, 0)
            return carry

        lax.fori_loop(0, heads, head, 0)
        a_t[image] = a_f[...].astype(BF16)

    def strips_of(make, send=None, copies=None, keep=None):
        for c in range(strips):
            cols = slice(c * STRIP, (c + 1) * STRIP)
            value = make(cols)
            if send is not None:
                send[:, cols] = value.astype(BF16)
                copies[c].start()
            else:
                keep[:, cols] = value

    loads[0].wait()
    heads_forward(0)
    for copy in go_h1:
        copy.wait_recv()
    heads_forward(1)
    loads[1].wait()
    strips_of(lambda cols: dot(a_t[1], wout[:, cols], 0, 0), send_a, go_a)
    strips_of(lambda cols: dot(a_t[0], wout[:, cols], 0, 0), keep=own)
    for copy in go_a:
        copy.wait_recv()

    def second_norm(rows):
        branch = own[rows, :] + recv_a[rows, :].astype(F32)
        attn[rows, :] = branch
        middle = tok[rows, :].astype(F32) + gate_one * branch
        x1[rows, :] = middle
        norm, _ = normed(middle)
        h2[0, rows, :] = (norm * (1.0 + scale_two) + shift_two).astype(BF16)

    rows_loop(second_norm, go_h2)

    for load in loads[2:]:
        load.wait()

    def feed_forward(image):
        def tile(j, carry):
            cols = pl.ds(pl.multiple_of(j * TILE, TILE), TILE)
            gate = dot(h2[image], wg[:, cols], 1, 0)
            up = dot(h2[image], wu[:, cols], 1, 0)
            grad = dot(dml[image], wdown[cols, :], 1, 1)
            sig = jax.nn.sigmoid(gate)
            act = gate * sig
            hid[image, :, cols] = (act * up).astype(BF16)
            dgate[image, :, cols] = (grad * up * sig * (1.0 + gate * (1.0 - sig))).astype(BF16)
            dup[image, :, cols] = (grad * act).astype(BF16)
            return carry

        lax.fori_loop(0, inner // TILE, tile, 0)

    for copy in go_dml:
        copy.wait_recv()
    feed_forward(0)
    for copy in go_h2:
        copy.wait_recv()
    feed_forward(1)

    def dh2_strip(image):
        return lambda cols: dot(dgate[image], wg[cols, :], 1, 1) + dot(dup[image], wu[cols, :], 1, 1)

    def mlp_strip(image):
        return lambda cols: dot(hid[image], wdown[:, cols], 1, 0)

    strips_of(dh2_strip(1), send_b, go_b)
    strips_of(mlp_strip(1), send_c, go_c)
    strips_of(dh2_strip(0), keep=own)

    def weight_grad(left, target, right_tile, columns):
        for image in range(2):
            flip[image] = left[image].T
        pend = {}
        tiles = [(s, min(TILE, columns - s)) for s in range(0, columns, TILE)]
        for n, (start, size) in enumerate(tiles):
            slot = n % 2
            total = dot(flip[0], *right_tile(0, start, size))
            total = total + dot(flip[1], *right_tile(1, start, size))
            if slot in pend:
                pend[slot].wait()
            stage[slot, :, 0:size] = total.astype(BF16)
            copy = pltpu.make_async_copy(
                stage.at[slot], target.at[:, pl.ds(start, TILE)], gsem.at[slot]
            )
            copy.start()
            pend[slot] = copy
        for copy in pend.values():
            copy.wait()

    weight_grad(dml, gdown, lambda i, s, n: (hid[i, :, s : s + n], 1, 0), inner)
    weight_grad(
        h2, ggu,
        lambda i, s, n: (dgate[i, :, s : s + n], 1, 0) if s < inner
        else (dup[i, :, s - inner : s - inner + n], 1, 0),
        2 * inner,
    )

    for copy in go_b:
        copy.wait_recv()

    def second_back(rows):
        grad = own[rows, :] + recv_b[rows, :].astype(F32)
        norm, inverse = normed(x1[rows, :])
        middle = cot[rows, :].astype(F32) + norm_back(grad * (1.0 + scale_two), norm, inverse)
        dx1[rows, :] = middle
        dat[0, rows, :] = (gate_one * middle).astype(BF16)
        sums[2] += fold(middle * attn[rows, :])
        sums[3] += fold(grad)
        sums[4] += fold(grad * norm)

    rows_loop(second_back, go_dat)

    def heads_back(image):
        a_f[...] = dot(wout[...], dat[image], 1, 1)
        cosine, sine = cos_t[image], sin_t[image]

        def head(h, carry):
            at = image * heads + h
            rows = pl.ds(pl.multiple_of(h * HD, 8), HD)
            da = a_f[rows, :].astype(BF16)
            probs = p_s[at]
            query, key, value = q_s[at], k_s[at], v_s[at]
            dprobs = dot(value, da, 0, 0)
            dvalue = dot(da, probs.astype(BF16), 1, 1)
            inside = jnp.sum(probs * dprobs, axis=0, keepdims=True)
            dscores = (probs * (dprobs - inside)).astype(BF16)
            dquery = dot(key, dscores, 1, 0)
            dkey = dot(query, dscores, 1, 1)
            dquery = (dquery * cosine - rotate_rows(dquery * sine)) * scale
            dkey = dkey * cosine - rotate_rows(dkey * sine)
            qkv_f[rows, :] = dquery
            qkv_f[pl.ds(pl.multiple_of(head_cols + h * HD, 8), HD), :] = dkey
            qkv_f[pl.ds(pl.multiple_of(2 * head_cols + h * HD, 8), HD), :] = dvalue
            return carry

        lax.fori_loop(0, heads, head, 0)
        dqkv[image] = qkv_f[...].astype(BF16)

    heads_back(0)
    for copy in go_dat:
        copy.wait_recv()
    heads_back(1)

    def dh1_strip(image):
        return lambda cols: dot(dqkv[image], wqkv[:, cols], 0, 0)

    strips_of(dh1_strip(1), send_d, go_d)
    strips_of(dh1_strip(0), keep=own)

    weight_grad(h1, gqkv, lambda i, s, n: (dqkv[i, s : s + n, :], 1, 1), 3 * head_cols)
    weight_grad(dat, gout, lambda i, s, n: (a_t[i, s : s + n, :], 1, 1), head_cols)

    for copy in go_d:
        copy.wait_recv()

    def first_back(rows):
        grad = own[rows, :] + recv_d[rows, :].astype(F32)
        norm, inverse = normed(tok[rows, :].astype(F32))
        dtok[rows, :] = dx1[rows, :] + norm_back(grad * (1.0 + scale_one), norm, inverse)
        sums[0] += fold(grad)
        sums[1] += fold(grad * norm)

    rows_loop(first_back)

    strips_of(mlp_strip(0), keep=own)
    for copy in go_c:
        copy.wait_recv()

    def finish(rows):
        branch = own[rows, :] + recv_c[rows, :].astype(F32)
        out[rows, :] = (x1[rows, :] + gate_two * branch).astype(BF16)
        sums[5] += fold(cot[rows, :].astype(F32) * branch)

    rows_loop(finish)
    for n in range(6):
        dmod[n : n + 1, :] = jnp.sum(sums[n], axis=0, keepdims=True)
    for copy in (*go_h1, *go_dml, *go_h2, *go_dat, *go_a, *go_b, *go_c, *go_d):
        copy.wait_send()


def run_block(tok, cot, mod, cos_t, sin_t, valid, wqkv, wout, wg, wu, wdown):
    width = tok.shape[1]
    head_cols = wout.shape[0]
    heads = head_cols // HD
    inner = wdown.shape[0]
    strips = width // STRIP
    vmem = pl.BlockSpec(memory_space=pltpu.VMEM)
    hbm = pl.BlockSpec(memory_space=pl.ANY)
    V = pltpu.VMEM
    copies = 8 + 4 * strips
    return pl.pallas_call(
        block_kernel,
        out_shape=(
            jax.ShapeDtypeStruct((LEN, width), BF16),
            jax.ShapeDtypeStruct((LEN, width), F32),
            jax.ShapeDtypeStruct((6, width), F32),
            jax.ShapeDtypeStruct((width, -(-3 * head_cols // TILE) * TILE), BF16),
            jax.ShapeDtypeStruct((width, -(-head_cols // TILE) * TILE), BF16),
            jax.ShapeDtypeStruct((width, 2 * inner), BF16),
            jax.ShapeDtypeStruct((width, inner), BF16),
        ),
        in_specs=[vmem] * 6 + [hbm] * 5,
        out_specs=[vmem] * 3 + [hbm] * 4,
        scratch_shapes=[
            V(wqkv.shape, BF16), V(wout.shape, BF16), V(wg.shape, BF16), V(wu.shape, BF16),
            V(wdown.shape, BF16),
            *[V((2, LEN, width), BF16)] * 4,
            *[V((2 * heads, HD, LEN), BF16)] * 3,
            V((2 * heads, LEN, LEN), F32),
            V((3 * head_cols, LEN), F32),
            V((head_cols, LEN), F32),
            V((2, head_cols, LEN), BF16),
            *[V((2, LEN, inner), BF16)] * 3,
            V((2, 3 * head_cols, LEN), BF16),
            *[V((LEN, width), F32)] * 4,
            *[V((LEN, width), BF16)] * 8,
            V((2, width, LEN), BF16),
            V((8, 128), F32),
            V((2, width, TILE), BF16),
            V((6, 8, width), F32),
            pltpu.SemaphoreType.DMA((5,)),
            pltpu.SemaphoreType.DMA((copies,)),
            pltpu.SemaphoreType.DMA((copies,)),
            pltpu.SemaphoreType.DMA((2,)),
        ],
        compiler_params=pltpu.CompilerParams(
            collective_id=0, has_side_effects=True, vmem_limit_bytes=60 * 1024 * 1024
        ),
    )(tok, cot, mod, cos_t, sin_t, valid, wqkv, wout, wg, wu, wdown)


def rope_tables(grid_shape):
    position = jnp.arange(LEN, dtype=jnp.int32)[None, :]
    widths = grid_shape[:, 1:2]
    rows_at = position // widths
    cols_at = position % widths
    key_valid = position < grid_shape[:, 0:1] * widths
    quarter = HD // 4
    frequency = 10000.0 ** (-jnp.arange(quarter, dtype=F32) / quarter)
    row_angle = rows_at.astype(F32)[:, None, :] * frequency[:, None]
    col_angle = cols_at.astype(F32)[:, None, :] * frequency[:, None]
    angles = jnp.concatenate([row_angle, row_angle, col_angle, col_angle], axis=1)
    valid = jnp.broadcast_to(key_valid.astype(F32)[:, :, None], (*key_valid.shape, 128))
    return jnp.cos(angles), jnp.sin(angles), valid


def sum_over_images(partial):
    count = lax.axis_size("dp")
    me = lax.axis_index("dp")
    held = partial.reshape(count, partial.shape[0] // count, partial.shape[1])
    stride = 1
    left = count
    while left > 1:
        bit = (me // stride) % 2
        pairs = held.reshape(left // 2, 2, *held.shape[1:])
        keep = lax.dynamic_index_in_dim(pairs, bit, 1, keepdims=False)
        send = lax.dynamic_index_in_dim(pairs, 1 - bit, 1, keepdims=False)
        came = lax.ppermute(send, "dp", [(i, i ^ stride) for i in range(count)])
        held = keep.astype(F32) + came.astype(F32)
        left //= 2
        stride *= 2
        if left > 1:
            held = held.astype(BF16)
    return held[0]


def body(tokens, condition, grid_shape, w_ada, b_ada, w_qkv, w_out, w_gate_up, w_down, cotangent):
    width = tokens.shape[1]
    inner = w_down.shape[0]
    head_cols = w_out.shape[0]
    cond = condition.astype(F32)
    cond_sigmoid = jax.nn.sigmoid(cond)
    silu_cond = (cond * cond_sigmoid).astype(BF16)
    mod = jnp.dot(silu_cond, w_ada, preferred_element_type=F32) + b_ada.astype(F32)
    mod = mod.reshape(6, width)
    mine = lax.axis_index("tensor")
    grid_shape = jnp.where(mine == 0, grid_shape, grid_shape[::-1])
    cos_t, sin_t, valid = rope_tables(grid_shape)
    wqkv = w_qkv.transpose(1, 2, 0).reshape(3 * head_cols, width)
    layer_out, d_tokens, d_mod, g_qkv, g_out, g_gu, g_down = run_block(
        tokens, cotangent, mod, cos_t, sin_t, valid, wqkv, w_out,
        w_gate_up[:, 0], w_gate_up[:, 1], w_down,
    )
    grad_down = sum_over_images(g_down).T
    grad_gate_up = sum_over_images(g_gu).reshape(-1, 2, inner)
    grad_out = sum_over_images(g_out[:, :head_cols]).T
    grad_qkv = sum_over_images(g_qkv[:, : 3 * head_cols]).reshape(-1, 3, head_cols)
    d_mod = d_mod.reshape(1, 6 * width).astype(BF16)
    d_condition = (
        dot(d_mod, w_ada, 1, 1) * cond_sigmoid * (1.0 + cond * (1.0 - cond_sigmoid))
    )
    devices_all = lax.axis_size("dp") * lax.axis_size("tensor")
    own_cols = 6 * width // devices_all
    packed = jnp.concatenate(
        [
            d_mod.reshape(devices_all, own_cols),
            jnp.broadcast_to(silu_cond, (devices_all, width)),
        ],
        axis=1,
    )
    packed = jnp.pad(packed, ((0, 0), (0, -packed.shape[1] % 128)))
    packed = lax.all_to_all(
        packed.reshape(devices_all, -1, 128), ("dp", "tensor"), 0, 0, tiled=True
    ).reshape(devices_all, -1)
    columns = packed[:, :own_cols]
    silu_rows = packed[:, own_cols : own_cols + width]
    weight_part = dot(silu_rows, columns, 0, 0)
    bias_part = jnp.sum(columns.astype(F32), axis=0)
    return (
        layer_out, d_tokens, d_condition, weight_part, bias_part,
        grad_qkv, grad_out, grad_gate_up, grad_down,
    )


def solution(mesh):
    placed = (
        P(("dp", "tensor"), None),
        P(("dp", "tensor"), None),
        P("dp", None),
        P(),
        P(),
        P(None, None, "tensor"),
        P("tensor", None),
        P(None, None, "tensor"),
        P("tensor", None),
        P(("dp", "tensor"), None),
    )
    return jax.shard_map(
        body,
        mesh=mesh,
        in_specs=placed,
        out_specs=(
            P(("dp", "tensor"), None),
            P(("dp", "tensor"), None),
            P(("dp", "tensor"), None),
            P(None, ("dp", "tensor")),
            P(("dp", "tensor")),
            P("dp", None, "tensor"),
            P("tensor", "dp"),
            P("dp", None, "tensor"),
            P("tensor", "dp"),
        ),
        check_vma=False,
    )
```

```python
import functools

import jax
import jax.numpy as jnp
from jax import lax
from jax.experimental import pallas as pl
from jax.experimental.pallas import tpu as pltpu
from jax.sharding import PartitionSpec as P

HD = 72
LEN = 256
EPSILON = 1e-06
MESH = pl.DeviceIdType.MESH
F32 = jnp.float32
BF16 = jnp.bfloat16
ROWS = 32
STRIP = 384
TILE = 256


def dot(left, right, left_dim, right_dim):
    return lax.dot_general(
        left, right, (((left_dim,), (right_dim,)), ((), ())), preferred_element_type=F32
    )


def normed(values):
    centered = values - jnp.mean(values, axis=-1, keepdims=True)
    variance = jnp.mean(centered * centered, axis=-1, keepdims=True)
    inverse = lax.rsqrt(variance + EPSILON)
    return centered * inverse, inverse


def norm_back(upstream, norm, inverse):
    mean_grad = jnp.mean(upstream, axis=-1, keepdims=True)
    mean_cross = jnp.mean(upstream * norm, axis=-1, keepdims=True)
    return inverse * (upstream - mean_grad - norm * mean_cross)


def rotate_rows(values):
    quarter = HD // 4
    a, b = values[:quarter], values[quarter : 2 * quarter]
    c, d = values[2 * quarter : 3 * quarter], values[3 * quarter :]
    return jnp.concatenate([-b, a, -d, c], axis=0)


def fold(values):
    return jnp.sum(values.reshape(values.shape[0] // 8, 8, values.shape[1]), axis=0)


def block_kernel(
    plan, tok, cot, mod, cos_t, sin_t, valid,
    wqkv_hbm, wout_hbm, wgu_hbm, wdown_hbm,
    out, dtok, dmod, *rest,
):
    results, rest = rest[: plan["results"]], rest[plan["results"] :]
    (
        wqkv, wout, wg, wu, wdown,
        h1, h2, dml, dat,
        q_s, k_s, v_s, p_s, qkv_f, a_f, a_t,
        hid, dgate, dup, dqkv,
        attn, dx1, own,
        send_a, send_c, recv_a, recv_b, recv_c,
        flip, sums,
        wsem, ssem, rsem, *extra,
    ) = rest
    width = tok.shape[1]
    heads = q_s.shape[0] // 2
    head_cols = heads * HD
    inner = wdown.shape[0]
    side = lax.axis_index("tensor")
    mate = {"tensor": 1 - side}
    scale = HD ** (-0.5)

    loads = [
        pltpu.make_async_copy(src, dst, wsem.at[i])
        for i, (src, dst) in enumerate(
            (
                (wqkv_hbm, wqkv), (wout_hbm, wout), (wgu_hbm.at[0], wg), (wgu_hbm.at[1], wu),
                (wdown_hbm, wdown),
            )
        )
    ]
    for load in loads:
        load.start()

    me = lax.axis_index("dp")

    def bit_of(stride):
        return lax.rem(lax.div(me, stride), 2)

    def partner(stride):
        return {"dp": me + stride - 2 * stride * bit_of(stride)}

    barrier = pltpu.get_barrier_semaphore()
    friends = [mate] + [partner(s) for s in plan["strides"]]
    for friend in friends:
        pl.semaphore_signal(barrier, inc=1, device_id=friend, device_id_type=MESH)
    pl.semaphore_wait(barrier, len(friends))

    def give(src, dst, slot):
        return pltpu.make_async_remote_copy(
            src_ref=src, dst_ref=dst, send_sem=ssem.at[slot], recv_sem=rsem.at[slot],
            device_id=mate, device_id_type=MESH,
        )

    def gather(buf, slot):
        half = LEN // 2
        return [
            give(buf.at[0, pl.ds(c * half, half)], buf.at[1, pl.ds(c * half, half)], slot + c)
            for c in range(2)
        ]

    strips = width // STRIP

    def scatter(send, recv, slot):
        return [
            give(
                send.at[:, pl.ds(c * STRIP, STRIP)], recv.at[:, pl.ds(c * STRIP, STRIP)], slot + c
            )
            for c in range(strips)
        ]

    go_h1, go_dml, go_h2, go_dat = (gather(b, 2 * i) for i, b in enumerate((h1, dml, h2, dat)))
    go_a, go_b, go_c, go_d = (
        scatter(s, r, 8 + strips * i)
        for i, (s, r) in enumerate(
            ((send_a, recv_a), (send_a, recv_b), (send_c, recv_c), (send_a, recv_a))
        )
    )

    def rows_loop(step, copies=None):
        half = LEN // 2
        count = half // ROWS
        for c in range(2):
            def one(i, carry, c=c):
                step(pl.ds(pl.multiple_of(c * half + i * ROWS, ROWS), ROWS))
                return carry
            lax.fori_loop(0, count, one, 0)
            if copies is not None:
                copies[c].start()

    shift_one, scale_one, gate_one = mod[0:1], mod[1:2], mod[2:3]
    shift_two, scale_two, gate_two = mod[3:4], mod[4:5], mod[5:6]

    def first_norm(rows):
        norm, _ = normed(tok[rows, :].astype(F32))
        h1[0, rows, :] = (norm * (1.0 + scale_one) + shift_one).astype(BF16)

    rows_loop(first_norm, go_h1)

    def mlp_grad(rows):
        dml[0, rows, :] = (gate_two * cot[rows, :].astype(F32)).astype(BF16)

    rows_loop(mlp_grad, go_dml)
    sums[...] = jnp.zeros_like(sums)

    def heads_forward(image):
        for part in range(3):
            qkv_f[part * head_cols : (part + 1) * head_cols, :] = dot(
                wqkv[part * head_cols : (part + 1) * head_cols, :], h1[image], 1, 1
            )
        cosine, sine = cos_t[image], sin_t[image]
        ok = valid[image][:, :1] > 0.0

        def head(h, carry):
            at = image * heads + h
            rows = pl.ds(pl.multiple_of(h * HD, 8), HD)
            query = qkv_f[rows, :]
            key = qkv_f[pl.ds(pl.multiple_of(head_cols + h * HD, 8), HD), :]
            value = qkv_f[pl.ds(pl.multiple_of(2 * head_cols + h * HD, 8), HD), :].astype(BF16)
            query = ((query * cosine + rotate_rows(query) * sine) * scale).astype(BF16)
            key = (key * cosine + rotate_rows(key) * sine).astype(BF16)
            q_s[at], k_s[at], v_s[at] = query, key, value
            scores = dot(key, query, 0, 0)
            scores = jnp.where(ok, scores, -1e30)
            top = jnp.max(scores, axis=0, keepdims=True)
            exps = jnp.exp(scores - top)
            probs = exps * (1.0 / jnp.sum(exps, axis=0, keepdims=True))
            p_s[at] = probs
            a_f[rows, :] = dot(value, probs.astype(BF16), 1, 0)
            return carry

        lax.fori_loop(0, heads, head, 0)
        a_t[image] = a_f[...].astype(BF16)

    def strips_of(make, send=None, copies=None, keep=None):
        for c in range(strips):
            cols = slice(c * STRIP, (c + 1) * STRIP)
            value = make(cols)
            if send is not None:
                send[:, cols] = value.astype(BF16)
                copies[c].start()
            else:
                keep[:, cols] = value

    loads[0].wait()
    heads_forward(0)
    for copy in go_h1:
        copy.wait_recv()
    heads_forward(1)
    loads[1].wait()
    strips_of(lambda cols: dot(a_t[1], wout[:, cols], 0, 0), send_a, go_a)
    strips_of(lambda cols: dot(a_t[0], wout[:, cols], 0, 0), keep=own)
    for copy in go_a:
        copy.wait_recv()

    def second_norm(rows):
        branch = own[rows, :] + recv_a[rows, :].astype(F32)
        attn[rows, :] = branch
        middle = tok[rows, :].astype(F32) + gate_one * branch
        norm, _ = normed(middle)
        h2[0, rows, :] = (norm * (1.0 + scale_two) + shift_two).astype(BF16)

    rows_loop(second_norm, go_h2)

    for load in loads[2:]:
        load.wait()

    def feed_forward(image):
        def tile(j, carry):
            cols = pl.ds(pl.multiple_of(j * TILE, TILE), TILE)
            gate = dot(h2[image], wg[:, cols], 1, 0)
            up = dot(h2[image], wu[:, cols], 1, 0)
            grad = dot(dml[image], wdown[cols, :], 1, 1)
            sig = jax.nn.sigmoid(gate)
            act = gate * sig
            hid[image, :, cols] = (act * up).astype(BF16)
            dgate[image, :, cols] = (grad * up * sig * (1.0 + gate * (1.0 - sig))).astype(BF16)
            dup[image, :, cols] = (grad * act).astype(BF16)
            return carry

        lax.fori_loop(0, inner // TILE, tile, 0)

    for copy in go_dml:
        copy.wait_recv()
    feed_forward(0)
    for copy in go_h2:
        copy.wait_recv()
    feed_forward(1)

    def dh2_strip(image):
        return lambda cols: dot(dgate[image], wg[cols, :], 1, 1) + dot(dup[image], wu[cols, :], 1, 1)

    def mlp_strip(image):
        return lambda cols: dot(hid[image], wdown[:, cols], 1, 0)

    for copy in go_a:
        copy.wait_send()
    strips_of(dh2_strip(1), send_a, go_b)
    strips_of(mlp_strip(1), send_c, go_c)
    strips_of(dh2_strip(0), keep=own)

    def turned(left, order):
        for image in range(2):
            flat = left[image].astype(F32).T
            chunk = width // plan["count"]
            for pair in range(plan["count"] // 2):
                place = [2 * pair, 2 * pair + 1]
                parts = []
                for spot in place:
                    which = 0
                    for level, stride in enumerate(order):
                        which += stride * ((spot >> (len(order) - 1 - level)) & 1)
                    parts.append(flat[which * chunk : (which + 1) * chunk])
                flip[2 * pair * chunk : 2 * (pair + 1) * chunk, image * LEN : (image + 1) * LEN] = (
                    jnp.concatenate(parts, axis=0).astype(BF16)
                )

    if plan["fused"]:
        (give_one, land0, final, gsend, grecv, osem, credit, *spots) = extra
        many = len(plan["pieces"])
        land1, land2, land3, held3 = (spots[n * many : (n + 1) * many] for n in range(4))
        half = width // 2
        gives = [wu.at[pl.ds(half, half)], give_one]
        core_bit = bit_of(1)
        state = {"gives": 0, "lands": 0}

        class Piece:
            def __init__(self, name, order, columns, padded, keep, offset, result, at):
                self.name, self.order, self.columns, self.padded = name, order, columns, padded
                self.keep, self.offset, self.result, self.at = keep, offset, result, at
                self.index = plan["pieces"].index(name)
                self.lanes = pl.ds(offset, padded)
                self.copies = {}

            def send(self, level, src, dst):
                copy = pltpu.make_async_remote_copy(
                    src_ref=src, dst_ref=dst, send_sem=gsend.at[self.index, level],
                    recv_sem=grecv.at[self.index, level], device_id=partner(self.order[level]),
                    device_id_type=MESH,
                )
                copy.start()
                self.copies[level] = copy

            def compute(self, right, give):
                self.give = gives[give]
                step = STRIP

                def tile(start, size, pad):
                    total = right(start, size)
                    low, high = total[:half], total[half:]
                    kept = jnp.where(core_bit == 0, low, high).astype(BF16)
                    gone = jnp.where(core_bit == 0, high, low).astype(BF16)
                    place = self.offset + start
                    if pad > size:
                        blank = jnp.zeros((half, pad - size), BF16)
                        kept = jnp.concatenate([kept, blank], axis=1)
                        gone = jnp.concatenate([gone, blank], axis=1)
                    if not isinstance(start, int):
                        place = pl.multiple_of(place, 128)
                        start = pl.multiple_of(start, 128)
                    self.keep[:, pl.ds(place, pad)] = kept
                    self.give[:, pl.ds(start, pad)] = gone

                whole = self.columns // step

                def one(n, carry):
                    tile(n * step, step, step)
                    return carry

                lax.fori_loop(0, whole, one, 0)
                left = self.columns - whole * step
                if left:
                    tile(whole * step, left, self.padded - whole * step)

            def go(self):
                pl.semaphore_wait(credit, 1)
                self.send(0, self.give.at[:, pl.ds(0, self.padded)], land0.at[:, pl.ds(0, self.padded)])

            def add(self, level):
                rows = half >> level
                base = 0
                for before in range(1, level + 1):
                    base = base + bit_of(self.order[before]) * (half >> before)
                self.copies[level].wait_recv()
                cut = pl.ds(0, self.padded)
                if level == 0:
                    source = land0
                elif level == 1:
                    source = land1[self.index]
                elif level == 2:
                    source = land2[self.index]
                if level < 2:
                    block = 48

                    def one(n, carry):
                        there = pl.ds(pl.multiple_of(n * block, 16), block)
                        here = pl.ds(pl.multiple_of(base + n * block, 16), block)
                        self.keep[here, self.lanes] = (
                            self.keep[here, self.lanes].astype(F32) + source[there, cut].astype(F32)
                        ).astype(BF16)
                        return carry

                    lax.fori_loop(0, rows // block, one, 0)
                    if level == 0:
                        pl.semaphore_signal(
                            credit, inc=1, device_id=partner(1), device_id_type=MESH
                        )
                    quarter = rows // 2
                    off = pl.multiple_of(base + (1 - bit_of(self.order[level + 1])) * quarter, 16)
                    target = (land1, land2)[level][self.index]
                    self.send(level + 1, self.keep.at[pl.ds(off, quarter), self.lanes], target)
                elif level == 2:
                    here = pl.ds(pl.multiple_of(base, 16), rows)
                    total = self.keep[here, self.lanes].astype(F32) + source[:, cut].astype(F32)
                    held3[self.index][0] = total[: rows // 2].astype(BF16)
                    held3[self.index][1] = total[rows // 2 :].astype(BF16)
                    bit = bit_of(self.order[3])
                    self.send(3, held3[self.index].at[1 - bit], land3[self.index].at[0])
                else:
                    bit = bit_of(self.order[3])
                    if state.get("final") is not None:
                        state["final"].wait()
                    final[:, cut] = held3[self.index][bit].astype(F32) + land3[self.index][
                        0
                    ].astype(F32)
                    copy = pltpu.make_async_copy(
                        final.at[:, cut], self.result.at[:, pl.ds(self.at, self.padded)], osem
                    )
                    copy.start()
                    state["final"] = copy

            def close(self):
                for copy in self.copies.values():
                    copy.wait_send()

        pl.semaphore_signal(credit, inc=1, device_id=partner(1), device_id_type=MESH)
        y_first, z_first = plan["orders"]
        low, high = wg.at[pl.ds(0, half)], wg.at[pl.ds(half, half)]
        third = [wqkv.at[pl.ds(n * half, half)] for n in range(3)]
        p_down = Piece("down", y_first, inner, inner, low, 0, results[0], 0)
        p_gate = Piece("gate", y_first, inner, inner, high, 0, results[0], inner)
        p_up = Piece("up", z_first, inner, inner, wu.at[pl.ds(0, half)], 0, results[0], 2 * inner)
        qk_cols = 2 * head_cols
        v_pad = -(-head_cols // 128) * 128
        p_qk = Piece("qk", y_first, qk_cols, qk_cols, third[0], 0, results[0], 3 * inner)
        p_v = Piece("v", y_first, head_cols, v_pad, third[1], 0, results[0], 3 * inner + qk_cols)
        p_out = Piece(
            "out", y_first, head_cols, v_pad, third[2], 0, results[0], 3 * inner + qk_cols + v_pad
        )

    def lane_right(array):
        def right(start, size):
            if not isinstance(start, int):
                start = pl.multiple_of(start, 128)
            part = [array[i, :, pl.ds(start, size)] for i in range(2)]
            return dot(flip[:, 0:LEN], part[0], 1, 0) + dot(flip[:, LEN:], part[1], 1, 0)
        return right

    def row_right(array, base):
        def right(start, size):
            at = base + start
            if not isinstance(start, int):
                at = pl.multiple_of(at, 16)
            part = [array[i, pl.ds(at, size), :] for i in range(2)]
            return dot(flip[:, 0:LEN], part[0], 1, 1) + dot(flip[:, LEN:], part[1], 1, 1)
        return right

    def plain_grad(right, columns, target):
        (stage, gsem) = extra
        pend = {}
        for n, start in enumerate(range(0, columns, TILE)):
            size = min(TILE, columns - start)
            slot = n % 2
            if slot in pend:
                pend[slot].wait()
            stage[slot, :, 0:size] = right(start, size).astype(BF16)
            copy = pltpu.make_async_copy(
                stage.at[slot], target.at[:, pl.ds(start, TILE)], gsem.at[slot]
            )
            copy.start()
            pend[slot] = copy
        for copy in pend.values():
            copy.wait()

    def plain_grad_in(left, right, columns, target):
        for image in range(2):
            flip[:, image * LEN : (image + 1) * LEN] = left[image].astype(F32).T.astype(BF16)
        plain_grad(right, columns, target)

    if plan["fused"]:
        turned(dml, y_first)
        p_down.compute(lane_right(hid), 0)
        p_down.go()
        turned(h2, y_first)
        p_gate.compute(lane_right(dgate), 1)
        p_down.add(0)
        p_gate.go()
    else:
        plain_grad_in(dml, lane_right(hid), inner, results[0])
        plain_grad_in(h2, lane_right(dgate), inner, results[1])
        plain_grad_in(h2, lane_right(dup), inner, results[2])

    for copy in go_b:
        copy.wait_recv()

    def second_back(rows):
        grad = own[rows, :] + recv_b[rows, :].astype(F32)
        norm, inverse = normed(tok[rows, :].astype(F32) + gate_one * attn[rows, :])
        middle = cot[rows, :].astype(F32) + norm_back(grad * (1.0 + scale_two), norm, inverse)
        dx1[rows, :] = middle
        dat[0, rows, :] = (gate_one * middle).astype(BF16)
        sums[2] += fold(middle * attn[rows, :])
        sums[3] += fold(grad)
        sums[4] += fold(grad * norm)

    rows_loop(second_back, go_dat)

    if plan["fused"]:
        p_gate.add(0)
        p_down.copies[0].wait_send()
        turned(h2, z_first)
        p_up.compute(lane_right(dup), 0)
        p_up.go()

    def heads_back(image):
        a_f[...] = dot(wout[...], dat[image], 1, 1)
        cosine, sine = cos_t[image], sin_t[image]

        def head(h, carry):
            at = image * heads + h
            rows = pl.ds(pl.multiple_of(h * HD, 8), HD)
            da = a_f[rows, :].astype(BF16)
            probs = p_s[at]
            query, key, value = q_s[at], k_s[at], v_s[at]
            dprobs = dot(value, da, 0, 0)
            dvalue = dot(da, probs.astype(BF16), 1, 1)
            inside = jnp.sum(probs * dprobs, axis=0, keepdims=True)
            dscores = (probs * (dprobs - inside)).astype(BF16)
            dquery = dot(key, dscores, 1, 0)
            dkey = dot(query, dscores, 1, 1)
            dquery = (dquery * cosine - rotate_rows(dquery * sine)) * scale
            dkey = dkey * cosine - rotate_rows(dkey * sine)
            qkv_f[rows, :] = dquery
            qkv_f[pl.ds(pl.multiple_of(head_cols + h * HD, 8), HD), :] = dkey
            qkv_f[pl.ds(pl.multiple_of(2 * head_cols + h * HD, 8), HD), :] = dvalue
            return carry

        lax.fori_loop(0, heads, head, 0)
        dqkv[image] = qkv_f[...].astype(BF16)

    heads_back(0)
    if plan["fused"]:
        p_up.add(0)
    for copy in go_dat:
        copy.wait_recv()
    heads_back(1)

    def dh1_strip(image):
        return lambda cols: dot(dqkv[image], wqkv[:, cols], 0, 0)

    for copy in go_b:
        copy.wait_send()
    strips_of(dh1_strip(1), send_a, go_d)
    strips_of(dh1_strip(0), keep=own)

    if plan["fused"]:
        p_gate.copies[0].wait_send()
        p_up.copies[0].wait_send()
        turned(h1, y_first)
        p_qk.compute(row_right(dqkv, 0), 0)
        p_qk.go()
        p_v.compute(row_right(dqkv, 2 * head_cols), 1)
        p_qk.add(0)
        p_v.go()
        p_qk.copies[0].wait_send()
        turned(dat, y_first)
        p_out.compute(row_right(a_t, 0), 0)
        p_v.add(0)
        p_out.go()
        p_down.add(1)
        p_up.add(1)
        p_out.add(0)
    else:
        plain_grad_in(h1, row_right(dqkv, 0), 3 * head_cols, results[3])
        plain_grad_in(dat, row_right(a_t, 0), head_cols, results[4])

    for copy in go_d:
        copy.wait_recv()

    def first_back(rows):
        grad = own[rows, :] + recv_a[rows, :].astype(F32)
        norm, inverse = normed(tok[rows, :].astype(F32))
        dtok[rows, :] = dx1[rows, :] + norm_back(grad * (1.0 + scale_one), norm, inverse)
        sums[0] += fold(grad)
        sums[1] += fold(grad * norm)

    rows_loop(first_back)

    strips_of(mlp_strip(0), keep=own)
    for copy in go_c:
        copy.wait_recv()

    def finish(rows):
        branch = own[rows, :] + recv_c[rows, :].astype(F32)
        out[rows, :] = (
            tok[rows, :].astype(F32) + gate_one * attn[rows, :] + gate_two * branch
        ).astype(BF16)
        sums[5] += fold(cot[rows, :].astype(F32) * branch)

    rows_loop(finish)
    for n in range(6):
        dmod[n : n + 1, :] = jnp.sum(sums[n], axis=0, keepdims=True)
    if plan["fused"]:
        p_down.add(2)
        p_gate.add(1)
        p_down.add(3)
        p_up.add(2)
        p_qk.add(1)
        p_gate.add(2)
        p_up.add(3)
        p_v.add(1)
        p_qk.add(2)
        p_gate.add(3)
        p_out.add(1)
        p_v.add(2)
        p_qk.add(3)
        p_out.add(2)
        p_v.add(3)
        p_out.add(3)
        state["final"].wait()
        pl.semaphore_wait(credit, 1)
        for piece in (p_gate, p_up, p_qk, p_v, p_out, p_down):
            for level, copy in piece.copies.items():
                if level > 0 or piece in (p_v, p_out):
                    copy.wait_send()
    for copy in (*go_h1, *go_dml, *go_h2, *go_dat, *go_c, *go_d):
        copy.wait_send()


def run_block(tok, cot, mod, cos_t, sin_t, valid, wqkv, wout, wgu, wdown):
    width = tok.shape[1]
    head_cols = wout.shape[0]
    heads = head_cols // HD
    inner = wdown.shape[0]
    strips = width // STRIP
    count = lax.axis_size("dp")
    vmem = pl.BlockSpec(memory_space=pltpu.VMEM)
    hbm = pl.BlockSpec(memory_space=pl.ANY)
    V = pltpu.VMEM
    D = pltpu.SemaphoreType.DMA
    copies = 8 + 4 * strips
    fused = count == 16 and width % (8 * count) == 0
    names = ["down", "gate", "up", "qk", "v", "out"]
    pad = -(-head_cols // 128) * 128
    if fused:
        results = [jax.ShapeDtypeStruct((width // count, 3 * inner + 2 * head_cols + 2 * pad), F32)]
        chunk = width // count
        widths = [inner, inner, inner, 2 * head_cols, pad, pad]
        extra = [
            V((width // 2, inner), BF16),
            V((width // 2, inner), BF16),
            V((chunk, inner), F32),
            D((len(names), 4)),
            D((len(names), 4)),
            D(()),
            pltpu.SemaphoreType.REGULAR,
            *[V((width // 4, w), BF16) for w in widths],
            *[V((width // 8, w), BF16) for w in widths],
            *[V((1, chunk, w), BF16) for w in widths],
            *[V((2, chunk, w), BF16) for w in widths],
        ]
        strides = [1, 2, 4, 8]
    else:
        wide = [inner, inner, inner, 3 * head_cols, head_cols]
        results = [jax.ShapeDtypeStruct((width, -(-w // TILE) * TILE), BF16) for w in wide]
        extra = [V((2, width, TILE), BF16), D((2,))]
        strides = []
    plan = {
        "fused": fused, "results": len(results), "count": count, "pieces": names,
        "strides": strides, "orders": ((1, 2, 4, 8), (1, 4, 2, 8)),
    }
    return pl.pallas_call(
        functools.partial(block_kernel, plan),
        out_shape=(
            jax.ShapeDtypeStruct((LEN, width), BF16),
            jax.ShapeDtypeStruct((LEN, width), F32),
            jax.ShapeDtypeStruct((6, width), F32),
            *results,
        ),
        in_specs=[vmem] * 6 + [hbm] * 4,
        out_specs=[vmem] * 3 + [hbm] * len(results),
        scratch_shapes=[
            V(wqkv.shape, BF16), V(wout.shape, BF16), V(wgu.shape[1:], BF16),
            V(wgu.shape[1:], BF16), V(wdown.shape, BF16),
            *[V((2, LEN, width), BF16)] * 4,
            *[V((2 * heads, HD, LEN), BF16)] * 3,
            V((2 * heads, LEN, LEN), F32),
            V((3 * head_cols, LEN), F32),
            V((head_cols, LEN), F32),
            V((2, head_cols, LEN), BF16),
            *[V((2, LEN, inner), BF16)] * 3,
            V((2, 3 * head_cols, LEN), BF16),
            *[V((LEN, width), F32)] * 3,
            *[V((LEN, width), BF16)] * 5,
            V((width, 2 * LEN), BF16),
            V((6, 8, width), F32),
            D((5,)),
            D((copies,)),
            D((copies,)),
            *extra,
        ],
        compiler_params=pltpu.CompilerParams(
            collective_id=0, has_side_effects=True, vmem_limit_bytes=62 * 1024 * 1024
        ),
    )(tok, cot, mod, cos_t, sin_t, valid, wqkv, wout, wgu, wdown)


def rope_tables(grid_shape):
    position = jnp.arange(LEN, dtype=jnp.int32)[None, :]
    widths = grid_shape[:, 1:2]
    rows_at = position // widths
    cols_at = position % widths
    key_valid = position < grid_shape[:, 0:1] * widths
    quarter = HD // 4
    frequency = 10000.0 ** (-jnp.arange(quarter, dtype=F32) / quarter)
    row_angle = rows_at.astype(F32)[:, None, :] * frequency[:, None]
    col_angle = cols_at.astype(F32)[:, None, :] * frequency[:, None]
    angles = jnp.concatenate([row_angle, row_angle, col_angle, col_angle], axis=1)
    valid = jnp.broadcast_to(key_valid.astype(F32)[:, :, None], (*key_valid.shape, 128))
    return jnp.cos(angles), jnp.sin(angles), valid


def sum_over_images(partial):
    count = lax.axis_size("dp")
    me = lax.axis_index("dp")
    held = partial.reshape(count, partial.shape[0] // count, partial.shape[1])
    stride = 1
    left = count
    while left > 1:
        bit = (me // stride) % 2
        pairs = held.reshape(left // 2, 2, *held.shape[1:])
        keep = lax.dynamic_index_in_dim(pairs, bit, 1, keepdims=False)
        send = lax.dynamic_index_in_dim(pairs, 1 - bit, 1, keepdims=False)
        came = lax.ppermute(send, "dp", [(i, i ^ stride) for i in range(count)])
        held = keep.astype(F32) + came.astype(F32)
        left //= 2
        stride *= 2
        if left > 1:
            held = held.astype(BF16)
    return held[0]


def body(tokens, condition, grid_shape, w_ada, b_ada, w_qkv, w_out, w_gate_up, w_down, cotangent):
    width = tokens.shape[1]
    inner = w_down.shape[0]
    head_cols = w_out.shape[0]
    cond = condition.astype(F32)
    cond_sigmoid = jax.nn.sigmoid(cond)
    silu_cond = (cond * cond_sigmoid).astype(BF16)
    mod = jnp.dot(silu_cond, w_ada, preferred_element_type=F32) + b_ada.astype(F32)
    mod = mod.reshape(6, width)
    mine = lax.axis_index("tensor")
    grid_shape = jnp.where(mine == 0, grid_shape, grid_shape[::-1])
    cos_t, sin_t, valid = rope_tables(grid_shape)
    wqkv = w_qkv.transpose(1, 2, 0).reshape(3 * head_cols, width)
    layer_out, d_tokens, d_mod, *grads = run_block(
        tokens, cotangent, mod, cos_t, sin_t, valid, wqkv, w_out,
        w_gate_up.transpose(1, 0, 2), w_down,
    )
    if len(grads) == 1:
        whole = grads[0]
        pad = -(-head_cols // 128) * 128
        grad_down = whole[:, :inner].T
        grad_gate_up = whole[:, inner : 3 * inner].reshape(-1, 2, inner)
        grad_qkv = whole[:, 3 * inner : 3 * inner + 3 * head_cols].reshape(-1, 3, head_cols)
        start = 3 * inner + 2 * head_cols + pad
        grad_out = whole[:, start : start + head_cols].T
    else:
        grad_down = sum_over_images(grads[0]).T
        grad_gate_up = jnp.stack([sum_over_images(grads[1]), sum_over_images(grads[2])], axis=1)
        grad_qkv = sum_over_images(grads[3][:, : 3 * head_cols]).reshape(-1, 3, head_cols)
        grad_out = sum_over_images(grads[4][:, :head_cols]).T
    d_mod = d_mod.reshape(1, 6 * width).astype(BF16)
    d_condition = (
        dot(d_mod, w_ada, 1, 1) * cond_sigmoid * (1.0 + cond * (1.0 - cond_sigmoid))
    )
    devices_all = lax.axis_size("dp") * lax.axis_size("tensor")
    own_cols = 6 * width // devices_all
    packed = jnp.concatenate(
        [
            d_mod.reshape(devices_all, own_cols),
            jnp.broadcast_to(silu_cond, (devices_all, width)),
        ],
        axis=1,
    )
    packed = jnp.pad(packed, ((0, 0), (0, -packed.shape[1] % 128)))
    packed = lax.all_to_all(
        packed.reshape(devices_all, -1, 128), ("dp", "tensor"), 0, 0, tiled=True
    ).reshape(devices_all, -1)
    columns = packed[:, :own_cols]
    silu_rows = packed[:, own_cols : own_cols + width]
    weight_part = dot(silu_rows, columns, 0, 0)
    bias_part = jnp.sum(columns.astype(F32), axis=0)
    return (
        layer_out, d_tokens, d_condition, weight_part, bias_part,
        grad_qkv, grad_out, grad_gate_up, grad_down,
    )


def solution(mesh):
    placed = (
        P(("dp", "tensor"), None),
        P(("dp", "tensor"), None),
        P("dp", None),
        P(),
        P(),
        P(None, None, "tensor"),
        P("tensor", None),
        P(None, None, "tensor"),
        P("tensor", None),
        P(("dp", "tensor"), None),
    )
    return jax.shard_map(
        body,
        mesh=mesh,
        in_specs=placed,
        out_specs=(
            P(("dp", "tensor"), None),
            P(("dp", "tensor"), None),
            P(("dp", "tensor"), None),
            P(None, ("dp", "tensor")),
            P(("dp", "tensor")),
            P("dp", None, "tensor"),
            P("tensor", "dp"),
            P("dp", None, "tensor"),
            P("tensor", "dp"),
        ),
        check_vma=False,
    )
```

```python
import functools

import jax
import jax.numpy as jnp
from jax import lax
from jax.experimental import pallas as pl
from jax.experimental.pallas import tpu as pltpu
from jax.sharding import PartitionSpec as P

HD = 72
LEN = 256
EPSILON = 1e-06
MESH = pl.DeviceIdType.MESH
F32 = jnp.float32
BF16 = jnp.bfloat16
ROWS = 32
STRIP = 384
TILE = 256


def dot(left, right, left_dim, right_dim):
    return lax.dot_general(
        left, right, (((left_dim,), (right_dim,)), ((), ())), preferred_element_type=F32
    )


def normed(values):
    centered = values - jnp.mean(values, axis=-1, keepdims=True)
    variance = jnp.mean(centered * centered, axis=-1, keepdims=True)
    inverse = lax.rsqrt(variance + EPSILON)
    return centered * inverse, inverse


def norm_back(upstream, norm, inverse):
    mean_grad = jnp.mean(upstream, axis=-1, keepdims=True)
    mean_cross = jnp.mean(upstream * norm, axis=-1, keepdims=True)
    return inverse * (upstream - mean_grad - norm * mean_cross)


def rotate_rows(values):
    quarter = HD // 4
    a, b = values[:quarter], values[quarter : 2 * quarter]
    c, d = values[2 * quarter : 3 * quarter], values[3 * quarter :]
    return jnp.concatenate([-b, a, -d, c], axis=0)


def fold(values):
    return jnp.sum(values.reshape(values.shape[0] // 8, 8, values.shape[1]), axis=0)


def block_kernel(
    plan, tok, cot, cond, grid, bias,
    wada_hbm, wqkv_hbm, wout_hbm, wgu_hbm, wdown_hbm,
    out, dtok, *rest,
):
    results, rest = rest[: plan["results"]], rest[plan["results"] :]
    (
        mod, silu_two, cos_t, sin_t, raw,
        wqkv, wout, wg, wu, wdown,
        h1, h2, dml, dat,
        q_s, k_s, v_s, p_s, qkv_f, a_f, a_t,
        hid, dgate, dup, dqkv,
        attn, dx1, own,
        send_a, send_c, recv_a, recv_b, recv_c,
        flip, sums,
        wsem, asem, ssem, rsem, *extra,
    ) = rest
    width = tok.shape[1]
    heads = q_s.shape[0] // 2
    head_cols = heads * HD
    inner = wdown.shape[0]
    side = lax.axis_index("tensor")
    mate = {"tensor": 1 - side}
    scale = HD ** (-0.5)

    loads = [
        pltpu.make_async_copy(src, dst, wsem.at[i])
        for i, (src, dst) in enumerate(
            ((wqkv_hbm, wqkv), (wout_hbm, wout), (wdown_hbm, wdown))
        )
    ]
    half_rows = width // 2
    slots = [
        ref.at[pl.ds(n * half_rows, half_rows), pl.ds(0, width)] for ref in (wg, wu) for n in range(2)
    ]

    class Stream:
        def __init__(self, blocks, slots):
            self.chunks = [(b, h) for b in blocks for h in range(2)]
            self.slots = slots
            self.copies = []
            self.at = 0

        def fill(self, most):
            while len(self.copies) < min(most, len(self.chunks), self.at + len(self.slots)):
                n = len(self.copies)
                b, h = self.chunks[n]
                copy = pltpu.make_async_copy(
                    wada_hbm.at[pl.ds(h * half_rows, half_rows), pl.ds(b * width, width)],
                    self.slots[n % len(self.slots)], asem.at[n % len(self.slots)],
                )
                copy.start()
                self.copies.append(copy)

        def take(self):
            n = self.at
            self.copies[n].wait()
            b, h = self.chunks[n]
            self.at += 1
            return b, h, self.slots[n % len(self.slots)]

    stream = Stream((0, 1, 5, 2, 3, 4), slots)
    stream.fill(4)
    for load in loads:
        load.start()

    me = lax.axis_index("dp")

    def bit_of(stride):
        return lax.rem(lax.div(me, stride), 2)

    def partner(stride):
        return {"dp": me + stride - 2 * stride * bit_of(stride)}

    barrier = pltpu.get_barrier_semaphore()
    friends = [mate] + [partner(s) for s in plan["strides"]]
    for friend in friends:
        pl.semaphore_signal(barrier, inc=1, device_id=friend, device_id_type=MESH)
    pl.semaphore_wait(barrier, len(friends))

    def give(src, dst, slot):
        return pltpu.make_async_remote_copy(
            src_ref=src, dst_ref=dst, send_sem=ssem.at[slot], recv_sem=rsem.at[slot],
            device_id=mate, device_id_type=MESH,
        )

    def gather(buf, slot):
        half = LEN // 2
        return [
            give(buf.at[0, pl.ds(c * half, half)], buf.at[1, pl.ds(c * half, half)], slot + c)
            for c in range(2)
        ]

    strips = width // STRIP

    def scatter(send, recv, slot):
        return [
            give(
                send.at[:, pl.ds(c * STRIP, STRIP)], recv.at[:, pl.ds(c * STRIP, STRIP)], slot + c
            )
            for c in range(strips)
        ]

    go_h1, go_dml, go_h2, go_dat = (gather(b, 2 * i) for i, b in enumerate((h1, dml, h2, dat)))
    go_a, go_b, go_c, go_d = (
        scatter(s, r, 8 + strips * i)
        for i, (s, r) in enumerate(
            ((send_a, recv_a), (send_a, recv_b), (send_c, recv_c), (send_a, recv_a))
        )
    )

    def rows_loop(step, copies=None):
        half = LEN // 2
        count = half // ROWS
        for c in range(2):
            def one(i, carry, c=c):
                step(pl.ds(pl.multiple_of(c * half + i * ROWS, ROWS), ROWS))
                return carry
            lax.fori_loop(0, count, one, 0)
            if copies is not None:
                copies[c].start()

    cond_f = cond[...].astype(F32)
    cond_sig = jax.nn.sigmoid(cond_f)
    silu = (cond_f * cond_sig).astype(BF16)
    silu_rows = jnp.broadcast_to(silu.astype(F32), (16, width))
    for h in range(2):
        silu_two[h] = silu_rows[:, h * half_rows : (h + 1) * half_rows].astype(BF16)

    def modulate(count):
        for _ in range(count):
            row = None
            for _ in range(2):
                b, h, slot = stream.take()
                part = dot(silu_two[h], slot[...], 1, 0)[0:1]
                row = part if row is None else row + part
                stream.fill(99)
            mod[b : b + 1, :] = row + bias[b : b + 1, :].astype(F32)

    modulate(2)
    shift_one, scale_one = mod[0:1], mod[1:2]

    def first_norm(rows):
        norm, _ = normed(tok[rows, :].astype(F32))
        h1[0, rows, :] = (norm * (1.0 + scale_one) + shift_one).astype(BF16)

    rows_loop(first_norm, go_h1)
    modulate(1)
    gate_two = mod[5:6]

    def mlp_grad(rows):
        dml[0, rows, :] = (gate_two * cot[rows, :].astype(F32)).astype(BF16)

    rows_loop(mlp_grad, go_dml)
    sums[...] = jnp.zeros_like(sums)

    quarter = HD // 4
    limits = []
    for image in range(2):
        at = side if image == 0 else 1 - side
        tall, wide = grid[at, 0], grid[at, 1]
        limits.append(tall * wide)
        spot = lax.broadcasted_iota(jnp.int32, (1, LEN), 1).astype(F32)
        wide_f = jnp.full((1, LEN), wide, jnp.int32).astype(F32)
        row_at = jnp.floor((spot + 0.5) / wide_f)
        col_at = spot - row_at * wide_f
        step = lax.broadcasted_iota(jnp.int32, (quarter, LEN), 0).astype(F32)
        frequency = jnp.exp(step * (-9.210340371976184 / quarter))
        both = jnp.concatenate([row_at * frequency, col_at * frequency], axis=0)
        for table, turn in ((cos_t, jnp.cos), (sin_t, jnp.sin)):
            seen = turn(both)
            first, second = seen[:quarter], seen[quarter:]
            table[image] = jnp.concatenate([first, first, second, second], axis=0)

    def heads_forward(image):
        for part in range(3):
            qkv_f[part * head_cols : (part + 1) * head_cols, :] = dot(
                wqkv[part * head_cols : (part + 1) * head_cols, :], h1[image], 1, 1
            )
        cosine, sine = cos_t[image], sin_t[image]
        ok = lax.broadcasted_iota(jnp.int32, (LEN, LEN), 0) < limits[image]

        def head(h, carry):
            at = image * heads + h
            rows = pl.ds(pl.multiple_of(h * HD, 8), HD)
            query = qkv_f[rows, :]
            key = qkv_f[pl.ds(pl.multiple_of(head_cols + h * HD, 8), HD), :]
            value = qkv_f[pl.ds(pl.multiple_of(2 * head_cols + h * HD, 8), HD), :].astype(BF16)
            query = ((query * cosine + rotate_rows(query) * sine) * scale).astype(BF16)
            key = (key * cosine + rotate_rows(key) * sine).astype(BF16)
            q_s[at], k_s[at], v_s[at] = query, key, value
            scores = dot(key, query, 0, 0)
            scores = jnp.where(ok, scores, -1e30)
            top = jnp.max(scores, axis=0, keepdims=True)
            exps = jnp.exp(scores - top)
            probs = exps * (1.0 / jnp.sum(exps, axis=0, keepdims=True))
            p_s[at] = probs
            a_f[rows, :] = dot(value, probs.astype(BF16), 1, 0)
            return carry

        lax.fori_loop(0, heads, head, 0)
        a_t[image] = a_f[...].astype(BF16)

    def strips_of(make, send=None, copies=None, keep=None):
        for c in range(strips):
            cols = slice(c * STRIP, (c + 1) * STRIP)
            value = make(cols)
            if send is not None:
                send[:, cols] = value.astype(BF16)
                copies[c].start()
            else:
                keep[:, cols] = value

    loads[0].wait()
    heads_forward(0)
    modulate(3)
    gate_one, shift_two, scale_two = mod[2:3], mod[3:4], mod[4:5]
    for copy in go_h1:
        copy.wait_recv()
    heads_forward(1)
    loads[1].wait()
    strips_of(lambda cols: dot(a_t[1], wout[:, cols], 0, 0), send_a, go_a)
    strips_of(lambda cols: dot(a_t[0], wout[:, cols], 0, 0), keep=own)

    depth = raw.shape[1]

    def fetch(n, slot):
        return pltpu.make_async_copy(
            wgu_hbm.at[pl.ds(pl.multiple_of(n * depth, depth), depth)], raw.at[slot], wsem.at[3 + slot]
        )

    fetch(0, 0).start()
    r = lax.broadcasted_iota(jnp.int32, (2 * depth, 2 * depth), 0)
    c = lax.broadcasted_iota(jnp.int32, (2 * depth, 2 * depth), 1)
    sorter = jnp.where(c == jnp.where(r < depth, 2 * r, 2 * (r - depth) + 1), 1.0, 0.0).astype(BF16)

    def apart(n, carry):
        slot = lax.rem(n, 2)

        @pl.when(n + 1 < width // depth)
        def _():
            fetch(n + 1, 1 - slot).start()

        fetch(n, slot).wait()
        parted = dot(sorter, raw[slot].reshape(2 * depth, inner), 1, 0).astype(BF16)
        rows = pl.ds(pl.multiple_of(n * depth, depth), depth)
        wg[rows, :] = parted[:depth]
        wu[rows, :] = parted[depth:]
        return carry

    lax.fori_loop(0, width // depth, apart, 0)
    for copy in go_a:
        copy.wait_recv()

    def second_norm(rows):
        branch = own[rows, :] + recv_a[rows, :].astype(F32)
        attn[rows, :] = branch
        middle = tok[rows, :].astype(F32) + gate_one * branch
        norm, _ = normed(middle)
        h2[0, rows, :] = (norm * (1.0 + scale_two) + shift_two).astype(BF16)

    rows_loop(second_norm, go_h2)

    loads[2].wait()

    def feed_forward(image):
        def tile(j, carry):
            cols = pl.ds(pl.multiple_of(j * TILE, TILE), TILE)
            gate = dot(h2[image], wg[:, cols], 1, 0)
            up = dot(h2[image], wu[:, cols], 1, 0)
            grad = dot(dml[image], wdown[cols, :], 1, 1)
            sig = jax.nn.sigmoid(gate)
            act = gate * sig
            hid[image, :, cols] = (act * up).astype(BF16)
            dgate[image, :, cols] = (grad * up * sig * (1.0 + gate * (1.0 - sig))).astype(BF16)
            dup[image, :, cols] = (grad * act).astype(BF16)
            return carry

        lax.fori_loop(0, inner // TILE, tile, 0)

    for copy in go_dml:
        copy.wait_recv()
    feed_forward(0)
    for copy in go_h2:
        copy.wait_recv()
    feed_forward(1)

    def dh2_strip(image):
        return lambda cols: dot(dgate[image], wg[cols, :], 1, 1) + dot(dup[image], wu[cols, :], 1, 1)

    def mlp_strip(image):
        return lambda cols: dot(hid[image], wdown[:, cols], 1, 0)

    for copy in go_a:
        copy.wait_send()
    strips_of(dh2_strip(1), send_a, go_b)
    strips_of(mlp_strip(1), send_c, go_c)
    strips_of(dh2_strip(0), keep=own)

    def turned(left, order):
        for image in range(2):
            flat = left[image].astype(F32).T
            chunk = width // plan["count"]
            for pair in range(plan["count"] // 2):
                place = [2 * pair, 2 * pair + 1]
                parts = []
                for spot in place:
                    which = 0
                    for level, stride in enumerate(order):
                        which += stride * ((spot >> (len(order) - 1 - level)) & 1)
                    parts.append(flat[which * chunk : (which + 1) * chunk])
                flip[2 * pair * chunk : 2 * (pair + 1) * chunk, image * LEN : (image + 1) * LEN] = (
                    jnp.concatenate(parts, axis=0).astype(BF16)
                )

    if plan["fused"]:
        (
            give_one, land0, final, gsend, grecv, osem, credit, packs, came, dflat, dcond, psem,
            *spots,
        ) = extra
        _, ada_out, cond_out, bias_out = results
        dflat[...] = jnp.zeros_like(dflat)
        dcond[...] = jnp.zeros_like(dcond)
        many = len(plan["pieces"])
        land1, land2, land3, held3 = (spots[n * many : (n + 1) * many] for n in range(4))
        half = width // 2
        gives = [wu.at[pl.ds(half, half)], give_one]
        core_bit = bit_of(1)
        state = {"gives": 0, "lands": 0}

        class Piece:
            def __init__(self, name, order, columns, padded, keep, offset, result, at):
                self.name, self.order, self.columns, self.padded = name, order, columns, padded
                self.keep, self.offset, self.result, self.at = keep, offset, result, at
                self.index = plan["pieces"].index(name)
                self.lanes = pl.ds(offset, padded)
                self.copies = {}

            def send(self, level, src, dst):
                copy = pltpu.make_async_remote_copy(
                    src_ref=src, dst_ref=dst, send_sem=gsend.at[self.index, level],
                    recv_sem=grecv.at[self.index, level], device_id=partner(self.order[level]),
                    device_id_type=MESH,
                )
                copy.start()
                self.copies[level] = copy

            def compute(self, right, give):
                self.give = gives[give]
                step = STRIP

                def tile(start, size, pad):
                    total = right(start, size)
                    low, high = total[:half], total[half:]
                    kept = jnp.where(core_bit == 0, low, high).astype(BF16)
                    gone = jnp.where(core_bit == 0, high, low).astype(BF16)
                    place = self.offset + start
                    if pad > size:
                        blank = jnp.zeros((half, pad - size), BF16)
                        kept = jnp.concatenate([kept, blank], axis=1)
                        gone = jnp.concatenate([gone, blank], axis=1)
                    if not isinstance(start, int):
                        place = pl.multiple_of(place, 128)
                        start = pl.multiple_of(start, 128)
                    self.keep[:, pl.ds(place, pad)] = kept
                    self.give[:, pl.ds(start, pad)] = gone

                whole = self.columns // step

                def one(n, carry):
                    tile(n * step, step, step)
                    return carry

                lax.fori_loop(0, whole, one, 0)
                left = self.columns - whole * step
                if left:
                    tile(whole * step, left, self.padded - whole * step)

            def go(self):
                pl.semaphore_wait(credit, 1)
                self.send(0, self.give.at[:, pl.ds(0, self.padded)], land0.at[:, pl.ds(0, self.padded)])

            def add(self, level):
                rows = half >> level
                base = 0
                for before in range(1, level + 1):
                    base = base + bit_of(self.order[before]) * (half >> before)
                self.copies[level].wait_recv()
                cut = pl.ds(0, self.padded)
                if level == 0:
                    source = land0
                elif level == 1:
                    source = land1[self.index]
                elif level == 2:
                    source = land2[self.index]
                if level < 2:
                    block = 48

                    def one(n, carry):
                        there = pl.ds(pl.multiple_of(n * block, 16), block)
                        here = pl.ds(pl.multiple_of(base + n * block, 16), block)
                        self.keep[here, self.lanes] = (
                            self.keep[here, self.lanes].astype(F32) + source[there, cut].astype(F32)
                        ).astype(BF16)
                        return carry

                    lax.fori_loop(0, rows // block, one, 0)
                    if level == 0:
                        pl.semaphore_signal(
                            credit, inc=1, device_id=partner(1), device_id_type=MESH
                        )
                    quarter = rows // 2
                    off = pl.multiple_of(base + (1 - bit_of(self.order[level + 1])) * quarter, 16)
                    target = (land1, land2)[level][self.index]
                    self.send(level + 1, self.keep.at[pl.ds(off, quarter), self.lanes], target)
                elif level == 2:
                    here = pl.ds(pl.multiple_of(base, 16), rows)
                    total = self.keep[here, self.lanes].astype(F32) + source[:, cut].astype(F32)
                    held3[self.index][0] = total[: rows // 2].astype(BF16)
                    held3[self.index][1] = total[rows // 2 :].astype(BF16)
                    bit = bit_of(self.order[3])
                    self.send(3, held3[self.index].at[1 - bit], land3[self.index].at[0])
                else:
                    bit = bit_of(self.order[3])
                    if state.get("final") is not None:
                        state["final"].wait()
                    final[:, cut] = held3[self.index][bit].astype(F32) + land3[self.index][
                        0
                    ].astype(F32)
                    copy = pltpu.make_async_copy(
                        final.at[:, cut], self.result.at[:, pl.ds(self.at, self.padded)], osem
                    )
                    copy.start()
                    state["final"] = copy

            def close(self):
                for copy in self.copies.values():
                    copy.wait_send()

        pl.semaphore_signal(credit, inc=1, device_id=partner(1), device_id_type=MESH)
        y_first, z_first = plan["orders"]
        low, high = wg.at[pl.ds(0, half)], wg.at[pl.ds(half, half)]
        third = [wqkv.at[pl.ds(n * half, half)] for n in range(3)]
        p_down = Piece("down", y_first, inner, inner, low, 0, results[0], 0)
        p_gate = Piece("gate", y_first, inner, inner, high, 0, results[0], inner)
        p_up = Piece("up", z_first, inner, inner, wu.at[pl.ds(0, half)], 0, results[0], 2 * inner)
        qk_cols = 2 * head_cols
        v_pad = -(-head_cols // 128) * 128
        p_qk = Piece("qk", y_first, qk_cols, qk_cols, third[0], 0, results[0], 3 * inner)
        p_v = Piece("v", y_first, head_cols, v_pad, third[1], 0, results[0], 3 * inner + qk_cols)
        p_out = Piece(
            "out", y_first, head_cols, v_pad, third[2], 0, results[0], 3 * inner + qk_cols + v_pad
        )

        tail = Stream(
            (3, 4, 2, 5, 0, 1), [wdown.at[pl.ds(n * half, half)] for n in range(2)] + [wout]
        )
        devices = plan["devices"]
        side_count = plan["sides"]
        mine = me * side_count + side
        own_cols = plan["own_cols"]

        def condition_back(blocks):
            for block in blocks:
                row = jnp.sum(sums[block], axis=0, keepdims=True)
                dflat[0:1, block * width : (block + 1) * width] = row
                rows = jnp.broadcast_to(row, (16, width)).astype(BF16)
                for _ in range(2):
                    b, h, slot = tail.take()
                    dcond[h : h + 1, :] += dot(rows, slot[...], 1, 1)[0:1]
                    tail.fill(99)

        def share_out():
            lanes = lax.broadcasted_iota(jnp.int32, (16, 128), 0)
            base = jnp.zeros((16, 128), F32)
            silu_f = silu.astype(F32)
            for n in range(width // 128):
                base = jnp.where(lanes == n, silu_f[:, n * 128 : (n + 1) * 128], base)
            row_a = width // 128
            for n in range(devices):
                first = dflat[0:1, n * own_cols : n * own_cols + 128]
                rest = own_cols - 128
                second = dflat[0:1, n * own_cols + 128 : n * own_cols + 256]
                packet = jnp.where(lanes == row_a, first, base)
                packet = jnp.where(lanes == row_a + 1, second, packet)
                packs[n] = packet.astype(BF16)

            def one(n, carry):
                other = lax.rem(mine + n, devices)
                pltpu.make_async_remote_copy(
                    src_ref=packs.at[other], dst_ref=came.at[mine], send_sem=psem.at[0],
                    recv_sem=psem.at[1],
                    device_id={
                        "dp": lax.div(other, side_count), "tensor": lax.rem(other, side_count)
                    },
                    device_id_type=MESH,
                ).start()
                return carry

            lax.fori_loop(1, devices, one, 0)
            came[mine] = packs[mine]

        def take_in():
            every = pl.ds(0, devices - 1)
            whole = pltpu.make_async_remote_copy(
                src_ref=packs.at[every], dst_ref=came.at[every], send_sem=psem.at[0],
                recv_sem=psem.at[1], device_id=mate, device_id_type=MESH,
            )
            whole.wait_send()
            whole.wait_recv()
            seen = came[...].astype(F32)
            row_a = width // 128
            silu_all = jnp.concatenate([seen[:, n, :] for n in range(row_a)], axis=1).astype(BF16)
            columns = jnp.concatenate([seen[:, row_a, :], seen[:, row_a + 1, :]], axis=1)
            bias_out[...] = jnp.broadcast_to(jnp.sum(columns, axis=0, keepdims=True), bias_out.shape)
            value = dot(silu_all, columns.astype(BF16), 0, 0)
            for n in range(-(-width // LEN)):
                size = min(LEN, width - n * LEN)
                p_s[n, 0:size, :] = value[n * LEN : n * LEN + size]
                copy = pltpu.make_async_copy(
                    p_s.at[n, pl.ds(0, size)], ada_out.at[pl.ds(n * LEN, size)], asem.at[n]
                )
                copy.start()
                copy.wait()
            slope = cond_sig * (1.0 + cond_f * (1.0 - cond_sig))
            whole_row = jnp.concatenate([dcond[0:1, :], dcond[1:2, :]], axis=1)
            cond_out[...] = whole_row * slope

    def lane_right(array):
        def right(start, size):
            if not isinstance(start, int):
                start = pl.multiple_of(start, 128)
            part = [array[i, :, pl.ds(start, size)] for i in range(2)]
            return dot(flip[:, 0:LEN], part[0], 1, 0) + dot(flip[:, LEN:], part[1], 1, 0)
        return right

    def row_right(array, base):
        def right(start, size):
            at = base + start
            if not isinstance(start, int):
                at = pl.multiple_of(at, 16)
            part = [array[i, pl.ds(at, size), :] for i in range(2)]
            return dot(flip[:, 0:LEN], part[0], 1, 1) + dot(flip[:, LEN:], part[1], 1, 1)
        return right

    def plain_grad(right, columns, target):
        (stage, gsem) = extra
        pend = {}
        for n, start in enumerate(range(0, columns, TILE)):
            size = min(TILE, columns - start)
            slot = n % 2
            if slot in pend:
                pend[slot].wait()
            stage[slot, :, 0:size] = right(start, size).astype(BF16)
            copy = pltpu.make_async_copy(
                stage.at[slot], target.at[:, pl.ds(start, TILE)], gsem.at[slot]
            )
            copy.start()
            pend[slot] = copy
        for copy in pend.values():
            copy.wait()

    def plain_grad_in(left, right, columns, target):
        for image in range(2):
            flip[:, image * LEN : (image + 1) * LEN] = left[image].astype(F32).T.astype(BF16)
        plain_grad(right, columns, target)

    if plan["fused"]:
        turned(dml, y_first)
        p_down.compute(lane_right(hid), 0)
        p_down.go()
        turned(h2, y_first)
        p_gate.compute(lane_right(dgate), 1)
        p_down.add(0)
        p_gate.go()
    else:
        plain_grad_in(dml, lane_right(hid), inner, results[0])
        plain_grad_in(h2, lane_right(dgate), inner, results[1])
        plain_grad_in(h2, lane_right(dup), inner, results[2])

    for copy in go_b:
        copy.wait_recv()

    def second_back(rows):
        grad = own[rows, :] + recv_b[rows, :].astype(F32)
        norm, inverse = normed(tok[rows, :].astype(F32) + gate_one * attn[rows, :])
        middle = cot[rows, :].astype(F32) + norm_back(grad * (1.0 + scale_two), norm, inverse)
        dx1[rows, :] = middle
        dat[0, rows, :] = (gate_one * middle).astype(BF16)
        sums[2] += fold(middle * attn[rows, :])
        sums[3] += fold(grad)
        sums[4] += fold(grad * norm)

    rows_loop(second_back, go_dat)

    if plan["fused"]:
        p_gate.add(0)
        p_down.copies[0].wait_send()
        turned(h2, z_first)
        p_up.compute(lane_right(dup), 0)
        p_up.go()

    def heads_back(image):
        a_f[...] = dot(wout[...], dat[image], 1, 1)
        cosine, sine = cos_t[image], sin_t[image]

        def head(h, carry):
            at = image * heads + h
            rows = pl.ds(pl.multiple_of(h * HD, 8), HD)
            da = a_f[rows, :].astype(BF16)
            probs = p_s[at]
            query, key, value = q_s[at], k_s[at], v_s[at]
            dprobs = dot(value, da, 0, 0)
            dvalue = dot(da, probs.astype(BF16), 1, 1)
            inside = jnp.sum(probs * dprobs, axis=0, keepdims=True)
            dscores = (probs * (dprobs - inside)).astype(BF16)
            dquery = dot(key, dscores, 1, 0)
            dkey = dot(query, dscores, 1, 1)
            dquery = (dquery * cosine - rotate_rows(dquery * sine)) * scale
            dkey = dkey * cosine - rotate_rows(dkey * sine)
            qkv_f[rows, :] = dquery
            qkv_f[pl.ds(pl.multiple_of(head_cols + h * HD, 8), HD), :] = dkey
            qkv_f[pl.ds(pl.multiple_of(2 * head_cols + h * HD, 8), HD), :] = dvalue
            return carry

        lax.fori_loop(0, heads, head, 0)
        dqkv[image] = qkv_f[...].astype(BF16)

    heads_back(0)
    strips_of(mlp_strip(0), keep=own)
    for copy in go_c:
        copy.wait_recv()

    def finish(rows):
        branch = own[rows, :] + recv_c[rows, :].astype(F32)
        out[rows, :] = (
            tok[rows, :].astype(F32) + gate_one * attn[rows, :] + gate_two * branch
        ).astype(BF16)
        sums[5] += fold(cot[rows, :].astype(F32) * branch)

    rows_loop(finish)
    if plan["fused"]:
        p_up.add(0)
    for copy in go_dat:
        copy.wait_recv()
    heads_back(1)

    def dh1_strip(image):
        return lambda cols: dot(dqkv[image], wqkv[:, cols], 0, 0)

    for copy in go_b:
        copy.wait_send()
    strips_of(dh1_strip(1), send_a, go_d)
    strips_of(dh1_strip(0), keep=own)

    if plan["fused"]:
        p_gate.copies[0].wait_send()
        p_up.copies[0].wait_send()
        turned(h1, y_first)
        p_qk.compute(row_right(dqkv, 0), 0)
        p_qk.go()
        p_v.compute(row_right(dqkv, 2 * head_cols), 1)
        p_qk.add(0)
        p_v.go()
        p_qk.copies[0].wait_send()
        turned(dat, y_first)
        p_out.compute(row_right(a_t, 0), 0)
        p_v.add(0)
        p_out.go()
        p_down.add(1)
        p_up.add(1)
        p_out.add(0)
        tail.fill(99)
        condition_back((3, 4, 2, 5))
    else:
        plain_grad_in(h1, row_right(dqkv, 0), 3 * head_cols, results[3])
        plain_grad_in(dat, row_right(a_t, 0), head_cols, results[4])

    for copy in go_d:
        copy.wait_recv()

    def first_back(rows):
        grad = own[rows, :] + recv_a[rows, :].astype(F32)
        norm, inverse = normed(tok[rows, :].astype(F32))
        dtok[rows, :] = dx1[rows, :] + norm_back(grad * (1.0 + scale_one), norm, inverse)
        sums[0] += fold(grad)
        sums[1] += fold(grad * norm)

    rows_loop(first_back)

    if plan["fused"]:
        condition_back((0, 1))
    else:
        for n in range(6):
            results[5][n : n + 1, :] = jnp.sum(sums[n], axis=0, keepdims=True)
    if plan["fused"]:
        p_down.add(2)
        p_gate.add(1)
        p_down.add(3)
        share_out()
        p_up.add(2)
        p_qk.add(1)
        p_gate.add(2)
        p_up.add(3)
        p_v.add(1)
        p_qk.add(2)
        p_gate.add(3)
        p_out.add(1)
        p_v.add(2)
        p_qk.add(3)
        p_out.add(2)
        p_v.add(3)
        p_out.add(3)
        take_in()
        state["final"].wait()
        pl.semaphore_wait(credit, 1)
        for piece in (p_gate, p_up, p_qk, p_v, p_out, p_down):
            for level, copy in piece.copies.items():
                if level > 0 or piece in (p_v, p_out):
                    copy.wait_send()
    for copy in (*go_h1, *go_dml, *go_h2, *go_dat, *go_c, *go_d):
        copy.wait_send()


def run_block(tok, cot, cond, grid, bias, wada, wqkv, wout, wgu, wdown):
    width = tok.shape[1]
    head_cols = wout.shape[0]
    heads = head_cols // HD
    inner = wdown.shape[0]
    strips = width // STRIP
    count = lax.axis_size("dp")
    sides = lax.axis_size("tensor")
    devices = count * sides
    own_cols = 6 * width // devices
    vmem = pl.BlockSpec(memory_space=pltpu.VMEM)
    hbm = pl.BlockSpec(memory_space=pl.ANY)
    V = pltpu.VMEM
    D = pltpu.SemaphoreType.DMA
    copies = 8 + 4 * strips
    fused = count == 16 and width % (8 * count) == 0 and 128 < own_cols <= 256
    names = ["down", "gate", "up", "qk", "v", "out"]
    pad = -(-head_cols // 128) * 128
    if fused:
        results = [
            jax.ShapeDtypeStruct((width // count, 3 * inner + 2 * head_cols + 2 * pad), F32),
            jax.ShapeDtypeStruct((width, 256), F32),
            jax.ShapeDtypeStruct((1, width), F32),
            jax.ShapeDtypeStruct((8, 256), F32),
        ]
        result_specs = [hbm, hbm, vmem, vmem]
        chunk = width // count
        widths = [inner, inner, inner, 2 * head_cols, pad, pad]
        extra = [
            V((width // 2, inner), BF16),
            V((width // 2, inner), BF16),
            V((chunk, inner), F32),
            D((len(names), 4)),
            D((len(names), 4)),
            D(()),
            pltpu.SemaphoreType.REGULAR,
            V((devices, 16, 128), BF16),
            V((devices, 16, 128), BF16),
            V((8, 6 * width + 128), F32),
            V((8, width // 2), F32),
            D((2,)),
            *[V((width // 4, w), BF16) for w in widths],
            *[V((width // 8, w), BF16) for w in widths],
            *[V((1, chunk, w), BF16) for w in widths],
            *[V((2, chunk, w), BF16) for w in widths],
        ]
        strides = [1, 2, 4, 8]
    else:
        wide = [inner, inner, inner, 3 * head_cols, head_cols]
        results = [jax.ShapeDtypeStruct((width, -(-w // TILE) * TILE), BF16) for w in wide]
        results += [jax.ShapeDtypeStruct((6, width), F32)]
        result_specs = [hbm] * 5 + [vmem]
        extra = [V((2, width, TILE), BF16), D((2,))]
        strides = []
    plan = {
        "fused": fused, "results": len(results), "count": count, "pieces": names,
        "devices": devices, "sides": sides, "own_cols": own_cols,
        "strides": strides, "orders": ((1, 2, 4, 8), (1, 4, 2, 8)),
    }
    return pl.pallas_call(
        functools.partial(block_kernel, plan),
        out_shape=(
            jax.ShapeDtypeStruct((LEN, width), BF16),
            jax.ShapeDtypeStruct((LEN, width), F32),
            *results,
        ),
        in_specs=[vmem] * 3 + [pl.BlockSpec(memory_space=pltpu.SMEM), vmem] + [hbm] * 5,
        out_specs=[vmem] * 2 + result_specs,
        scratch_shapes=[
            V((8, width), F32), V((2, 16, width // 2), BF16), V((2, HD, LEN), F32),
            V((2, HD, LEN), F32), V((2, 32, 2, inner), BF16),
                        V(wqkv.shape, BF16), V(wout.shape, BF16), V((width, inner), BF16),
            V((width, inner), BF16), V(wdown.shape, BF16),
            *[V((2, LEN, width), BF16)] * 4,
            *[V((2 * heads, HD, LEN), BF16)] * 3,
            V((2 * heads, LEN, LEN), F32),
            V((3 * head_cols, LEN), F32),
            V((head_cols, LEN), F32),
            V((2, head_cols, LEN), BF16),
            *[V((2, LEN, inner), BF16)] * 3,
            V((2, 3 * head_cols, LEN), BF16),
            *[V((LEN, width), F32)] * 3,
            *[V((LEN, width), BF16)] * 5,
            V((width, 2 * LEN), BF16),
            V((6, 8, width), F32),
            D((5,)),
            D((8,)),
            D((copies,)),
            D((copies,)),
            *extra,
        ],
        compiler_params=pltpu.CompilerParams(
            collective_id=0, has_side_effects=True, vmem_limit_bytes=62 * 1024 * 1024
        ),
    )(tok, cot, cond, grid, bias, wada, wqkv, wout, wgu, wdown)


def sum_over_images(partial):
    count = lax.axis_size("dp")
    me = lax.axis_index("dp")
    held = partial.reshape(count, partial.shape[0] // count, partial.shape[1])
    stride = 1
    left = count
    while left > 1:
        bit = (me // stride) % 2
        pairs = held.reshape(left // 2, 2, *held.shape[1:])
        keep = lax.dynamic_index_in_dim(pairs, bit, 1, keepdims=False)
        send = lax.dynamic_index_in_dim(pairs, 1 - bit, 1, keepdims=False)
        came = lax.ppermute(send, "dp", [(i, i ^ stride) for i in range(count)])
        held = keep.astype(F32) + came.astype(F32)
        left //= 2
        stride *= 2
        if left > 1:
            held = held.astype(BF16)
    return held[0]


def body(tokens, condition, grid_shape, w_ada, b_ada, w_qkv, w_out, w_gate_up, w_down, cotangent):
    width = tokens.shape[1]
    inner = w_down.shape[0]
    head_cols = w_out.shape[0]
    wqkv = w_qkv.transpose(1, 2, 0).reshape(3 * head_cols, width)
    layer_out, d_tokens, *grads = run_block(
        tokens, cotangent, condition, grid_shape, b_ada.reshape(6, width), w_ada, wqkv, w_out,
        w_gate_up, w_down,
    )
    devices_all = lax.axis_size("dp") * lax.axis_size("tensor")
    own_cols = 6 * width // devices_all
    if len(grads) == 4:
        whole, ada, d_condition, bias_rows = grads
        weight_part = ada[:, :own_cols]
        bias_part = bias_rows[0, :own_cols]
        pad = -(-head_cols // 128) * 128
        grad_down = whole[:, :inner].T
        grad_gate_up = whole[:, inner : 3 * inner].reshape(-1, 2, inner)
        grad_qkv = whole[:, 3 * inner : 3 * inner + 3 * head_cols].reshape(-1, 3, head_cols)
        start = 3 * inner + 2 * head_cols + pad
        grad_out = whole[:, start : start + head_cols].T
    else:
        grad_down = sum_over_images(grads[0]).T
        grad_gate_up = jnp.stack([sum_over_images(grads[1]), sum_over_images(grads[2])], axis=1)
        grad_qkv = sum_over_images(grads[3][:, : 3 * head_cols]).reshape(-1, 3, head_cols)
        grad_out = sum_over_images(grads[4][:, :head_cols]).T
        cond = condition.astype(F32)
        cond_sigmoid = jax.nn.sigmoid(cond)
        silu_cond = (cond * cond_sigmoid).astype(BF16)
        d_mod = grads[5].reshape(1, 6 * width).astype(BF16)
        d_condition = (
            dot(d_mod, w_ada, 1, 1) * cond_sigmoid * (1.0 + cond * (1.0 - cond_sigmoid))
        )
        packed = jnp.concatenate(
            [
                d_mod.reshape(devices_all, own_cols),
                jnp.broadcast_to(silu_cond, (devices_all, width)),
            ],
            axis=1,
        )
        packed = jnp.pad(packed, ((0, 0), (0, -packed.shape[1] % 128)))
        packed = lax.all_to_all(
            packed.reshape(devices_all, -1, 128), ("dp", "tensor"), 0, 0, tiled=True
        ).reshape(devices_all, -1)
        columns = packed[:, :own_cols]
        silu_rows = packed[:, own_cols : own_cols + width]
        weight_part = dot(silu_rows, columns, 0, 0)
        bias_part = jnp.sum(columns.astype(F32), axis=0)
    return (
        layer_out, d_tokens, d_condition, weight_part, bias_part,
        grad_qkv, grad_out, grad_gate_up, grad_down,
    )


def solution(mesh):
    placed = (
        P(("dp", "tensor"), None),
        P(("dp", "tensor"), None),
        P("dp", None),
        P(),
        P(),
        P(None, None, "tensor"),
        P("tensor", None),
        P(None, None, "tensor"),
        P("tensor", None),
        P(("dp", "tensor"), None),
    )
    return jax.shard_map(
        body,
        mesh=mesh,
        in_specs=placed,
        out_specs=(
            P(("dp", "tensor"), None),
            P(("dp", "tensor"), None),
            P(("dp", "tensor"), None),
            P(None, ("dp", "tensor")),
            P(("dp", "tensor")),
            P("dp", None, "tensor"),
            P("tensor", "dp"),
            P("dp", None, "tensor"),
            P("tensor", "dp"),
        ),
        check_vma=False,
    )
```

```python
import functools

import jax
import jax.numpy as jnp
from jax import lax
from jax.experimental import pallas as pl
from jax.experimental.pallas import tpu as pltpu
from jax.sharding import PartitionSpec as P

HD = 72
LEN = 256
EPSILON = 1e-06
MESH = pl.DeviceIdType.MESH
F32 = jnp.float32
BF16 = jnp.bfloat16
ROWS = 32
STRIP = 384
TILE = 256


def dot(left, right, left_dim, right_dim):
    return lax.dot_general(
        left, right, (((left_dim,), (right_dim,)), ((), ())), preferred_element_type=F32
    )


def normed(values):
    centered = values - jnp.mean(values, axis=-1, keepdims=True)
    variance = jnp.mean(centered * centered, axis=-1, keepdims=True)
    inverse = lax.rsqrt(variance + EPSILON)
    return centered * inverse, inverse


def norm_back(upstream, norm, inverse):
    mean_grad = jnp.mean(upstream, axis=-1, keepdims=True)
    mean_cross = jnp.mean(upstream * norm, axis=-1, keepdims=True)
    return inverse * (upstream - mean_grad - norm * mean_cross)


def rotate_rows(values):
    quarter = HD // 4
    a, b = values[:quarter], values[quarter : 2 * quarter]
    c, d = values[2 * quarter : 3 * quarter], values[3 * quarter :]
    return jnp.concatenate([-b, a, -d, c], axis=0)


def fold(values):
    return jnp.sum(values.reshape(values.shape[0] // 8, 8, values.shape[1]), axis=0)


def block_kernel(
    plan, tok, cot, cond, grid, bias,
    wada_hbm, wqkv_hbm, wout_hbm, wgu_hbm, wdown_hbm,
    out, dtok, *rest,
):
    results, rest = rest[: plan["results"]], rest[plan["results"] :]
    (
        mod, silu_two, cos_t, sin_t, raw,
        wqkv, wout, wg, wu, wdown,
        h1, h2, dml, dat,
        q_s, k_s, v_s, p_s, qkv_f, a_f, a_t,
        hid, dgate, dup, dqkv,
        attn, dx1, own,
        send_a, send_c, recv_a, recv_c, row_out, row_in,
        flip, sums,
        wsem, asem, ssem, rsem, *extra,
    ) = rest
    width = tok.shape[1]
    heads = q_s.shape[0] // 2
    head_cols = heads * HD
    inner = wdown.shape[0]
    side = lax.axis_index("tensor")
    mate = {"tensor": 1 - side}
    scale = HD ** (-0.5)

    loads = [
        pltpu.make_async_copy(src, dst, wsem.at[i])
        for i, (src, dst) in enumerate(
            ((wqkv_hbm, wqkv), (wout_hbm, wout), (wdown_hbm, wdown))
        )
    ]
    half_rows = width // 2
    slots = [
        ref.at[pl.ds(n * half_rows, half_rows), pl.ds(0, width)] for ref in (wg, wu) for n in range(2)
    ]

    class Stream:
        def __init__(self, blocks, slots):
            self.chunks = [(b, h) for b in blocks for h in range(2)]
            self.slots = slots
            self.copies = []
            self.at = 0

        def fill(self, most):
            while len(self.copies) < min(most, len(self.chunks), self.at + len(self.slots)):
                n = len(self.copies)
                b, h = self.chunks[n]
                copy = pltpu.make_async_copy(
                    wada_hbm.at[pl.ds(h * half_rows, half_rows), pl.ds(b * width, width)],
                    self.slots[n % len(self.slots)], asem.at[n % len(self.slots)],
                )
                copy.start()
                self.copies.append(copy)

        def take(self):
            n = self.at
            self.copies[n].wait()
            b, h = self.chunks[n]
            self.at += 1
            return b, h, self.slots[n % len(self.slots)]

    stream = Stream((0, 1, 5, 2, 3, 4), slots)
    stream.fill(4)
    for load in loads:
        load.start()

    me = lax.axis_index("dp")

    def bit_of(stride):
        return lax.rem(lax.div(me, stride), 2)

    def partner(stride):
        return {"dp": me + stride - 2 * stride * bit_of(stride)}

    barrier = pltpu.get_barrier_semaphore()
    friends = [mate] + [partner(s) for s in plan["strides"]]
    for friend in friends:
        pl.semaphore_signal(barrier, inc=1, device_id=friend, device_id_type=MESH)

    def give(src, dst, slot):
        return pltpu.make_async_remote_copy(
            src_ref=src, dst_ref=dst, send_sem=ssem.at[slot], recv_sem=rsem.at[slot],
            device_id=mate, device_id_type=MESH,
        )

    def gather(buf, slot):
        half = LEN // 2
        return [
            give(buf.at[0, pl.ds(c * half, half)], buf.at[1, pl.ds(c * half, half)], slot + c)
            for c in range(2)
        ]

    strips = width // STRIP

    def scatter(send, recv, slot):
        return [
            give(
                send.at[:, pl.ds(c * STRIP, STRIP)], recv.at[:, pl.ds(c * STRIP, STRIP)], slot + c
            )
            for c in range(strips)
        ]

    go_h1, go_h2, go_dat = (gather(b, 2 * i) for i, b in enumerate((h1, h2, dat)))
    go_cot = [
        give(cot.at[pl.ds(c * (LEN // 2), LEN // 2)], dml.at[1, pl.ds(c * (LEN // 2), LEN // 2)], 6 + c)
        for c in range(2)
    ]
    go_row = give(row_out, row_in, 8 + 4 * (width // STRIP))
    go_a, go_b, go_c, go_d = (
        scatter(s, r, 8 + strips * i)
        for i, (s, r) in enumerate(
            ((send_a, recv_a), (send_a, recv_a), (send_c, recv_c), (send_a, recv_a))
        )
    )

    def rows_loop(step, copies=None):
        half = LEN // 2
        count = half // ROWS
        for c in range(2):
            def one(i, carry, c=c):
                step(pl.ds(pl.multiple_of(c * half + i * ROWS, ROWS), ROWS))
                return carry
            lax.fori_loop(0, count, one, 0)
            if copies is not None:
                copies[c].start()

    cond_f = cond[...].astype(F32)
    cond_sig = jax.nn.sigmoid(cond_f)
    silu = (cond_f * cond_sig).astype(BF16)
    silu_rows = jnp.broadcast_to(silu.astype(F32), (16, width))
    for h in range(2):
        silu_two[h] = silu_rows[:, h * half_rows : (h + 1) * half_rows].astype(BF16)

    bias_f = bias[...].astype(F32)
    tiles = width // bias.shape[1]

    def bias_row(b):
        return jnp.concatenate([bias_f[b * tiles + n : b * tiles + n + 1] for n in range(tiles)], axis=1)

    def modulate(count):
        for _ in range(count):
            row = None
            for _ in range(2):
                b, h, slot = stream.take()
                part = dot(silu_two[h], slot[...], 1, 0)[0:1]
                row = part if row is None else row + part
                stream.fill(99)
            mod[b : b + 1, :] = row + bias_row(b)

    def pre_norm(rows):
        norm, _ = normed(tok[rows, :].astype(F32))
        dx1[rows, :] = norm

    rows_loop(pre_norm)
    pl.semaphore_wait(barrier, len(friends))
    go_cot[0].start()
    modulate(2)
    shift_one, scale_one = mod[0:1], mod[1:2]

    def first_norm(rows):
        h1[0, rows, :] = (dx1[rows, :] * (1.0 + scale_one) + shift_one).astype(BF16)

    rows_loop(first_norm, go_h1)
    modulate(1)
    gate_two = mod[5:6]
    row_out[...] = jnp.broadcast_to(gate_two, row_out.shape)
    go_row.start()
    go_cot[1].start()
    sums[...] = jnp.zeros_like(sums)

    quarter = HD // 4
    limits = []
    for image in range(2):
        at = side if image == 0 else 1 - side
        tall, wide = grid[at, 0], grid[at, 1]
        limits.append(tall * wide)
        spot = lax.broadcasted_iota(jnp.int32, (1, LEN), 1).astype(F32)
        wide_f = jnp.full((1, LEN), wide, jnp.int32).astype(F32)
        row_at = jnp.floor((spot + 0.5) / wide_f)
        col_at = spot - row_at * wide_f
        step = lax.broadcasted_iota(jnp.int32, (quarter, LEN), 0).astype(F32)
        frequency = jnp.exp(step * (-9.210340371976184 / quarter))
        both = jnp.concatenate([row_at * frequency, col_at * frequency], axis=0)
        for table, turn in ((cos_t, jnp.cos), (sin_t, jnp.sin)):
            seen = turn(both)
            first, second = seen[:quarter], seen[quarter:]
            table[image] = jnp.concatenate([first, first, second, second], axis=0)

    depth = raw.shape[1]
    ring = raw.shape[0]
    parts = {"next": 0, "copies": []}
    r = lax.broadcasted_iota(jnp.int32, (2 * depth, 2 * depth), 0)
    c = lax.broadcasted_iota(jnp.int32, (2 * depth, 2 * depth), 1)
    sorter = jnp.where(c == jnp.where(r < depth, 2 * r, 2 * (r - depth) + 1), 1.0, 0.0).astype(BF16)

    def fetch(n):
        if n < width // depth:
            copy = pltpu.make_async_copy(
                wgu_hbm.at[pl.ds(n * depth, depth)], raw.at[n % ring], wsem.at[3 + n % ring]
            )
            copy.start()
            parts["copies"].append(copy)

    def pull_apart(until):
        while parts["next"] < until:
            n = parts["next"]
            parts["copies"][n].wait()
            parted = dot(sorter, raw[n % ring].reshape(2 * depth, inner), 1, 0).astype(BF16)
            wg[n * depth : (n + 1) * depth, :] = parted[:depth]
            wu[n * depth : (n + 1) * depth, :] = parted[depth:]
            fetch(n + ring)
            parts["next"] += 1

    def heads_forward(image):
        for part in range(3):
            qkv_f[part * head_cols : (part + 1) * head_cols, :] = dot(
                wqkv[part * head_cols : (part + 1) * head_cols, :], h1[image], 1, 1
            )
        cosine, sine = cos_t[image], sin_t[image]
        ok = lax.broadcasted_iota(jnp.int32, (LEN, LEN), 0) < limits[image]

        def head(h, carry):
            at = image * heads + h
            rows = pl.ds(pl.multiple_of(h * HD, 8), HD)
            query = qkv_f[rows, :]
            key = qkv_f[pl.ds(pl.multiple_of(head_cols + h * HD, 8), HD), :]
            value = qkv_f[pl.ds(pl.multiple_of(2 * head_cols + h * HD, 8), HD), :].astype(BF16)
            query = ((query * cosine + rotate_rows(query) * sine) * scale).astype(BF16)
            key = (key * cosine + rotate_rows(key) * sine).astype(BF16)
            q_s[at], k_s[at], v_s[at] = query, key, value
            scores = dot(key, query, 0, 0)
            scores = jnp.where(ok, scores, -1e30)
            top = jnp.max(scores, axis=0, keepdims=True)
            exps = jnp.exp(scores - top)
            probs = exps * (1.0 / jnp.sum(exps, axis=0, keepdims=True))
            p_s[at] = probs
            a_f[rows, :] = dot(value, probs.astype(BF16), 1, 0)
            return carry

        lax.fori_loop(0, heads, head, 0, unroll=2)
        a_t[image] = a_f[...].astype(BF16)

    def strips_of(make, send=None, copies=None, keep=None):
        for c in range(strips):
            cols = slice(c * STRIP, (c + 1) * STRIP)
            value = make(cols)
            if send is not None:
                send[:, cols] = value.astype(BF16)
                copies[c].start()
            else:
                keep[:, cols] = value

    for n in range(ring):
        fetch(n)
    loads[0].wait()
    heads_forward(0)
    modulate(3)
    pull_apart(plan["early"])
    gate_one, shift_two, scale_two = mod[2:3], mod[3:4], mod[4:5]
    for copy in go_h1:
        copy.wait_recv()
    heads_forward(1)
    loads[1].wait()
    strips_of(lambda cols: dot(a_t[1], wout[:, cols], 0, 0), send_a, go_a)
    strips_of(lambda cols: dot(a_t[0], wout[:, cols], 0, 0), keep=own)

    for copy in go_cot:
        copy.wait_recv()
    go_row.wait_recv()
    gate_mate = row_in[0:1]

    def mlp_grad(rows):
        dml[0, rows, :] = (gate_two * cot[rows, :].astype(F32)).astype(BF16)
        dml[1, rows, :] = (gate_mate * dml[1, rows, :].astype(F32)).astype(BF16)

    rows_loop(mlp_grad)

    pull_apart(width // depth)
    for copy in go_a:
        copy.wait_recv()

    def second_norm(rows):
        branch = own[rows, :] + recv_a[rows, :].astype(F32)
        attn[rows, :] = branch
        middle = tok[rows, :].astype(F32) + gate_one * branch
        norm, _ = normed(middle)
        h2[0, rows, :] = (norm * (1.0 + scale_two) + shift_two).astype(BF16)

    rows_loop(second_norm, go_h2)

    loads[2].wait()

    def feed_forward(image):
        def tile(j, carry):
            cols = pl.ds(pl.multiple_of(j * TILE, TILE), TILE)
            gate = dot(h2[image], wg[:, cols], 1, 0)
            up = dot(h2[image], wu[:, cols], 1, 0)
            grad = dot(dml[image], wdown[cols, :], 1, 1)
            sig = jax.nn.sigmoid(gate)
            act = gate * sig
            hid[image, :, cols] = (act * up).astype(BF16)
            dgate[image, :, cols] = (grad * up * sig * (1.0 + gate * (1.0 - sig))).astype(BF16)
            dup[image, :, cols] = (grad * act).astype(BF16)
            return carry

        lax.fori_loop(0, inner // TILE, tile, 0)

    feed_forward(0)
    for copy in go_h2:
        copy.wait_recv()
    feed_forward(1)

    def dh2_strip(image):
        return lambda cols: dot(dgate[image], wg[cols, :], 1, 1) + dot(dup[image], wu[cols, :], 1, 1)

    def mlp_strip(image):
        return lambda cols: dot(hid[image], wdown[:, cols], 1, 0)

    for copy in go_a:
        copy.wait_send()
    strips_of(dh2_strip(1), send_a, go_b)
    strips_of(dh2_strip(0), keep=own)

    def turned(left, order):
        for image in range(2):
            flat = left[image].astype(F32).T
            chunk = width // plan["count"]
            for pair in range(plan["count"] // 2):
                place = [2 * pair, 2 * pair + 1]
                parts = []
                for spot in place:
                    which = 0
                    for level, stride in enumerate(order):
                        which += stride * ((spot >> (len(order) - 1 - level)) & 1)
                    parts.append(flat[which * chunk : (which + 1) * chunk])
                flip[2 * pair * chunk : 2 * (pair + 1) * chunk, image * LEN : (image + 1) * LEN] = (
                    jnp.concatenate(parts, axis=0).astype(BF16)
                )

    if plan["fused"]:
        (
            give_one, keep_out, land0, final, gsend, grecv, osem, credit, packs, came, dflat, dcond, psem,
            *spots,
        ) = extra
        _, ada_out, cond_out, bias_out = results
        dflat[...] = jnp.zeros_like(dflat)
        dcond[...] = jnp.zeros_like(dcond)
        many = len(plan["pieces"])
        land1, land2, land3, held3 = (spots[n * many : (n + 1) * many] for n in range(4))
        half = width // 2
        gives = [wu.at[pl.ds(half, half)], give_one]
        core_bit = bit_of(1)
        state = {"gives": 0, "lands": 0}

        class Piece:
            def __init__(self, name, order, columns, padded, keep, offset, result, at):
                self.name, self.order, self.columns, self.padded = name, order, columns, padded
                self.keep, self.offset, self.result, self.at = keep, offset, result, at
                self.index = plan["pieces"].index(name)
                self.lanes = pl.ds(offset, padded)
                self.copies = {}

            def send(self, level, src, dst):
                copy = pltpu.make_async_remote_copy(
                    src_ref=src, dst_ref=dst, send_sem=gsend.at[self.index, level],
                    recv_sem=grecv.at[self.index, level], device_id=partner(self.order[level]),
                    device_id_type=MESH,
                )
                copy.start()
                self.copies[level] = copy

            def compute(self, right, give):
                self.give = gives[give]
                step = STRIP

                def tile(start, size, pad):
                    total = right(start, size)
                    low, high = total[:half], total[half:]
                    kept = jnp.where(core_bit == 0, low, high).astype(BF16)
                    gone = jnp.where(core_bit == 0, high, low).astype(BF16)
                    place = self.offset + start
                    if pad > size:
                        blank = jnp.zeros((half, pad - size), BF16)
                        kept = jnp.concatenate([kept, blank], axis=1)
                        gone = jnp.concatenate([gone, blank], axis=1)
                    if not isinstance(start, int):
                        place = pl.multiple_of(place, 128)
                        start = pl.multiple_of(start, 128)
                    self.keep[:, pl.ds(place, pad)] = kept
                    self.give[:, pl.ds(start, pad)] = gone

                whole = self.columns // step

                def one(n, carry):
                    tile(n * step, step, step)
                    return carry

                lax.fori_loop(0, whole, one, 0)
                left = self.columns - whole * step
                if left:
                    tile(whole * step, left, self.padded - whole * step)

            def go(self):
                pl.semaphore_wait(credit, 1)
                self.send(0, self.give.at[:, pl.ds(0, self.padded)], land0.at[:, pl.ds(0, self.padded)])

            def add(self, level):
                rows = half >> level
                base = 0
                for before in range(1, level + 1):
                    base = base + bit_of(self.order[before]) * (half >> before)
                self.copies[level].wait_recv()
                cut = pl.ds(0, self.padded)
                if level == 0:
                    source = land0
                elif level == 1:
                    source = land1[self.index]
                elif level == 2:
                    source = land2[self.index]
                if level < 2:
                    block = 48

                    def one(n, carry):
                        there = pl.ds(pl.multiple_of(n * block, 16), block)
                        here = pl.ds(pl.multiple_of(base + n * block, 16), block)
                        self.keep[here, self.lanes] = (
                            self.keep[here, self.lanes].astype(F32) + source[there, cut].astype(F32)
                        ).astype(BF16)
                        return carry

                    lax.fori_loop(0, rows // block, one, 0)
                    if level == 0:
                        pl.semaphore_signal(
                            credit, inc=1, device_id=partner(1), device_id_type=MESH
                        )
                    quarter = rows // 2
                    off = pl.multiple_of(base + (1 - bit_of(self.order[level + 1])) * quarter, 16)
                    target = (land1, land2)[level][self.index]
                    self.send(level + 1, self.keep.at[pl.ds(off, quarter), self.lanes], target)
                elif level == 2:
                    here = pl.ds(pl.multiple_of(base, 16), rows)
                    total = self.keep[here, self.lanes].astype(F32) + source[:, cut].astype(F32)
                    held3[self.index][0] = total[: rows // 2].astype(BF16)
                    held3[self.index][1] = total[rows // 2 :].astype(BF16)
                    bit = bit_of(self.order[3])
                    self.send(3, held3[self.index].at[1 - bit], land3[self.index].at[0])
                else:
                    bit = bit_of(self.order[3])
                    if state.get("final") is not None:
                        state["final"].wait()
                    final[:, cut] = held3[self.index][bit].astype(F32) + land3[self.index][
                        0
                    ].astype(F32)
                    copy = pltpu.make_async_copy(
                        final.at[:, cut], self.result.at[:, pl.ds(self.at, self.padded)], osem
                    )
                    copy.start()
                    state["final"] = copy

            def close(self):
                for copy in self.copies.values():
                    copy.wait_send()

        pl.semaphore_signal(credit, inc=1, device_id=partner(1), device_id_type=MESH)
        y_first, z_first = plan["orders"]
        low, high = wg.at[pl.ds(0, half)], wg.at[pl.ds(half, half)]
        third = [wqkv.at[pl.ds(n * half, half)] for n in range(3)]
        p_down = Piece("down", y_first, inner, inner, low, 0, results[0], 0)
        p_gate = Piece("gate", z_first, inner, inner, high, 0, results[0], inner)
        p_up = Piece("up", y_first, inner, inner, wu.at[pl.ds(0, half)], 0, results[0], 2 * inner)
        pad = -(-head_cols // 128) * 128
        small = [
            Piece(
                name, order, head_cols, pad, place, offset, results[0], 3 * inner + n * pad
            )
            for n, (name, order, place, offset) in enumerate(
                (
                    ("q", y_first, third[0], 0),
                    ("k", z_first, third[1], 0),
                    ("v", y_first, third[2], 0),
                    ("out", y_first, keep_out, 0),
                )
            )
        ]
        p_q, p_k, p_v, p_out = small

        tail = Stream(
            (3, 4, 2, 5, 0, 1), [wdown.at[pl.ds(n * half, half)] for n in range(2)] + [wout]
        )
        devices = plan["devices"]
        side_count = plan["sides"]
        mine = me * side_count + side
        own_cols = plan["own_cols"]

        def condition_back(blocks):
            for block in blocks:
                row = jnp.sum(sums[block], axis=0, keepdims=True)
                dflat[0:1, block * width : (block + 1) * width] = row
                rows = jnp.broadcast_to(row, (16, width)).astype(BF16)
                for _ in range(2):
                    b, h, slot = tail.take()
                    dcond[h : h + 1, :] += dot(rows, slot[...], 1, 1)[0:1]
                    tail.fill(99)

        def share_out():
            lanes = lax.broadcasted_iota(jnp.int32, (16, 128), 0)
            base = jnp.zeros((16, 128), F32)
            silu_f = silu.astype(F32)
            for n in range(width // 128):
                base = jnp.where(lanes == n, silu_f[:, n * 128 : (n + 1) * 128], base)
            row_a = width // 128
            for n in range(devices):
                first = dflat[0:1, n * own_cols : n * own_cols + 128]
                rest = own_cols - 128
                second = dflat[0:1, n * own_cols + 128 : n * own_cols + 256]
                packet = jnp.where(lanes == row_a, first, base)
                packet = jnp.where(lanes == row_a + 1, second, packet)
                packs[n] = packet.astype(BF16)

            def one(n, carry):
                other = lax.rem(mine + n, devices)
                pltpu.make_async_remote_copy(
                    src_ref=packs.at[other], dst_ref=came.at[mine], send_sem=psem.at[0],
                    recv_sem=psem.at[1],
                    device_id={
                        "dp": lax.div(other, side_count), "tensor": lax.rem(other, side_count)
                    },
                    device_id_type=MESH,
                ).start()
                return carry

            lax.fori_loop(1, devices, one, 0)
            came[mine] = packs[mine]

        def take_in():
            every = pl.ds(0, devices - 1)
            whole = pltpu.make_async_remote_copy(
                src_ref=packs.at[every], dst_ref=came.at[every], send_sem=psem.at[0],
                recv_sem=psem.at[1], device_id=mate, device_id_type=MESH,
            )
            whole.wait_send()
            whole.wait_recv()
            seen = came[...].astype(F32)
            row_a = width // 128
            silu_all = jnp.concatenate([seen[:, n, :] for n in range(row_a)], axis=1).astype(BF16)
            columns = jnp.concatenate([seen[:, row_a, :], seen[:, row_a + 1, :]], axis=1)
            bias_out[...] = jnp.broadcast_to(jnp.sum(columns, axis=0, keepdims=True), bias_out.shape)
            own[...] = dot(columns.astype(BF16), silu_all, 0, 0)
            copy = pltpu.make_async_copy(own.at[pl.ds(0, own_cols)], ada_out, asem.at[0])
            copy.start()
            copy.wait()
            slope = cond_sig * (1.0 + cond_f * (1.0 - cond_sig))
            whole_row = jnp.concatenate([dcond[0:1, :], dcond[1:2, :]], axis=1)
            cond_out[...] = whole_row * slope

    def lane_right(array):
        def right(start, size):
            if not isinstance(start, int):
                start = pl.multiple_of(start, 128)
            part = [array[i, :, pl.ds(start, size)] for i in range(2)]
            return dot(flip[:, 0:LEN], part[0], 1, 0) + dot(flip[:, LEN:], part[1], 1, 0)
        return right

    def row_right(array, base):
        def right(start, size):
            at = base + start
            if not isinstance(start, int):
                at = pl.multiple_of(at, 16)
            part = [array[i, pl.ds(at, size), :] for i in range(2)]
            return dot(flip[:, 0:LEN], part[0], 1, 1) + dot(flip[:, LEN:], part[1], 1, 1)
        return right

    def plain_grad(right, columns, target):
        (stage, gsem) = extra
        pend = {}
        for n, start in enumerate(range(0, columns, TILE)):
            size = min(TILE, columns - start)
            slot = n % 2
            if slot in pend:
                pend[slot].wait()
            stage[slot, :, 0:size] = right(start, size).astype(BF16)
            copy = pltpu.make_async_copy(
                stage.at[slot], target.at[:, pl.ds(start, TILE)], gsem.at[slot]
            )
            copy.start()
            pend[slot] = copy
        for copy in pend.values():
            copy.wait()

    def plain_grad_in(left, right, columns, target):
        for image in range(2):
            flip[:, image * LEN : (image + 1) * LEN] = left[image].astype(F32).T.astype(BF16)
        plain_grad(right, columns, target)

    if plan["fused"]:
        turned(dml, p_down.order)
        p_down.compute(lane_right(hid), 0)
        p_down.go()
        turned(h2, p_gate.order)
        p_gate.compute(lane_right(dgate), 1)
        p_down.add(0)
        p_gate.go()
    else:
        plain_grad_in(dml, lane_right(hid), inner, results[0])
        plain_grad_in(h2, lane_right(dgate), inner, results[1])
        plain_grad_in(h2, lane_right(dup), inner, results[2])

    for copy in go_b:
        copy.wait_recv()

    def second_back(rows):
        grad = own[rows, :] + recv_a[rows, :].astype(F32)
        norm, inverse = normed(tok[rows, :].astype(F32) + gate_one * attn[rows, :])
        middle = cot[rows, :].astype(F32) + norm_back(grad * (1.0 + scale_two), norm, inverse)
        dx1[rows, :] = middle
        dat[0, rows, :] = (gate_one * middle).astype(BF16)
        sums[2] += fold(middle * attn[rows, :])
        sums[3] += fold(grad)
        sums[4] += fold(grad * norm)

    rows_loop(second_back, go_dat)

    strips_of(mlp_strip(1), send_c, go_c)
    if plan["fused"]:
        p_gate.add(0)
        p_down.copies[0].wait_send()
        turned(h2, p_up.order)
        p_up.compute(lane_right(dup), 0)
        p_up.go()

    def heads_back(image):
        a_f[...] = dot(wout[...], dat[image], 1, 1)
        cosine, sine = cos_t[image], sin_t[image]

        def head(h, carry):
            at = image * heads + h
            rows = pl.ds(pl.multiple_of(h * HD, 8), HD)
            da = a_f[rows, :].astype(BF16)
            probs = p_s[at]
            query, key, value = q_s[at], k_s[at], v_s[at]
            dprobs = dot(value, da, 0, 0)
            dvalue = dot(da, probs.astype(BF16), 1, 1)
            inside = jnp.sum(probs * dprobs, axis=0, keepdims=True)
            dscores = (probs * (dprobs - inside)).astype(BF16)
            dquery = dot(key, dscores, 1, 0)
            dkey = dot(query, dscores, 1, 1)
            dquery = (dquery * cosine - rotate_rows(dquery * sine)) * scale
            dkey = dkey * cosine - rotate_rows(dkey * sine)
            qkv_f[rows, :] = dquery
            qkv_f[pl.ds(pl.multiple_of(head_cols + h * HD, 8), HD), :] = dkey
            qkv_f[pl.ds(pl.multiple_of(2 * head_cols + h * HD, 8), HD), :] = dvalue
            return carry

        lax.fori_loop(0, heads, head, 0, unroll=2)
        dqkv[image] = qkv_f[...].astype(BF16)

    heads_back(0)
    if plan["fused"]:
        p_up.add(0)
    for copy in go_dat:
        copy.wait_recv()
    heads_back(1)

    def dh1_strip(image):
        return lambda cols: dot(dqkv[image], wqkv[:, cols], 0, 0)

    for copy in go_b:
        copy.wait_send()
    strips_of(dh1_strip(1), send_a, go_d)
    strips_of(dh1_strip(0), keep=own)

    if plan["fused"]:
        p_gate.copies[0].wait_send()
        p_up.copies[0].wait_send()
        p_down.add(1)
        p_gate.add(1)
        turned(h1, p_q.order)
        p_q.compute(row_right(dqkv, 0), 0)
        p_q.go()
        p_v.compute(row_right(dqkv, 2 * head_cols), 1)
        p_q.add(0)
        p_v.go()
        p_q.copies[0].wait_send()
        turned(h1, p_k.order)
        p_k.compute(row_right(dqkv, head_cols), 0)
        p_v.add(0)
        p_k.go()
        p_v.copies[0].wait_send()
        turned(dat, p_out.order)
        p_out.compute(row_right(a_t, 0), 1)
        p_k.add(0)
        p_out.go()
        p_down.add(2)
        p_out.add(0)
    else:
        plain_grad_in(h1, row_right(dqkv, 0), 3 * head_cols, results[3])
        plain_grad_in(dat, row_right(a_t, 0), head_cols, results[4])

    for copy in go_d:
        copy.wait_recv()

    def first_back(rows):
        grad = own[rows, :] + recv_a[rows, :].astype(F32)
        norm, inverse = normed(tok[rows, :].astype(F32))
        dtok[rows, :] = dx1[rows, :] + norm_back(grad * (1.0 + scale_one), norm, inverse)
        sums[0] += fold(grad)
        sums[1] += fold(grad * norm)

    rows_loop(first_back)

    strips_of(mlp_strip(0), keep=own)
    for copy in go_c:
        copy.wait_recv()

    def finish(rows):
        branch = own[rows, :] + recv_c[rows, :].astype(F32)
        out[rows, :] = (
            tok[rows, :].astype(F32) + gate_one * attn[rows, :] + gate_two * branch
        ).astype(BF16)
        sums[5] += fold(cot[rows, :].astype(F32) * branch)

    rows_loop(finish)
    if plan["fused"]:
        tail.fill(99)
        p_up.add(1)
        condition_back((3, 4))
        p_down.add(3)
        condition_back((2, 5))
        p_gate.add(2)
        condition_back((0, 1))
        share_out()
        p_up.add(2)
        p_k.add(1)
        p_q.add(1)
        p_gate.add(3)
        p_up.add(3)
        p_v.add(1)
        p_q.add(2)
        p_k.add(2)
        p_out.add(1)
        p_v.add(2)
        take_in()
        p_q.add(3)
        p_k.add(3)
        p_out.add(2)
        p_v.add(3)
        p_out.add(3)
        state["final"].wait()
        pl.semaphore_wait(credit, 1)
        for piece in (p_gate, p_up, p_down, *small):
            for level, copy in piece.copies.items():
                if level > 0 or piece in (p_k, p_out):
                    copy.wait_send()
    else:
        for n in range(6):
            results[5][n : n + 1, :] = jnp.sum(sums[n], axis=0, keepdims=True)
    for copy in (*go_h1, *go_cot, go_row, *go_h2, *go_dat, *go_c, *go_d):
        copy.wait_send()


def lay_out_kernel(cuts, whole, ada, tok, out, bias, *refs):
    (down, gate_up, qkv, wout, ada_to, tok_to, out_to, bias_to) = refs
    inner, head_cols, pad, own_cols = cuts
    ada_to[...] = ada[...]
    tok_to[...] = tok[...]
    out_to[...] = out[...]
    down[...] = whole[:, 0:inner]
    gate_up[:, 0, :] = whole[:, inner : 2 * inner]
    gate_up[:, 1, :] = whole[:, 2 * inner : 3 * inner]
    start = 3 * inner
    for n in range(3):
        qkv[n] = whole[:, start + n * pad : start + n * pad + head_cols]
    start += 3 * pad
    wout[...] = whole[:, start : start + head_cols]
    bias_to[...] = bias[0:1, 0:own_cols]


def lay_out(whole, ada, tok, out, bias, inner, head_cols, own_cols):
    rows = whole.shape[0]
    vmem = pl.BlockSpec(memory_space=pltpu.VMEM)
    pad = -(-head_cols // 128) * 128
    S = jax.ShapeDtypeStruct
    return pl.pallas_call(
        functools.partial(lay_out_kernel, (inner, head_cols, pad, own_cols)),
        out_shape=(
            S((rows, inner), F32), S((rows, 2, inner), F32), S((3, rows, head_cols), F32),
            S((rows, head_cols), F32), S(ada.shape, F32), S(tok.shape, F32), S(out.shape, BF16),
            S((1, own_cols), F32),
        ),
        in_specs=[vmem] * 5,
        out_specs=[vmem] * 8,
        compiler_params=pltpu.CompilerParams(vmem_limit_bytes=62 * 1024 * 1024),
    )(whole, ada, tok, out, bias)


def run_block(tok, cot, cond, grid, bias, wada, wqkv, wout, wgu, wdown):
    width = tok.shape[1]
    head_cols = wout.shape[0]
    heads = head_cols // HD
    inner = wdown.shape[0]
    strips = width // STRIP
    count = lax.axis_size("dp")
    sides = lax.axis_size("tensor")
    devices = count * sides
    own_cols = 6 * width // devices
    vmem = pl.BlockSpec(memory_space=pltpu.VMEM)
    hbm = pl.BlockSpec(memory_space=pl.ANY)
    V = pltpu.VMEM
    D = pltpu.SemaphoreType.DMA
    copies = 9 + 4 * strips
    fused = count == 16 and width % (8 * count) == 0 and 128 < own_cols <= 256 and own_cols % 8 == 0
    names = ["down", "gate", "up", "q", "k", "v", "out"]
    pad = -(-head_cols // 128) * 128
    if fused:
        results = [
            jax.ShapeDtypeStruct((width // count, 3 * inner + 4 * pad), F32),
            jax.ShapeDtypeStruct((own_cols, width), F32),
            jax.ShapeDtypeStruct((1, width), F32),
            jax.ShapeDtypeStruct((8, 256), F32),
        ]
        result_specs = [hbm, hbm, vmem, vmem]
        chunk = width // count
        widths = [inner, inner, inner, pad, pad, pad, pad]
        extra = [
            V((width // 2, inner), BF16),
            V((width // 2, pad), BF16),
            V((width // 2, inner), BF16),
            V((chunk, inner), F32),
            D((len(names), 4)),
            D((len(names), 4)),
            D(()),
            pltpu.SemaphoreType.REGULAR,
            V((devices, 16, 128), BF16),
            V((devices, 16, 128), BF16),
            V((8, 6 * width + 128), F32),
            V((8, width // 2), F32),
            D((2,)),
            *[V((width // 4, w), BF16) for w in widths],
            *[V((width // 8, w), BF16) for w in widths],
            *[V((1, chunk, w), BF16) for w in widths],
            *[V((2, chunk, w), BF16) for w in widths],
        ]
        strides = [1, 2, 4, 8]
    else:
        wide = [inner, inner, inner, 3 * head_cols, head_cols]
        results = [jax.ShapeDtypeStruct((width, -(-w // TILE) * TILE), BF16) for w in wide]
        results += [jax.ShapeDtypeStruct((6, width), F32)]
        result_specs = [hbm] * 5 + [vmem]
        extra = [V((2, width, TILE), BF16), D((2,))]
        strides = []
    plan = {
        "fused": fused, "results": len(results), "count": count, "pieces": names,
        "devices": devices, "sides": sides, "own_cols": own_cols,
        "early": 8, "strides": strides, "orders": ((1, 2, 4, 8), (1, 4, 2, 8)),
    }
    return pl.pallas_call(
        functools.partial(block_kernel, plan),
        out_shape=(
            jax.ShapeDtypeStruct((LEN, width), BF16),
            jax.ShapeDtypeStruct((LEN, width), F32),
            *results,
        ),
        in_specs=[vmem] * 3 + [pl.BlockSpec(memory_space=pltpu.SMEM), vmem] + [hbm] * 5,
        out_specs=[vmem] * 2 + result_specs,
        scratch_shapes=[
            V((8, width), F32), V((2, 16, width // 2), BF16), V((2, HD, LEN), F32),
            V((2, HD, LEN), F32), V((3, 48, 2, inner), BF16),
                        V(wqkv.shape, BF16), V(wout.shape, BF16), V((width, inner), BF16),
            V((width, inner), BF16), V(wdown.shape, BF16),
            *[V((2, LEN, width), BF16)] * 4,
            *[V((2 * heads, HD, LEN), BF16)] * 3,
            V((2 * heads, LEN, LEN), F32),
            V((3 * head_cols, LEN), F32),
            V((head_cols, LEN), F32),
            V((2, head_cols, LEN), BF16),
            *[V((2, LEN, inner), BF16)] * 3,
            V((2, 3 * head_cols, LEN), BF16),
            *[V((LEN, width), F32)] * 3,
            *[V((LEN, width), BF16)] * 4,
            *[V((8, width), F32)] * 2,
            V((width, 2 * LEN), BF16),
            V((6, 8, width), F32),
            D((6,)),
            D((8,)),
            D((copies,)),
            D((copies,)),
            *extra,
        ],
        compiler_params=pltpu.CompilerParams(
            collective_id=0, has_side_effects=True, vmem_limit_bytes=62 * 1024 * 1024
        ),
    )(tok, cot, cond, grid, bias, wada, wqkv, wout, wgu, wdown)


def sum_over_images(partial):
    count = lax.axis_size("dp")
    me = lax.axis_index("dp")
    held = partial.reshape(count, partial.shape[0] // count, partial.shape[1])
    stride = 1
    left = count
    while left > 1:
        bit = (me // stride) % 2
        pairs = held.reshape(left // 2, 2, *held.shape[1:])
        keep = lax.dynamic_index_in_dim(pairs, bit, 1, keepdims=False)
        send = lax.dynamic_index_in_dim(pairs, 1 - bit, 1, keepdims=False)
        came = lax.ppermute(send, "dp", [(i, i ^ stride) for i in range(count)])
        held = keep.astype(F32) + came.astype(F32)
        left //= 2
        stride *= 2
        if left > 1:
            held = held.astype(BF16)
    return held[0]


def body(tokens, condition, grid_shape, w_ada, b_ada, w_qkv, w_out, w_gate_up, w_down, cotangent):
    width = tokens.shape[1]
    inner = w_down.shape[0]
    head_cols = w_out.shape[0]
    wqkv = w_qkv.transpose(1, 2, 0).reshape(3 * head_cols, width)
    layer_out, d_tokens, *grads = run_block(
        tokens, cotangent, condition, grid_shape, b_ada.reshape(-1, 128), w_ada, wqkv, w_out,
        w_gate_up, w_down,
    )
    devices_all = lax.axis_size("dp") * lax.axis_size("tensor")
    own_cols = 6 * width // devices_all
    if len(grads) == 4:
        whole, ada, d_condition, bias_rows = grads
        down, gate_up, qkv, g_out, ada, d_tokens, layer_out, bias_part = lay_out(
            whole, ada, d_tokens, layer_out, bias_rows, inner, head_cols, own_cols
        )
        grad_down, grad_gate_up = down.T, gate_up
        grad_qkv, grad_out = qkv.transpose(1, 0, 2), g_out.T
        weight_part, bias_part = ada.T, bias_part.reshape(own_cols)
    else:
        grad_down = sum_over_images(grads[0]).T
        grad_gate_up = jnp.stack([sum_over_images(grads[1]), sum_over_images(grads[2])], axis=1)
        grad_qkv = sum_over_images(grads[3][:, : 3 * head_cols]).reshape(-1, 3, head_cols)
        grad_out = sum_over_images(grads[4][:, :head_cols]).T
        cond = condition.astype(F32)
        cond_sigmoid = jax.nn.sigmoid(cond)
        silu_cond = (cond * cond_sigmoid).astype(BF16)
        d_mod = grads[5].reshape(1, 6 * width).astype(BF16)
        d_condition = (
            dot(d_mod, w_ada, 1, 1) * cond_sigmoid * (1.0 + cond * (1.0 - cond_sigmoid))
        )
        packed = jnp.concatenate(
            [
                d_mod.reshape(devices_all, own_cols),
                jnp.broadcast_to(silu_cond, (devices_all, width)),
            ],
            axis=1,
        )
        packed = jnp.pad(packed, ((0, 0), (0, -packed.shape[1] % 128)))
        packed = lax.all_to_all(
            packed.reshape(devices_all, -1, 128), ("dp", "tensor"), 0, 0, tiled=True
        ).reshape(devices_all, -1)
        columns = packed[:, :own_cols]
        silu_rows = packed[:, own_cols : own_cols + width]
        weight_part = dot(silu_rows, columns, 0, 0)
        bias_part = jnp.sum(columns.astype(F32), axis=0)
    return (
        layer_out, d_tokens, d_condition, weight_part, bias_part,
        grad_qkv, grad_out, grad_gate_up, grad_down,
    )


def solution(mesh):
    placed = (
        P(("dp", "tensor"), None),
        P(("dp", "tensor"), None),
        P("dp", None),
        P(),
        P(),
        P(None, None, "tensor"),
        P("tensor", None),
        P(None, None, "tensor"),
        P("tensor", None),
        P(("dp", "tensor"), None),
    )
    return jax.shard_map(
        body,
        mesh=mesh,
        in_specs=placed,
        out_specs=(
            P(("dp", "tensor"), None),
            P(("dp", "tensor"), None),
            P(("dp", "tensor"), None),
            P(None, ("dp", "tensor")),
            P(("dp", "tensor")),
            P("dp", None, "tensor"),
            P("tensor", "dp"),
            P("dp", None, "tensor"),
            P("tensor", "dp"),
        ),
        check_vma=False,
    )
```

```python
import functools

import jax
import jax.numpy as jnp
from jax import lax
from jax.experimental import pallas as pl
from jax.experimental.pallas import tpu as pltpu
from jax.sharding import PartitionSpec as P

HD = 72
LEN = 256
EPSILON = 1e-06
MESH = pl.DeviceIdType.MESH
F32 = jnp.float32
BF16 = jnp.bfloat16
ROWS = 32
STRIP = 384
TILE = 256


def dot(left, right, left_dim, right_dim):
    return lax.dot_general(
        left, right, (((left_dim,), (right_dim,)), ((), ())), preferred_element_type=F32
    )


def normed(values):
    centered = values - jnp.mean(values, axis=-1, keepdims=True)
    variance = jnp.mean(centered * centered, axis=-1, keepdims=True)
    inverse = lax.rsqrt(variance + EPSILON)
    return centered * inverse, inverse


def norm_back(upstream, norm, inverse):
    mean_grad = jnp.mean(upstream, axis=-1, keepdims=True)
    mean_cross = jnp.mean(upstream * norm, axis=-1, keepdims=True)
    return inverse * (upstream - mean_grad - norm * mean_cross)


def rotate_rows(values):
    quarter = HD // 4
    a, b = values[:quarter], values[quarter : 2 * quarter]
    c, d = values[2 * quarter : 3 * quarter], values[3 * quarter :]
    return jnp.concatenate([-b, a, -d, c], axis=0)


def fold(values):
    return jnp.sum(values.reshape(values.shape[0] // 8, 8, values.shape[1]), axis=0)


class Several:
    def __init__(self, copies):
        self.copies = copies

    def wait_send(self):
        for copy in self.copies:
            copy.wait_send()

    def wait_recv(self):
        for copy in self.copies:
            copy.wait_recv()


def block_kernel(
    plan, tok, cot, cond, grid, bias,
    wada_hbm, wqkv_hbm, wout_hbm, wgu_hbm, wdown_hbm,
    out, dtok, *rest,
):
    results, rest = rest[: plan["results"]], rest[plan["results"] :]
    (
        mod, silu_two, cos_t, sin_t, raw,
        wqkv, wout, wg, wu, wdown,
        h1, h2, dml, dat,
        q_s, k_s, v_s, p_s, qkv_f, a_f, a_t,
        hid, dgate, dup, dqkv,
        attn, dx1, own,
        send_a, send_c, recv_a, recv_c, row_out, row_in,
        flip, sums,
        wsem, asem, ssem, rsem, *extra,
    ) = rest
    width = tok.shape[1]
    heads = q_s.shape[0] // 2
    head_cols = heads * HD
    inner = wdown.shape[0]
    side = lax.axis_index("tensor")
    mate = {"tensor": 1 - side}
    scale = HD ** (-0.5)

    loads = [
        pltpu.make_async_copy(src, dst, wsem.at[i])
        for i, (src, dst) in enumerate(
            ((wqkv_hbm, wqkv), (wout_hbm, wout), (wdown_hbm, wdown))
        )
    ]
    half_rows = width // 2
    slots = [
        ref.at[pl.ds(n * half_rows, half_rows), pl.ds(0, width)] for ref in (wg, wu) for n in range(2)
    ]

    class Stream:
        def __init__(self, blocks, slots):
            self.chunks = [(b, h) for b in blocks for h in range(2)]
            self.slots = slots
            self.copies = []
            self.at = 0

        def fill(self, most):
            while len(self.copies) < min(most, len(self.chunks), self.at + len(self.slots)):
                n = len(self.copies)
                b, h = self.chunks[n]
                copy = pltpu.make_async_copy(
                    wada_hbm.at[pl.ds(h * half_rows, half_rows), pl.ds(b * width, width)],
                    self.slots[n % len(self.slots)], asem.at[n % len(self.slots)],
                )
                copy.start()
                self.copies.append(copy)

        def take(self):
            n = self.at
            self.copies[n].wait()
            b, h = self.chunks[n]
            self.at += 1
            return b, h, self.slots[n % len(self.slots)]

    stream = Stream((0, 1, 5, 2, 3, 4), slots)
    stream.fill(4)

    me = lax.axis_index("dp")

    def bit_of(stride):
        return lax.rem(lax.div(me, stride), 2)

    def partner(stride):
        return {"dp": me + stride - 2 * stride * bit_of(stride)}

    barrier = pltpu.get_barrier_semaphore()
    friends = [mate] + [partner(s) for s in plan["strides"]]
    for friend in friends:
        pl.semaphore_signal(barrier, inc=1, device_id=friend, device_id_type=MESH)

    def give(src, dst, slot):
        return pltpu.make_async_remote_copy(
            src_ref=src, dst_ref=dst, send_sem=ssem.at[slot], recv_sem=rsem.at[slot],
            device_id=mate, device_id_type=MESH,
        )

    def gather(buf, slot):
        half = LEN // 2
        return [
            give(buf.at[0, pl.ds(c * half, half)], buf.at[1, pl.ds(c * half, half)], slot + c)
            for c in range(2)
        ]

    strips = width // STRIP

    def scatter(send, recv, slot):
        return [
            give(
                send.at[:, pl.ds(c * STRIP, STRIP)], recv.at[:, pl.ds(c * STRIP, STRIP)], slot + c
            )
            for c in range(strips)
        ]

    go_h1, go_h2, go_dat = (gather(b, 2 * i) for i, b in enumerate((h1, h2, dat)))
    go_cot = [
        give(cot.at[pl.ds(at, size)], dml.at[1, pl.ds(at, size)], slot)
        for at, size, slot in ((0, 96, 6), (96, 96, 7), (192, 64, 9 + 4 * (width // STRIP)))
    ]
    go_row = give(row_out, row_in, 8 + 4 * (width // STRIP))
    go_a, go_b, go_c, go_d = (
        scatter(s, r, 8 + strips * i)
        for i, (s, r) in enumerate(
            ((send_a, recv_a), (send_a, recv_a), (send_c, recv_c), (send_a, recv_a))
        )
    )

    def rows_loop(step, copies=None):
        half = LEN // 2
        count = half // ROWS
        for c in range(2):
            def one(i, carry, c=c):
                step(pl.ds(pl.multiple_of(c * half + i * ROWS, ROWS), ROWS))
                return carry
            lax.fori_loop(0, count, one, 0)
            if copies is not None:
                copies[c].start()

    cond_f = cond[...].astype(F32)
    cond_sig = jax.nn.sigmoid(cond_f)
    silu = (cond_f * cond_sig).astype(BF16)
    silu_rows = jnp.broadcast_to(silu.astype(F32), (16, width))
    for h in range(2):
        silu_two[h] = silu_rows[:, h * half_rows : (h + 1) * half_rows].astype(BF16)

    bias_f = bias[...].astype(F32)
    tiles = width // bias.shape[1]

    def bias_row(b):
        return jnp.concatenate([bias_f[b * tiles + n : b * tiles + n + 1] for n in range(tiles)], axis=1)

    def modulate(count):
        for _ in range(count):
            row = None
            for _ in range(2):
                b, h, slot = stream.take()
                part = dot(silu_two[h], slot[...], 1, 0)[0:1]
                row = part if row is None else row + part
                stream.fill(99)
            mod[b : b + 1, :] = row + bias_row(b)

    def pre_norm(rows):
        norm, _ = normed(tok[rows, :].astype(F32))
        dx1[rows, :] = norm

    rows_loop(pre_norm)
    pl.semaphore_wait(barrier, len(friends))
    go_cot[0].start()
    modulate(2)
    for load in loads:
        load.start()
    shift_one, scale_one = mod[0:1], mod[1:2]

    def first_norm(rows):
        h1[0, rows, :] = (dx1[rows, :] * (1.0 + scale_one) + shift_one).astype(BF16)

    rows_loop(first_norm, go_h1)
    modulate(1)
    gate_two = mod[5:6]
    row_out[...] = jnp.broadcast_to(gate_two, row_out.shape)
    go_row.start()
    go_cot[1].start()
    sums[...] = jnp.zeros_like(sums)

    quarter = HD // 4
    limits = []
    for image in range(2):
        at = side if image == 0 else 1 - side
        tall, wide = grid[at, 0], grid[at, 1]
        limits.append(tall * wide)
        spot = lax.broadcasted_iota(jnp.int32, (1, LEN), 1).astype(F32)
        wide_f = jnp.full((1, LEN), wide, jnp.int32).astype(F32)
        row_at = jnp.floor((spot + 0.5) / wide_f)
        col_at = spot - row_at * wide_f
        step = lax.broadcasted_iota(jnp.int32, (quarter, LEN), 0).astype(F32)
        frequency = jnp.exp(step * (-9.210340371976184 / quarter))
        both = jnp.concatenate([row_at * frequency, col_at * frequency], axis=0)
        for table, turn in ((cos_t, jnp.cos), (sin_t, jnp.sin)):
            seen = turn(both)
            first, second = seen[:quarter], seen[quarter:]
            table[image] = jnp.concatenate([first, first, second, second], axis=0)

    depth = raw.shape[1]
    ring = raw.shape[0]
    parts = {"next": 0, "copies": []}
    r = lax.broadcasted_iota(jnp.int32, (2 * depth, 2 * depth), 0)
    c = lax.broadcasted_iota(jnp.int32, (2 * depth, 2 * depth), 1)
    sorter = jnp.where(c == jnp.where(r < depth, 2 * r, 2 * (r - depth) + 1), 1.0, 0.0).astype(BF16)

    def fetch(n):
        if n < width // depth:
            copy = pltpu.make_async_copy(
                wgu_hbm.at[pl.ds(n * depth, depth)], raw.at[n % ring], wsem.at[3 + n % ring]
            )
            copy.start()
            parts["copies"].append(copy)

    def pull_apart(until):
        while parts["next"] < until:
            n = parts["next"]
            parts["copies"][n].wait()
            parted = dot(sorter, raw[n % ring].reshape(2 * depth, inner), 1, 0).astype(BF16)
            wg[n * depth : (n + 1) * depth, :] = parted[:depth]
            wu[n * depth : (n + 1) * depth, :] = parted[depth:]
            fetch(n + ring)
            parts["next"] += 1

    def heads_forward(image):
        for part in range(3):
            qkv_f[part * head_cols : (part + 1) * head_cols, :] = dot(
                wqkv[part * head_cols : (part + 1) * head_cols, :], h1[image], 1, 1
            )
        cosine, sine = cos_t[image], sin_t[image]
        ok = lax.broadcasted_iota(jnp.int32, (LEN, LEN), 0) < limits[image]

        def head(h, carry):
            at = image * heads + h
            rows = pl.ds(pl.multiple_of(h * HD, 8), HD)
            query = qkv_f[rows, :]
            key = qkv_f[pl.ds(pl.multiple_of(head_cols + h * HD, 8), HD), :]
            value = qkv_f[pl.ds(pl.multiple_of(2 * head_cols + h * HD, 8), HD), :].astype(BF16)
            query = ((query * cosine + rotate_rows(query) * sine) * scale).astype(BF16)
            key = (key * cosine + rotate_rows(key) * sine).astype(BF16)
            q_s[at], k_s[at], v_s[at] = query, key, value
            scores = dot(key, query, 0, 0)
            scores = jnp.where(ok, scores, -1e30)
            top = jnp.max(scores, axis=0, keepdims=True)
            exps = jnp.exp(scores - top)
            probs = exps * (1.0 / jnp.sum(exps, axis=0, keepdims=True))
            p_s[at] = probs
            a_f[rows, :] = dot(value, probs.astype(BF16), 1, 0)
            return carry

        lax.fori_loop(0, heads, head, 0, unroll=2)
        a_t[image] = a_f[...].astype(BF16)

    def strips_of(make, send=None, copies=None, keep=None):
        for c in range(strips):
            cols = slice(c * STRIP, (c + 1) * STRIP)
            value = make(cols)
            if send is not None:
                send[:, cols] = value.astype(BF16)
                copies[c].start()
            else:
                keep[:, cols] = value

    for n in range(ring):
        fetch(n)
    loads[0].wait()
    heads_forward(0)
    modulate(3)
    pull_apart(plan["early"])
    gate_one, shift_two, scale_two = mod[2:3], mod[3:4], mod[4:5]
    for copy in go_h1:
        copy.wait_recv()
    heads_forward(1)
    loads[1].wait()
    strips_of(lambda cols: dot(a_t[1], wout[:, cols], 0, 0), send_a, go_a)
    go_cot[2].start()
    strips_of(lambda cols: dot(a_t[0], wout[:, cols], 0, 0), keep=own)

    gate_two_row = gate_two

    def mlp_grad(rows):
        dml[0, rows, :] = (gate_two_row * cot[rows, :].astype(F32)).astype(BF16)

    rows_loop(mlp_grad)
    pull_apart(width // depth)
    for copy in go_a:
        copy.wait_recv()

    def second_norm(rows):
        branch = own[rows, :] + recv_a[rows, :].astype(F32)
        attn[rows, :] = branch
        middle = tok[rows, :].astype(F32) + gate_one * branch
        norm, _ = normed(middle)
        h2[0, rows, :] = (norm * (1.0 + scale_two) + shift_two).astype(BF16)

    rows_loop(second_norm, go_h2)

    def turned(left, order):
        for image in range(2):
            flat = left[image].astype(F32).T
            chunk = width // plan["count"]
            for pair in range(plan["count"] // 2):
                place = [2 * pair, 2 * pair + 1]
                parts = []
                for spot in place:
                    which = 0
                    for level, stride in enumerate(order):
                        which += stride * ((spot >> (len(order) - 1 - level)) & 1)
                    parts.append(flat[which * chunk : (which + 1) * chunk])
                flip[2 * pair * chunk : 2 * (pair + 1) * chunk, image * LEN : (image + 1) * LEN] = (
                    jnp.concatenate(parts, axis=0).astype(BF16)
                )

    loads[2].wait()

    def feed_forward(image):
        def tile(j, carry):
            cols = pl.ds(pl.multiple_of(j * TILE, TILE), TILE)
            gate = dot(h2[image], wg[:, cols], 1, 0)
            up = dot(h2[image], wu[:, cols], 1, 0)
            grad = dot(dml[image], wdown[cols, :], 1, 1)
            sig = jax.nn.sigmoid(gate)
            act = gate * sig
            hid[image, :, cols] = (act * up).astype(BF16)
            dgate[image, :, cols] = (grad * up * sig * (1.0 + gate * (1.0 - sig))).astype(BF16)
            dup[image, :, cols] = (grad * act).astype(BF16)
            return carry

        lax.fori_loop(0, inner // TILE, tile, 0)

    def dh2_strip(image):
        return lambda cols: dot(dgate[image], wg[cols, :], 1, 1) + dot(dup[image], wu[cols, :], 1, 1)

    feed_forward(0)
    strips_of(dh2_strip(0), keep=own)
    for copy in go_cot:
        copy.wait_recv()
    go_row.wait_recv()
    gate_mate = row_in[0:1]

    def mate_grad(rows):
        dml[1, rows, :] = (gate_mate * dml[1, rows, :].astype(F32)).astype(BF16)

    rows_loop(mate_grad)
    if plan["fused"]:
        turned(dml, plan["orders"][0])
    for copy in go_h2:
        copy.wait_recv()
    feed_forward(1)

    def mlp_strip(image):
        return lambda cols: dot(hid[image], wdown[:, cols], 1, 0)

    for copy in go_a:
        copy.wait_send()
    strips_of(dh2_strip(1), send_a, go_b)

    if plan["fused"]:
        (
            give_one, keep_out, land0, final, gsend, grecv, osem, credit, packs, came, dflat, dcond, psem,
            *spots,
        ) = extra
        _, ada_out, cond_out, bias_out = results
        dflat[...] = jnp.zeros_like(dflat)
        dcond[...] = jnp.zeros_like(dcond)
        many = len(plan["pieces"])
        land1, land2, land3, held3 = (spots[n * many : (n + 1) * many] for n in range(4))
        half = width // 2
        gives = [wu.at[pl.ds(half, half)], give_one]
        core_bit = bit_of(1)
        state = {"gives": 0, "lands": 0}

        class Piece:
            def __init__(self, name, order, columns, padded, keep, offset, result, at):
                self.name, self.order, self.columns, self.padded = name, order, columns, padded
                self.keep, self.offset, self.result, self.at = keep, offset, result, at
                self.index = plan["pieces"].index(name)
                self.lanes = pl.ds(offset, padded)
                self.copies = {}

            def send(self, level, src, dst):
                copy = pltpu.make_async_remote_copy(
                    src_ref=src, dst_ref=dst, send_sem=gsend.at[self.index, level],
                    recv_sem=grecv.at[self.index, level], device_id=partner(self.order[level]),
                    device_id_type=MESH,
                )
                copy.start()
                self.copies[level] = copy

            def compute(self, right, give, cuts=0):
                self.give = gives[give]
                step = STRIP

                def tile(start, size, pad):
                    total = right(start, size)
                    low, high = total[:half], total[half:]
                    kept = jnp.where(core_bit == 0, low, high).astype(BF16)
                    gone = jnp.where(core_bit == 0, high, low).astype(BF16)
                    place = self.offset + start
                    if pad > size:
                        blank = jnp.zeros((half, pad - size), BF16)
                        kept = jnp.concatenate([kept, blank], axis=1)
                        gone = jnp.concatenate([gone, blank], axis=1)
                    if not isinstance(start, int):
                        place = pl.multiple_of(place, 128)
                        start = pl.multiple_of(start, 128)
                    self.keep[:, pl.ds(place, pad)] = kept
                    self.give[:, pl.ds(start, pad)] = gone

                whole = self.columns // step

                def one(n, carry):
                    tile(n * step, step, step)
                    return carry

                if cuts:
                    copies = []
                    for n in range(cuts):
                        part = whole // cuts
                        lax.fori_loop(n * part, (n + 1) * part, one, 0)
                        if n == 0:
                            pl.semaphore_wait(credit, 1)
                        lanes = pl.ds(n * part * step, part * step)
                        copy = pltpu.make_async_remote_copy(
                            src_ref=self.give.at[:, lanes], dst_ref=land0.at[:, lanes],
                            send_sem=gsend.at[self.index, 4 * n], recv_sem=grecv.at[self.index, 4 * n],
                            device_id=partner(1), device_id_type=MESH,
                        )
                        copy.start()
                        copies.append(copy)
                    self.copies[0] = Several(copies)
                    return
                lax.fori_loop(0, whole, one, 0)
                left = self.columns - whole * step
                if left:
                    tile(whole * step, left, self.padded - whole * step)

            def go(self):
                pl.semaphore_wait(credit, 1)
                self.send(0, self.give.at[:, pl.ds(0, self.padded)], land0.at[:, pl.ds(0, self.padded)])

            def add(self, level):
                rows = half >> level
                base = 0
                for before in range(1, level + 1):
                    base = base + bit_of(self.order[before]) * (half >> before)
                self.copies[level].wait_recv()
                cut = pl.ds(0, self.padded)
                if level == 0:
                    source = land0
                elif level == 1:
                    source = land1[self.index]
                elif level == 2:
                    source = land2[self.index]
                if level < 2:
                    block = 48

                    def one(n, carry):
                        there = pl.ds(pl.multiple_of(n * block, 16), block)
                        here = pl.ds(pl.multiple_of(base + n * block, 16), block)
                        self.keep[here, self.lanes] = (
                            self.keep[here, self.lanes].astype(F32) + source[there, cut].astype(F32)
                        ).astype(BF16)
                        return carry

                    lax.fori_loop(0, rows // block, one, 0)
                    if level == 0:
                        pl.semaphore_signal(
                            credit, inc=1, device_id=partner(1), device_id_type=MESH
                        )
                    quarter = rows // 2
                    off = pl.multiple_of(base + (1 - bit_of(self.order[level + 1])) * quarter, 16)
                    target = (land1, land2)[level][self.index]
                    self.send(level + 1, self.keep.at[pl.ds(off, quarter), self.lanes], target)
                elif level == 2:
                    here = pl.ds(pl.multiple_of(base, 16), rows)
                    total = self.keep[here, self.lanes].astype(F32) + source[:, cut].astype(F32)
                    held3[self.index][0] = total[: rows // 2].astype(BF16)
                    held3[self.index][1] = total[rows // 2 :].astype(BF16)
                    bit = bit_of(self.order[3])
                    self.send(3, held3[self.index].at[1 - bit], land3[self.index].at[0])
                else:
                    bit = bit_of(self.order[3])
                    if state.get("final") is not None:
                        state["final"].wait()
                    final[:, cut] = held3[self.index][bit].astype(F32) + land3[self.index][
                        0
                    ].astype(F32)
                    copy = pltpu.make_async_copy(
                        final.at[:, cut], self.result.at[:, pl.ds(self.at, self.padded)], osem
                    )
                    copy.start()
                    state["final"] = copy

            def close(self):
                for copy in self.copies.values():
                    copy.wait_send()

        pl.semaphore_signal(credit, inc=1, device_id=partner(1), device_id_type=MESH)
        y_first, z_first = plan["orders"]
        low, high = wg.at[pl.ds(0, half)], wg.at[pl.ds(half, half)]
        third = [wqkv.at[pl.ds(n * half, half)] for n in range(3)]
        p_down = Piece("down", y_first, inner, inner, low, 0, results[0], 0)
        p_gate = Piece("gate", z_first, inner, inner, high, 0, results[0], inner)
        p_up = Piece("up", y_first, inner, inner, wu.at[pl.ds(0, half)], 0, results[0], 2 * inner)
        pad = -(-head_cols // 128) * 128
        small = [
            Piece(
                name, order, head_cols, pad, place, offset, results[0], 3 * inner + n * pad
            )
            for n, (name, order, place, offset) in enumerate(
                (
                    ("q", y_first, third[0], 0),
                    ("k", y_first, third[1], 0),
                    ("v", y_first, third[2], 0),
                    ("out", y_first, keep_out, 0),
                )
            )
        ]
        p_q, p_k, p_v, p_out = small

        tail = Stream(
            (3, 4, 2, 5, 0, 1), [wdown.at[pl.ds(n * half, half)] for n in range(2)] + [wout]
        )
        devices = plan["devices"]
        side_count = plan["sides"]
        mine = me * side_count + side
        own_cols = plan["own_cols"]

        def condition_back(blocks):
            for block in blocks:
                row = jnp.sum(sums[block], axis=0, keepdims=True)
                dflat[0:1, block * width : (block + 1) * width] = row
                rows = jnp.broadcast_to(row, (16, width)).astype(BF16)
                for _ in range(2):
                    b, h, slot = tail.take()
                    dcond[h : h + 1, :] += dot(rows, slot[...], 1, 1)[0:1]
                    tail.fill(99)

        def share_out():
            lanes = lax.broadcasted_iota(jnp.int32, (16, 128), 0)
            base = jnp.zeros((16, 128), F32)
            silu_f = silu.astype(F32)
            for n in range(width // 128):
                base = jnp.where(lanes == n, silu_f[:, n * 128 : (n + 1) * 128], base)
            row_a = width // 128
            for n in range(devices):
                first = dflat[0:1, n * own_cols : n * own_cols + 128]
                rest = own_cols - 128
                second = dflat[0:1, n * own_cols + 128 : n * own_cols + 256]
                packet = jnp.where(lanes == row_a, first, base)
                packet = jnp.where(lanes == row_a + 1, second, packet)
                packs[n] = packet.astype(BF16)

            def one(n, carry):
                other = lax.rem(mine + n, devices)
                pltpu.make_async_remote_copy(
                    src_ref=packs.at[other], dst_ref=came.at[mine], send_sem=psem.at[0],
                    recv_sem=psem.at[1],
                    device_id={
                        "dp": lax.div(other, side_count), "tensor": lax.rem(other, side_count)
                    },
                    device_id_type=MESH,
                ).start()
                return carry

            lax.fori_loop(1, devices, one, 0)
            came[mine] = packs[mine]

        def take_in():
            every = pl.ds(0, devices - 1)
            whole = pltpu.make_async_remote_copy(
                src_ref=packs.at[every], dst_ref=came.at[every], send_sem=psem.at[0],
                recv_sem=psem.at[1], device_id=mate, device_id_type=MESH,
            )
            whole.wait_send()
            whole.wait_recv()
            seen = came[...].astype(F32)
            row_a = width // 128
            silu_all = jnp.concatenate([seen[:, n, :] for n in range(row_a)], axis=1).astype(BF16)
            columns = jnp.concatenate([seen[:, row_a, :], seen[:, row_a + 1, :]], axis=1)
            bias_out[...] = jnp.broadcast_to(jnp.sum(columns, axis=0, keepdims=True), bias_out.shape)
            own[...] = dot(columns.astype(BF16), silu_all, 0, 0)
            copy = pltpu.make_async_copy(own.at[pl.ds(0, own_cols)], ada_out, asem.at[0])
            copy.start()
            copy.wait()
            slope = cond_sig * (1.0 + cond_f * (1.0 - cond_sig))
            whole_row = jnp.concatenate([dcond[0:1, :], dcond[1:2, :]], axis=1)
            cond_out[...] = whole_row * slope

    def lane_right(array):
        def right(start, size):
            if not isinstance(start, int):
                start = pl.multiple_of(start, 128)
            part = [array[i, :, pl.ds(start, size)] for i in range(2)]
            return dot(flip[:, 0:LEN], part[0], 1, 0) + dot(flip[:, LEN:], part[1], 1, 0)
        return right

    def row_right(array, base):
        def right(start, size):
            at = base + start
            if not isinstance(start, int):
                at = pl.multiple_of(at, 16)
            part = [array[i, pl.ds(at, size), :] for i in range(2)]
            return dot(flip[:, 0:LEN], part[0], 1, 1) + dot(flip[:, LEN:], part[1], 1, 1)
        return right

    def plain_grad(right, columns, target):
        (stage, gsem) = extra
        pend = {}
        for n, start in enumerate(range(0, columns, TILE)):
            size = min(TILE, columns - start)
            slot = n % 2
            if slot in pend:
                pend[slot].wait()
            stage[slot, :, 0:size] = right(start, size).astype(BF16)
            copy = pltpu.make_async_copy(
                stage.at[slot], target.at[:, pl.ds(start, TILE)], gsem.at[slot]
            )
            copy.start()
            pend[slot] = copy
        for copy in pend.values():
            copy.wait()

    def plain_grad_in(left, right, columns, target):
        for image in range(2):
            flip[:, image * LEN : (image + 1) * LEN] = left[image].astype(F32).T.astype(BF16)
        plain_grad(right, columns, target)

    if plan["fused"]:
        p_down.compute(lane_right(hid), 0, 2)
        turned(h2, p_gate.order)
        p_down.add(0)
        p_gate.compute(lane_right(dgate), 1, 2)
        p_gate.add(0)
    else:
        plain_grad_in(dml, lane_right(hid), inner, results[0])
        plain_grad_in(h2, lane_right(dgate), inner, results[1])
        plain_grad_in(h2, lane_right(dup), inner, results[2])

    for copy in go_b:
        copy.wait_recv()

    def second_back(rows):
        grad = own[rows, :] + recv_a[rows, :].astype(F32)
        norm, inverse = normed(tok[rows, :].astype(F32) + gate_one * attn[rows, :])
        middle = cot[rows, :].astype(F32) + norm_back(grad * (1.0 + scale_two), norm, inverse)
        dx1[rows, :] = middle
        dat[0, rows, :] = (gate_one * middle).astype(BF16)
        sums[2] += fold(middle * attn[rows, :])
        sums[3] += fold(grad)
        sums[4] += fold(grad * norm)

    rows_loop(second_back, go_dat)

    strips_of(mlp_strip(1), send_c, go_c)
    if plan["fused"]:
        p_down.copies[0].wait_send()
        turned(h2, p_up.order)
        p_up.compute(lane_right(dup), 0, 2)

    def heads_back(image):
        a_f[...] = dot(wout[...], dat[image], 1, 1)
        cosine, sine = cos_t[image], sin_t[image]

        def head(h, carry):
            at = image * heads + h
            rows = pl.ds(pl.multiple_of(h * HD, 8), HD)
            da = a_f[rows, :].astype(BF16)
            probs = p_s[at]
            query, key, value = q_s[at], k_s[at], v_s[at]
            dprobs = dot(value, da, 0, 0)
            dvalue = dot(da, probs.astype(BF16), 1, 1)
            inside = jnp.sum(probs * dprobs, axis=0, keepdims=True)
            dscores = (probs * (dprobs - inside)).astype(BF16)
            dquery = dot(key, dscores, 1, 0)
            dkey = dot(query, dscores, 1, 1)
            dquery = (dquery * cosine - rotate_rows(dquery * sine)) * scale
            dkey = dkey * cosine - rotate_rows(dkey * sine)
            qkv_f[rows, :] = dquery
            qkv_f[pl.ds(pl.multiple_of(head_cols + h * HD, 8), HD), :] = dkey
            qkv_f[pl.ds(pl.multiple_of(2 * head_cols + h * HD, 8), HD), :] = dvalue
            return carry

        lax.fori_loop(0, heads, head, 0, unroll=2)
        dqkv[image] = qkv_f[...].astype(BF16)

    heads_back(0)
    if plan["fused"]:
        p_up.add(0)
        p_down.add(1)
    for copy in go_dat:
        copy.wait_recv()
    heads_back(1)

    def dh1_strip(image):
        return lambda cols: dot(dqkv[image], wqkv[:, cols], 0, 0)

    for copy in go_b:
        copy.wait_send()
    strips_of(dh1_strip(1), send_a, go_d)
    strips_of(dh1_strip(0), keep=own)

    if plan["fused"]:
        p_gate.copies[0].wait_send()
        p_up.copies[0].wait_send()
        p_gate.add(1)
        turned(h1, p_q.order)
        p_q.compute(row_right(dqkv, 0), 0)
        p_q.go()
        p_k.compute(row_right(dqkv, head_cols), 1)
        p_q.add(0)
        p_k.go()
        p_q.copies[0].wait_send()
        p_v.compute(row_right(dqkv, 2 * head_cols), 0)
        p_k.add(0)
        p_v.go()
        p_down.add(2)
        p_k.copies[0].wait_send()
        turned(dat, p_out.order)
        p_out.compute(row_right(a_t, 0), 1)
        p_v.add(0)
        p_out.go()
        p_up.add(1)
        p_out.add(0)
    else:
        plain_grad_in(h1, row_right(dqkv, 0), 3 * head_cols, results[3])
        plain_grad_in(dat, row_right(a_t, 0), head_cols, results[4])

    pieces = [(n, min(LEN, width - n)) for n in range(0, width, LEN)]
    for n, size in pieces:
        p_s[n // LEN, :, 0:size] = dot(hid[0], wdown[:, n : n + size], 1, 0)
    for copy in go_c:
        copy.wait_recv()

    def finish(rows):
        mine_part = [p_s[n // LEN, rows, 0:size] for n, size in pieces]
        branch = jnp.concatenate(mine_part, axis=1) + recv_c[rows, :].astype(F32)
        out[rows, :] = (
            tok[rows, :].astype(F32) + gate_one * attn[rows, :] + gate_two * branch
        ).astype(BF16)
        sums[5] += fold(cot[rows, :].astype(F32) * branch)

    rows_loop(finish)
    if plan["fused"]:
        tail.fill(99)
        condition_back((3, 4))
    for copy in go_d:
        copy.wait_recv()

    def first_back(rows):
        grad = own[rows, :] + recv_a[rows, :].astype(F32)
        norm, inverse = normed(tok[rows, :].astype(F32))
        dtok[rows, :] = dx1[rows, :] + norm_back(grad * (1.0 + scale_one), norm, inverse)
        sums[0] += fold(grad)
        sums[1] += fold(grad * norm)

    rows_loop(first_back)

    if plan["fused"]:
        p_gate.add(2)
        p_up.add(2)
        condition_back((2, 5))
        p_down.add(3)
        p_q.add(1)
        condition_back((0, 1))
        share_out()
        p_k.add(1)
        p_q.add(2)
        p_gate.add(3)
        p_up.add(3)
        p_v.add(1)
        p_k.add(2)
        p_q.add(3)
        p_out.add(1)
        p_v.add(2)
        p_k.add(3)
        take_in()
        p_out.add(2)
        p_v.add(3)
        p_out.add(3)
        state["final"].wait()
        pl.semaphore_wait(credit, 1)
        for piece in (p_gate, p_up, p_down, *small):
            for level, copy in piece.copies.items():
                if level > 0 or piece in (p_v, p_out):
                    copy.wait_send()
    else:
        for n in range(6):
            results[5][n : n + 1, :] = jnp.sum(sums[n], axis=0, keepdims=True)
    for copy in (*go_h1, *go_cot, go_row, *go_h2, *go_dat, *go_c, *go_d):
        copy.wait_send()


def lay_out_kernel(cuts, whole, ada, tok, out, bias, *refs):
    (down, gate_up, qkv, wout, ada_to, tok_to, out_to, bias_to) = refs
    inner, head_cols, pad, own_cols = cuts
    ada_to[...] = ada[...]
    tok_to[...] = tok[...]
    out_to[...] = out[...]
    down[...] = whole[:, 0:inner]
    gate_up[:, 0, :] = whole[:, inner : 2 * inner]
    gate_up[:, 1, :] = whole[:, 2 * inner : 3 * inner]
    start = 3 * inner
    for n in range(3):
        qkv[n] = whole[:, start + n * pad : start + n * pad + head_cols]
    start += 3 * pad
    wout[...] = whole[:, start : start + head_cols]
    bias_to[...] = bias[0:1, 0:own_cols]


def lay_out(whole, ada, tok, out, bias, inner, head_cols, own_cols):
    rows = whole.shape[0]
    vmem = pl.BlockSpec(memory_space=pltpu.VMEM)
    pad = -(-head_cols // 128) * 128
    S = jax.ShapeDtypeStruct
    return pl.pallas_call(
        functools.partial(lay_out_kernel, (inner, head_cols, pad, own_cols)),
        out_shape=(
            S((rows, inner), F32), S((rows, 2, inner), F32), S((3, rows, head_cols), F32),
            S((rows, head_cols), F32), S(ada.shape, F32), S(tok.shape, F32), S(out.shape, BF16),
            S((1, own_cols), F32),
        ),
        in_specs=[vmem] * 5,
        out_specs=[vmem] * 8,
        compiler_params=pltpu.CompilerParams(vmem_limit_bytes=62 * 1024 * 1024),
    )(whole, ada, tok, out, bias)


def run_block(tok, cot, cond, grid, bias, wada, wqkv, wout, wgu, wdown):
    width = tok.shape[1]
    head_cols = wout.shape[0]
    heads = head_cols // HD
    inner = wdown.shape[0]
    strips = width // STRIP
    count = lax.axis_size("dp")
    sides = lax.axis_size("tensor")
    devices = count * sides
    own_cols = 6 * width // devices
    vmem = pl.BlockSpec(memory_space=pltpu.VMEM)
    hbm = pl.BlockSpec(memory_space=pl.ANY)
    V = pltpu.VMEM
    D = pltpu.SemaphoreType.DMA
    copies = 10 + 4 * strips
    fused = count == 16 and width % (8 * count) == 0 and 128 < own_cols <= 256 and own_cols % 8 == 0
    names = ["down", "gate", "up", "q", "k", "v", "out"]
    pad = -(-head_cols // 128) * 128
    if fused:
        results = [
            jax.ShapeDtypeStruct((width // count, 3 * inner + 4 * pad), F32),
            jax.ShapeDtypeStruct((own_cols, width), F32),
            jax.ShapeDtypeStruct((1, width), F32),
            jax.ShapeDtypeStruct((8, 256), F32),
        ]
        result_specs = [hbm, hbm, vmem, vmem]
        chunk = width // count
        widths = [inner, inner, inner, pad, pad, pad, pad]
        extra = [
            V((width // 2, inner), BF16),
            V((width // 2, pad), BF16),
            V((width // 2, inner), BF16),
            V((chunk, inner), F32),
            D((len(names), 5)),
            D((len(names), 5)),
            D(()),
            pltpu.SemaphoreType.REGULAR,
            V((devices, 16, 128), BF16),
            V((devices, 16, 128), BF16),
            V((8, 6 * width + 128), F32),
            V((8, width // 2), F32),
            D((2,)),
            *[V((width // 4, w), BF16) for w in widths],
            *[V((width // 8, w), BF16) for w in widths],
            *[V((1, chunk, w), BF16) for w in widths],
            *[V((2, chunk, w), BF16) for w in widths],
        ]
        strides = [1, 2, 4, 8]
    else:
        wide = [inner, inner, inner, 3 * head_cols, head_cols]
        results = [jax.ShapeDtypeStruct((width, -(-w // TILE) * TILE), BF16) for w in wide]
        results += [jax.ShapeDtypeStruct((6, width), F32)]
        result_specs = [hbm] * 5 + [vmem]
        extra = [V((2, width, TILE), BF16), D((2,))]
        strides = []
    plan = {
        "fused": fused, "results": len(results), "count": count, "pieces": names,
        "devices": devices, "sides": sides, "own_cols": own_cols,
        "early": 8, "strides": strides, "orders": ((1, 2, 4, 8), (1, 4, 2, 8)),
    }
    return pl.pallas_call(
        functools.partial(block_kernel, plan),
        out_shape=(
            jax.ShapeDtypeStruct((LEN, width), BF16),
            jax.ShapeDtypeStruct((LEN, width), F32),
            *results,
        ),
        in_specs=[vmem] * 3 + [pl.BlockSpec(memory_space=pltpu.SMEM), vmem] + [hbm] * 5,
        out_specs=[vmem] * 2 + result_specs,
        scratch_shapes=[
            V((8, width), F32), V((2, 16, width // 2), BF16), V((2, HD, LEN), F32),
            V((2, HD, LEN), F32), V((3, 48, 2, inner), BF16),
                        V(wqkv.shape, BF16), V(wout.shape, BF16), V((width, inner), BF16),
            V((width, inner), BF16), V(wdown.shape, BF16),
            *[V((2, LEN, width), BF16)] * 4,
            *[V((2 * heads, HD, LEN), BF16)] * 3,
            V((2 * heads, LEN, LEN), F32),
            V((3 * head_cols, LEN), F32),
            V((head_cols, LEN), F32),
            V((2, head_cols, LEN), BF16),
            *[V((2, LEN, inner), BF16)] * 3,
            V((2, 3 * head_cols, LEN), BF16),
            *[V((LEN, width), F32)] * 3,
            *[V((LEN, width), BF16)] * 4,
            *[V((8, width), F32)] * 2,
            V((width, 2 * LEN), BF16),
            V((6, 8, width), F32),
            D((6,)),
            D((8,)),
            D((copies,)),
            D((copies,)),
            *extra,
        ],
        compiler_params=pltpu.CompilerParams(
            collective_id=0, has_side_effects=True, vmem_limit_bytes=62 * 1024 * 1024
        ),
    )(tok, cot, cond, grid, bias, wada, wqkv, wout, wgu, wdown)


def sum_over_images(partial):
    count = lax.axis_size("dp")
    me = lax.axis_index("dp")
    held = partial.reshape(count, partial.shape[0] // count, partial.shape[1])
    stride = 1
    left = count
    while left > 1:
        bit = (me // stride) % 2
        pairs = held.reshape(left // 2, 2, *held.shape[1:])
        keep = lax.dynamic_index_in_dim(pairs, bit, 1, keepdims=False)
        send = lax.dynamic_index_in_dim(pairs, 1 - bit, 1, keepdims=False)
        came = lax.ppermute(send, "dp", [(i, i ^ stride) for i in range(count)])
        held = keep.astype(F32) + came.astype(F32)
        left //= 2
        stride *= 2
        if left > 1:
            held = held.astype(BF16)
    return held[0]


def body(tokens, condition, grid_shape, w_ada, b_ada, w_qkv, w_out, w_gate_up, w_down, cotangent):
    width = tokens.shape[1]
    inner = w_down.shape[0]
    head_cols = w_out.shape[0]
    wqkv = w_qkv.transpose(1, 2, 0).reshape(3 * head_cols, width)
    layer_out, d_tokens, *grads = run_block(
        tokens, cotangent, condition, grid_shape, b_ada.reshape(-1, 128), w_ada, wqkv, w_out,
        w_gate_up, w_down,
    )
    devices_all = lax.axis_size("dp") * lax.axis_size("tensor")
    own_cols = 6 * width // devices_all
    if len(grads) == 4:
        whole, ada, d_condition, bias_rows = grads
        down, gate_up, qkv, g_out, ada, d_tokens, layer_out, bias_part = lay_out(
            whole, ada, d_tokens, layer_out, bias_rows, inner, head_cols, own_cols
        )
        grad_down, grad_gate_up = down.T, gate_up
        grad_qkv, grad_out = qkv.transpose(1, 0, 2), g_out.T
        weight_part, bias_part = ada.T, bias_part.reshape(own_cols)
    else:
        grad_down = sum_over_images(grads[0]).T
        grad_gate_up = jnp.stack([sum_over_images(grads[1]), sum_over_images(grads[2])], axis=1)
        grad_qkv = sum_over_images(grads[3][:, : 3 * head_cols]).reshape(-1, 3, head_cols)
        grad_out = sum_over_images(grads[4][:, :head_cols]).T
        cond = condition.astype(F32)
        cond_sigmoid = jax.nn.sigmoid(cond)
        silu_cond = (cond * cond_sigmoid).astype(BF16)
        d_mod = grads[5].reshape(1, 6 * width).astype(BF16)
        d_condition = (
            dot(d_mod, w_ada, 1, 1) * cond_sigmoid * (1.0 + cond * (1.0 - cond_sigmoid))
        )
        packed = jnp.concatenate(
            [
                d_mod.reshape(devices_all, own_cols),
                jnp.broadcast_to(silu_cond, (devices_all, width)),
            ],
            axis=1,
        )
        packed = jnp.pad(packed, ((0, 0), (0, -packed.shape[1] % 128)))
        packed = lax.all_to_all(
            packed.reshape(devices_all, -1, 128), ("dp", "tensor"), 0, 0, tiled=True
        ).reshape(devices_all, -1)
        columns = packed[:, :own_cols]
        silu_rows = packed[:, own_cols : own_cols + width]
        weight_part = dot(silu_rows, columns, 0, 0)
        bias_part = jnp.sum(columns.astype(F32), axis=0)
    return (
        layer_out, d_tokens, d_condition, weight_part, bias_part,
        grad_qkv, grad_out, grad_gate_up, grad_down,
    )


def solution(mesh):
    placed = (
        P(("dp", "tensor"), None),
        P(("dp", "tensor"), None),
        P("dp", None),
        P(),
        P(),
        P(None, None, "tensor"),
        P("tensor", None),
        P(None, None, "tensor"),
        P("tensor", None),
        P(("dp", "tensor"), None),
    )
    return jax.shard_map(
        body,
        mesh=mesh,
        in_specs=placed,
        out_specs=(
            P(("dp", "tensor"), None),
            P(("dp", "tensor"), None),
            P(("dp", "tensor"), None),
            P(None, ("dp", "tensor")),
            P(("dp", "tensor")),
            P("dp", None, "tensor"),
            P("tensor", "dp"),
            P("dp", None, "tensor"),
            P("tensor", "dp"),
        ),
        check_vma=False,
    )
```

```python
import functools

import jax
import jax.numpy as jnp
from jax import lax
from jax.experimental import pallas as pl
from jax.experimental.pallas import tpu as pltpu
from jax.sharding import PartitionSpec as P

HD = 72
LEN = 256
EPSILON = 1e-06
MESH = pl.DeviceIdType.MESH
F32 = jnp.float32
BF16 = jnp.bfloat16
ROWS = 32
STRIP = 384
TILE = 256


def dot(left, right, left_dim, right_dim):
    return lax.dot_general(
        left, right, (((left_dim,), (right_dim,)), ((), ())), preferred_element_type=F32
    )


def normed(values):
    centered = values - jnp.mean(values, axis=-1, keepdims=True)
    variance = jnp.mean(centered * centered, axis=-1, keepdims=True)
    inverse = lax.rsqrt(variance + EPSILON)
    return centered * inverse, inverse


def norm_back(upstream, norm, inverse):
    mean_grad = jnp.mean(upstream, axis=-1, keepdims=True)
    mean_cross = jnp.mean(upstream * norm, axis=-1, keepdims=True)
    return inverse * (upstream - mean_grad - norm * mean_cross)


def rotate_rows(values):
    quarter = HD // 4
    a, b = values[:quarter], values[quarter : 2 * quarter]
    c, d = values[2 * quarter : 3 * quarter], values[3 * quarter :]
    return jnp.concatenate([-b, a, -d, c], axis=0)


def fold(values):
    return jnp.sum(values.reshape(values.shape[0] // 8, 8, values.shape[1]), axis=0)


class Several:
    def __init__(self, copies):
        self.copies = copies

    def wait_send(self):
        for copy in self.copies:
            copy.wait_send()

    def wait_recv(self):
        for copy in self.copies:
            copy.wait_recv()


def block_kernel(
    plan, tok, cot, cond, grid, bias,
    wada_hbm, wqkv_hbm, wout_hbm, wgu_hbm, wdown_hbm,
    out, dtok, *rest,
):
    results, rest = rest[: plan["results"]], rest[plan["results"] :]
    (
        mod, silu_two, cos_t, sin_t, raw,
        wqkv, wout, wg, wu, wdown,
        h1, h2, dml, dat,
        q_s, k_s, v_s, p_s, qkv_f, a_f, a_t,
        hid, dgate, dup, dqkv,
        attn, dx1, own,
        send_a, send_c, recv_a, recv_c, row_out, row_in,
        flip, sums,
        wsem, asem, ssem, rsem, *extra,
    ) = rest
    width = tok.shape[1]
    heads = q_s.shape[0] // 2
    head_cols = heads * HD
    inner = wdown.shape[0]
    side = lax.axis_index("tensor")
    mate = {"tensor": 1 - side}
    scale = HD ** (-0.5)

    loads = [
        pltpu.make_async_copy(src, dst, wsem.at[i])
        for i, (src, dst) in enumerate(
            ((wqkv_hbm, wqkv), (wout_hbm, wout), (wdown_hbm, wdown))
        )
    ]
    half_rows = width // 2
    slots = [
        ref.at[pl.ds(n * half_rows, half_rows), pl.ds(0, width)] for ref in (wg, wu) for n in range(2)
    ]

    class Stream:
        def __init__(self, blocks, slots):
            self.chunks = [(b, h) for b in blocks for h in range(2)]
            self.slots = slots
            self.copies = []
            self.at = 0

        def fill(self, most):
            while len(self.copies) < min(most, len(self.chunks), self.at + len(self.slots)):
                n = len(self.copies)
                b, h = self.chunks[n]
                copy = pltpu.make_async_copy(
                    wada_hbm.at[pl.ds(h * half_rows, half_rows), pl.ds(b * width, width)],
                    self.slots[n % len(self.slots)], asem.at[n % len(self.slots)],
                )
                copy.start()
                self.copies.append(copy)

        def take(self):
            n = self.at
            self.copies[n].wait()
            b, h = self.chunks[n]
            self.at += 1
            return b, h, self.slots[n % len(self.slots)]

    stream = Stream((0, 1, 5, 2, 3, 4), slots)
    stream.fill(4)

    me = lax.axis_index("dp")

    def bit_of(stride):
        return lax.rem(lax.div(me, stride), 2)

    def partner(stride):
        return {"dp": me + stride - 2 * stride * bit_of(stride)}

    barrier = pltpu.get_barrier_semaphore()
    friends = [mate] + [partner(s) for s in plan["strides"]]
    for friend in friends:
        pl.semaphore_signal(barrier, inc=1, device_id=friend, device_id_type=MESH)

    def give(src, dst, slot):
        return pltpu.make_async_remote_copy(
            src_ref=src, dst_ref=dst, send_sem=ssem.at[slot], recv_sem=rsem.at[slot],
            device_id=mate, device_id_type=MESH,
        )

    def gather(buf, slot):
        half = LEN // 2
        return [
            give(buf.at[0, pl.ds(c * half, half)], buf.at[1, pl.ds(c * half, half)], slot + c)
            for c in range(2)
        ]

    strips = width // STRIP

    def scatter(send, recv, slot):
        return [
            give(
                send.at[:, pl.ds(c * STRIP, STRIP)], recv.at[:, pl.ds(c * STRIP, STRIP)], slot + c
            )
            for c in range(strips)
        ]

    go_h1, go_h2, go_dat = (gather(b, 2 * i) for i, b in enumerate((h1, h2, dat)))
    go_cot = [
        give(cot.at[pl.ds(at, size)], dml.at[1, pl.ds(at, size)], slot)
        for at, size, slot in ((0, 96, 6), (96, 96, 7), (192, 64, 9 + 4 * (width // STRIP)))
    ]
    go_row = give(row_out, row_in, 8 + 4 * (width // STRIP))
    go_a, go_b, go_c, go_d = (
        scatter(s, r, 8 + strips * i)
        for i, (s, r) in enumerate(
            ((send_a, recv_a), (send_a, recv_a), (send_c, recv_c), (send_a, recv_a))
        )
    )

    def rows_loop(step, copies=None):
        half = LEN // 2
        count = half // ROWS
        for c in range(2):
            def one(i, carry, c=c):
                step(pl.ds(pl.multiple_of(c * half + i * ROWS, ROWS), ROWS))
                return carry
            lax.fori_loop(0, count, one, 0)
            if copies is not None:
                copies[c].start()

    cond_f = cond[...].astype(F32)
    cond_sig = jax.nn.sigmoid(cond_f)
    silu = (cond_f * cond_sig).astype(BF16)
    silu_rows = jnp.broadcast_to(silu.astype(F32), (16, width))
    for h in range(2):
        silu_two[h] = silu_rows[:, h * half_rows : (h + 1) * half_rows].astype(BF16)

    bias_f = bias[...].astype(F32)
    tiles = width // bias.shape[1]

    def bias_row(b):
        return jnp.concatenate([bias_f[b * tiles + n : b * tiles + n + 1] for n in range(tiles)], axis=1)

    def modulate(count):
        for _ in range(count):
            row = None
            for _ in range(2):
                b, h, slot = stream.take()
                part = dot(silu_two[h], slot[...], 1, 0)[0:1]
                row = part if row is None else row + part
                stream.fill(99)
            mod[b : b + 1, :] = row + bias_row(b)

    def pre_norm(rows):
        norm, _ = normed(tok[rows, :].astype(F32))
        dx1[rows, :] = norm

    rows_loop(pre_norm)
    pl.semaphore_wait(barrier, len(friends))
    go_cot[0].start()
    modulate(2)
    for load in loads:
        load.start()
    shift_one, scale_one = mod[0:1], mod[1:2]

    def first_norm(rows):
        h1[0, rows, :] = (dx1[rows, :] * (1.0 + scale_one) + shift_one).astype(BF16)

    rows_loop(first_norm, go_h1)
    modulate(1)
    gate_two = mod[5:6]
    row_out[...] = jnp.broadcast_to(gate_two, row_out.shape)
    go_row.start()
    go_cot[1].start()
    sums[...] = jnp.zeros_like(sums)

    quarter = HD // 4
    limits = []
    for image in range(2):
        at = side if image == 0 else 1 - side
        tall, wide = grid[at, 0], grid[at, 1]
        limits.append(tall * wide)
        spot = lax.broadcasted_iota(jnp.int32, (1, LEN), 1).astype(F32)
        wide_f = jnp.full((1, LEN), wide, jnp.int32).astype(F32)
        row_at = jnp.floor((spot + 0.5) / wide_f)
        col_at = spot - row_at * wide_f
        step = lax.broadcasted_iota(jnp.int32, (quarter, LEN), 0).astype(F32)
        frequency = jnp.exp(step * (-9.210340371976184 / quarter))
        both = jnp.concatenate([row_at * frequency, col_at * frequency], axis=0)
        for table, turn in ((cos_t, jnp.cos), (sin_t, jnp.sin)):
            seen = turn(both)
            first, second = seen[:quarter], seen[quarter:]
            table[image] = jnp.concatenate([first, first, second, second], axis=0)

    depth = raw.shape[1]
    ring = raw.shape[0]
    parts = {"next": 0, "copies": []}
    r = lax.broadcasted_iota(jnp.int32, (2 * depth, 2 * depth), 0)
    c = lax.broadcasted_iota(jnp.int32, (2 * depth, 2 * depth), 1)
    sorter = jnp.where(c == jnp.where(r < depth, 2 * r, 2 * (r - depth) + 1), 1.0, 0.0).astype(BF16)

    def fetch(n):
        if n < width // depth:
            copy = pltpu.make_async_copy(
                wgu_hbm.at[pl.ds(n * depth, depth)], raw.at[n % ring], wsem.at[3 + n % ring]
            )
            copy.start()
            parts["copies"].append(copy)

    def pull_apart(until):
        while parts["next"] < until:
            n = parts["next"]
            parts["copies"][n].wait()
            parted = dot(sorter, raw[n % ring].reshape(2 * depth, inner), 1, 0).astype(BF16)
            wg[n * depth : (n + 1) * depth, :] = parted[:depth]
            wu[n * depth : (n + 1) * depth, :] = parted[depth:]
            fetch(n + ring)
            parts["next"] += 1

    def heads_forward(image):
        for part in range(3):
            qkv_f[part * head_cols : (part + 1) * head_cols, :] = dot(
                wqkv[part * head_cols : (part + 1) * head_cols, :], h1[image], 1, 1
            )
        cosine, sine = cos_t[image], sin_t[image]
        ok = lax.broadcasted_iota(jnp.int32, (LEN, LEN), 0) < limits[image]

        def head(h, carry):
            at = image * heads + h
            rows = pl.ds(pl.multiple_of(h * HD, 8), HD)
            query = qkv_f[rows, :]
            key = qkv_f[pl.ds(pl.multiple_of(head_cols + h * HD, 8), HD), :]
            value = qkv_f[pl.ds(pl.multiple_of(2 * head_cols + h * HD, 8), HD), :].astype(BF16)
            query = ((query * cosine + rotate_rows(query) * sine) * scale).astype(BF16)
            key = (key * cosine + rotate_rows(key) * sine).astype(BF16)
            q_s[at], k_s[at], v_s[at] = query, key, value
            scores = dot(key, query, 0, 0)
            scores = jnp.where(ok, scores, -1e30)
            top = jnp.max(scores, axis=0, keepdims=True)
            exps = jnp.exp(scores - top)
            probs = exps * (1.0 / jnp.sum(exps, axis=0, keepdims=True))
            p_s[at] = probs
            a_f[rows, :] = dot(value, probs.astype(BF16), 1, 0)
            return carry

        lax.fori_loop(0, heads, head, 0, unroll=4)
        a_t[image] = a_f[...].astype(BF16)

    def strips_of(make, send=None, copies=None, keep=None):
        for c in range(strips):
            cols = slice(c * STRIP, (c + 1) * STRIP)
            value = make(cols)
            if send is not None:
                send[:, cols] = value.astype(BF16)
                copies[c].start()
            else:
                keep[:, cols] = value

    for n in range(ring):
        fetch(n)
    loads[0].wait()
    heads_forward(0)
    modulate(3)
    pull_apart(plan["early"])
    gate_one, shift_two, scale_two = mod[2:3], mod[3:4], mod[4:5]
    for copy in go_h1:
        copy.wait_recv()
    heads_forward(1)
    loads[1].wait()
    strips_of(lambda cols: dot(a_t[1], wout[:, cols], 0, 0), send_a, go_a)
    go_cot[2].start()
    strips_of(lambda cols: dot(a_t[0], wout[:, cols], 0, 0), keep=own)

    gate_two_row = gate_two

    def mlp_grad(rows):
        dml[0, rows, :] = (gate_two_row * cot[rows, :].astype(F32)).astype(BF16)

    rows_loop(mlp_grad)
    pull_apart(width // depth)
    for copy in go_a:
        copy.wait_recv()

    def second_norm(rows):
        branch = own[rows, :] + recv_a[rows, :].astype(F32)
        attn[rows, :] = branch
        middle = tok[rows, :].astype(F32) + gate_one * branch
        norm, _ = normed(middle)
        h2[0, rows, :] = (norm * (1.0 + scale_two) + shift_two).astype(BF16)

    rows_loop(second_norm, go_h2)

    def turned(left, order):
        for image in range(2):
            flat = left[image].astype(F32).T
            chunk = width // plan["count"]
            for pair in range(plan["count"] // 2):
                place = [2 * pair, 2 * pair + 1]
                parts = []
                for spot in place:
                    which = 0
                    for level, stride in enumerate(order):
                        which += stride * ((spot >> (len(order) - 1 - level)) & 1)
                    parts.append(flat[which * chunk : (which + 1) * chunk])
                flip[2 * pair * chunk : 2 * (pair + 1) * chunk, image * LEN : (image + 1) * LEN] = (
                    jnp.concatenate(parts, axis=0).astype(BF16)
                )

    loads[2].wait()

    def feed_forward(image):
        def tile(j, carry):
            cols = pl.ds(pl.multiple_of(j * TILE, TILE), TILE)
            gate = dot(h2[image], wg[:, cols], 1, 0)
            up = dot(h2[image], wu[:, cols], 1, 0)
            grad = dot(dml[image], wdown[cols, :], 1, 1)
            sig = jax.nn.sigmoid(gate)
            act = gate * sig
            hid[image, :, cols] = (act * up).astype(BF16)
            dgate[image, :, cols] = (grad * up * sig * (1.0 + gate * (1.0 - sig))).astype(BF16)
            dup[image, :, cols] = (grad * act).astype(BF16)
            return carry

        lax.fori_loop(0, inner // TILE, tile, 0)

    def dh2_strip(image):
        return lambda cols: dot(dgate[image], wg[cols, :], 1, 1) + dot(dup[image], wu[cols, :], 1, 1)

    feed_forward(0)
    strips_of(dh2_strip(0), keep=own)
    for copy in go_cot:
        copy.wait_recv()
    go_row.wait_recv()
    gate_mate = row_in[0:1]

    def mate_grad(rows):
        dml[1, rows, :] = (gate_mate * dml[1, rows, :].astype(F32)).astype(BF16)

    rows_loop(mate_grad)
    if plan["fused"]:
        turned(dml, plan["orders"][0])
    for copy in go_h2:
        copy.wait_recv()
    feed_forward(1)

    def mlp_strip(image):
        return lambda cols: dot(hid[image], wdown[:, cols], 1, 0)

    for copy in go_a:
        copy.wait_send()
    strips_of(dh2_strip(1), send_a, go_b)

    if plan["fused"]:
        (
            give_one, keep_out, land0, final, gsend, grecv, osem, credit, packs, came, dflat, dcond, psem,
            *spots,
        ) = extra
        _, ada_out, cond_out, bias_out = results
        dflat[...] = jnp.zeros_like(dflat)
        dcond[...] = jnp.zeros_like(dcond)
        many = len(plan["pieces"])
        land1, land2, land3, held3 = (spots[n * many : (n + 1) * many] for n in range(4))
        half = width // 2
        gives = [wu.at[pl.ds(half, half)], give_one]
        core_bit = bit_of(1)
        state = {"gives": 0, "lands": 0}

        class Piece:
            def __init__(self, name, order, columns, padded, keep, offset, result, at):
                self.name, self.order, self.columns, self.padded = name, order, columns, padded
                self.keep, self.offset, self.result, self.at = keep, offset, result, at
                self.index = plan["pieces"].index(name)
                self.lanes = pl.ds(offset, padded)
                self.copies = {}

            def send(self, level, src, dst):
                copy = pltpu.make_async_remote_copy(
                    src_ref=src, dst_ref=dst, send_sem=gsend.at[self.index, level],
                    recv_sem=grecv.at[self.index, level], device_id=partner(self.order[level]),
                    device_id_type=MESH,
                )
                copy.start()
                self.copies[level] = copy

            def compute(self, right, give, cuts=0):
                self.give = gives[give]
                step = STRIP

                def tile(start, size, pad):
                    total = right(start, size)
                    low, high = total[:half], total[half:]
                    kept = jnp.where(core_bit == 0, low, high).astype(BF16)
                    gone = jnp.where(core_bit == 0, high, low).astype(BF16)
                    place = self.offset + start
                    if pad > size:
                        blank = jnp.zeros((half, pad - size), BF16)
                        kept = jnp.concatenate([kept, blank], axis=1)
                        gone = jnp.concatenate([gone, blank], axis=1)
                    if not isinstance(start, int):
                        place = pl.multiple_of(place, 128)
                        start = pl.multiple_of(start, 128)
                    self.keep[:, pl.ds(place, pad)] = kept
                    self.give[:, pl.ds(start, pad)] = gone

                whole = self.columns // step

                def one(n, carry):
                    tile(n * step, step, step)
                    return carry

                if cuts:
                    copies = []
                    for n in range(cuts):
                        part = whole // cuts
                        lax.fori_loop(n * part, (n + 1) * part, one, 0)
                        if n == 0:
                            pl.semaphore_wait(credit, 1)
                        lanes = pl.ds(n * part * step, part * step)
                        copy = pltpu.make_async_remote_copy(
                            src_ref=self.give.at[:, lanes], dst_ref=land0.at[:, lanes],
                            send_sem=gsend.at[self.index, 4 * n], recv_sem=grecv.at[self.index, 4 * n],
                            device_id=partner(1), device_id_type=MESH,
                        )
                        copy.start()
                        copies.append(copy)
                    self.copies[0] = Several(copies)
                    return
                lax.fori_loop(0, whole, one, 0)
                left = self.columns - whole * step
                if left:
                    tile(whole * step, left, self.padded - whole * step)

            def go(self):
                pl.semaphore_wait(credit, 1)
                self.send(0, self.give.at[:, pl.ds(0, self.padded)], land0.at[:, pl.ds(0, self.padded)])

            def add(self, level):
                rows = half >> level
                base = 0
                for before in range(1, level + 1):
                    base = base + bit_of(self.order[before]) * (half >> before)
                self.copies[level].wait_recv()
                cut = pl.ds(0, self.padded)
                if level == 0:
                    source = land0
                elif level == 1:
                    source = land1[self.index]
                elif level == 2:
                    source = land2[self.index]
                if level < 2:
                    block = 48

                    def one(n, carry):
                        there = pl.ds(pl.multiple_of(n * block, 16), block)
                        here = pl.ds(pl.multiple_of(base + n * block, 16), block)
                        self.keep[here, self.lanes] = (
                            self.keep[here, self.lanes].astype(F32) + source[there, cut].astype(F32)
                        ).astype(BF16)
                        return carry

                    lax.fori_loop(0, rows // block, one, 0)
                    if level == 0:
                        pl.semaphore_signal(
                            credit, inc=1, device_id=partner(1), device_id_type=MESH
                        )
                    quarter = rows // 2
                    off = pl.multiple_of(base + (1 - bit_of(self.order[level + 1])) * quarter, 16)
                    target = (land1, land2)[level][self.index]
                    self.send(level + 1, self.keep.at[pl.ds(off, quarter), self.lanes], target)
                elif level == 2:
                    here = pl.ds(pl.multiple_of(base, 16), rows)
                    total = self.keep[here, self.lanes].astype(F32) + source[:, cut].astype(F32)
                    held3[self.index][0] = total[: rows // 2].astype(BF16)
                    held3[self.index][1] = total[rows // 2 :].astype(BF16)
                    bit = bit_of(self.order[3])
                    self.send(3, held3[self.index].at[1 - bit], land3[self.index].at[0])
                else:
                    bit = bit_of(self.order[3])
                    if state.get("final") is not None:
                        state["final"].wait()
                    final[:, cut] = held3[self.index][bit].astype(F32) + land3[self.index][
                        0
                    ].astype(F32)
                    copy = pltpu.make_async_copy(
                        final.at[:, cut], self.result.at[:, pl.ds(self.at, self.padded)], osem
                    )
                    copy.start()
                    state["final"] = copy

            def close(self):
                for copy in self.copies.values():
                    copy.wait_send()

        pl.semaphore_signal(credit, inc=1, device_id=partner(1), device_id_type=MESH)
        y_first, z_first = plan["orders"]
        low, high = wg.at[pl.ds(0, half)], wg.at[pl.ds(half, half)]
        third = [wqkv.at[pl.ds(n * half, half)] for n in range(3)]
        p_down = Piece("down", y_first, inner, inner, low, 0, results[0], 0)
        p_gate = Piece("gate", z_first, inner, inner, high, 0, results[0], inner)
        p_up = Piece("up", y_first, inner, inner, wu.at[pl.ds(0, half)], 0, results[0], 2 * inner)
        pad = -(-head_cols // 128) * 128
        rest = 3 * head_cols - 2 * pad
        rest_pad = -(-rest // 128) * 128
        small = [
            Piece(name, y_first, columns, padded, place, 0, results[0], 3 * inner + at)
            for name, columns, padded, place, at in (
                ("q", pad, pad, third[0], 0),
                ("k", pad, pad, third[1], pad),
                ("v", rest, rest_pad, third[2], 2 * pad),
                ("out", head_cols, pad, keep_out, 2 * pad + rest_pad),
            )
        ]
        p_q, p_k, p_v, p_out = small

        tail = Stream(
            (3, 4, 2, 5, 0, 1), [wdown.at[pl.ds(n * half, half)] for n in range(2)] + [wout]
        )
        devices = plan["devices"]
        side_count = plan["sides"]
        mine = me * side_count + side
        own_cols = plan["own_cols"]

        def condition_back(blocks):
            for block in blocks:
                row = jnp.sum(sums[block], axis=0, keepdims=True)
                dflat[0:1, block * width : (block + 1) * width] = row
                rows = jnp.broadcast_to(row, (16, width)).astype(BF16)
                for _ in range(2):
                    b, h, slot = tail.take()
                    dcond[h : h + 1, :] += dot(rows, slot[...], 1, 1)[0:1]
                    tail.fill(99)

        def share_out():
            lanes = lax.broadcasted_iota(jnp.int32, (16, 128), 0)
            base = jnp.zeros((16, 128), F32)
            silu_f = silu.astype(F32)
            for n in range(width // 128):
                base = jnp.where(lanes == n, silu_f[:, n * 128 : (n + 1) * 128], base)
            row_a = width // 128
            for n in range(devices):
                first = dflat[0:1, n * own_cols : n * own_cols + 128]
                rest = own_cols - 128
                second = dflat[0:1, n * own_cols + 128 : n * own_cols + 256]
                packet = jnp.where(lanes == row_a, first, base)
                packet = jnp.where(lanes == row_a + 1, second, packet)
                packs[n] = packet.astype(BF16)

            def one(n, carry):
                other = lax.rem(mine + n, devices)
                pltpu.make_async_remote_copy(
                    src_ref=packs.at[other], dst_ref=came.at[mine], send_sem=psem.at[0],
                    recv_sem=psem.at[1],
                    device_id={
                        "dp": lax.div(other, side_count), "tensor": lax.rem(other, side_count)
                    },
                    device_id_type=MESH,
                ).start()
                return carry

            lax.fori_loop(1, devices, one, 0)
            came[mine] = packs[mine]

        def take_in():
            every = pl.ds(0, devices - 1)
            whole = pltpu.make_async_remote_copy(
                src_ref=packs.at[every], dst_ref=came.at[every], send_sem=psem.at[0],
                recv_sem=psem.at[1], device_id=mate, device_id_type=MESH,
            )
            whole.wait_send()
            whole.wait_recv()
            seen = came[...].astype(F32)
            row_a = width // 128
            silu_all = jnp.concatenate([seen[:, n, :] for n in range(row_a)], axis=1).astype(BF16)
            columns = jnp.concatenate([seen[:, row_a, :], seen[:, row_a + 1, :]], axis=1)
            bias_out[...] = jnp.broadcast_to(jnp.sum(columns, axis=0, keepdims=True), bias_out.shape)
            own[...] = dot(columns.astype(BF16), silu_all, 0, 0)
            copy = pltpu.make_async_copy(own.at[pl.ds(0, own_cols)], ada_out, asem.at[0])
            copy.start()
            copy.wait()
            slope = cond_sig * (1.0 + cond_f * (1.0 - cond_sig))
            whole_row = jnp.concatenate([dcond[0:1, :], dcond[1:2, :]], axis=1)
            cond_out[...] = whole_row * slope

    def lane_right(array):
        def right(start, size):
            if not isinstance(start, int):
                start = pl.multiple_of(start, 128)
            part = [array[i, :, pl.ds(start, size)] for i in range(2)]
            return dot(flip[:, 0:LEN], part[0], 1, 0) + dot(flip[:, LEN:], part[1], 1, 0)
        return right

    def row_right(array, base):
        def right(start, size):
            at = base + start
            if not isinstance(start, int):
                at = pl.multiple_of(at, 16)
            part = [array[i, pl.ds(at, size), :] for i in range(2)]
            return dot(flip[:, 0:LEN], part[0], 1, 1) + dot(flip[:, LEN:], part[1], 1, 1)
        return right

    def plain_grad(right, columns, target):
        (stage, gsem) = extra
        pend = {}
        for n, start in enumerate(range(0, columns, TILE)):
            size = min(TILE, columns - start)
            slot = n % 2
            if slot in pend:
                pend[slot].wait()
            stage[slot, :, 0:size] = right(start, size).astype(BF16)
            copy = pltpu.make_async_copy(
                stage.at[slot], target.at[:, pl.ds(start, TILE)], gsem.at[slot]
            )
            copy.start()
            pend[slot] = copy
        for copy in pend.values():
            copy.wait()

    def plain_grad_in(left, right, columns, target):
        for image in range(2):
            flip[:, image * LEN : (image + 1) * LEN] = left[image].astype(F32).T.astype(BF16)
        plain_grad(right, columns, target)

    if plan["fused"]:
        p_down.compute(lane_right(hid), 0, 2)
        turned(h2, p_gate.order)
        p_down.add(0)
        p_gate.compute(lane_right(dgate), 1, 2)
        p_gate.add(0)
    else:
        plain_grad_in(dml, lane_right(hid), inner, results[0])
        plain_grad_in(h2, lane_right(dgate), inner, results[1])
        plain_grad_in(h2, lane_right(dup), inner, results[2])

    for copy in go_b:
        copy.wait_recv()

    def second_back(rows):
        grad = own[rows, :] + recv_a[rows, :].astype(F32)
        norm, inverse = normed(tok[rows, :].astype(F32) + gate_one * attn[rows, :])
        middle = cot[rows, :].astype(F32) + norm_back(grad * (1.0 + scale_two), norm, inverse)
        dx1[rows, :] = middle
        dat[0, rows, :] = (gate_one * middle).astype(BF16)
        sums[2] += fold(middle * attn[rows, :])
        sums[3] += fold(grad)
        sums[4] += fold(grad * norm)

    rows_loop(second_back, go_dat)

    strips_of(mlp_strip(1), send_c, go_c)
    if plan["fused"]:
        p_down.copies[0].wait_send()
        turned(h2, p_up.order)
        p_up.compute(lane_right(dup), 0, 2)

    def heads_back(image):
        a_f[...] = dot(wout[...], dat[image], 1, 1)
        cosine, sine = cos_t[image], sin_t[image]

        def head(h, carry):
            at = image * heads + h
            rows = pl.ds(pl.multiple_of(h * HD, 8), HD)
            da = a_f[rows, :].astype(BF16)
            probs = p_s[at]
            query, key, value = q_s[at], k_s[at], v_s[at]
            dprobs = dot(value, da, 0, 0)
            dvalue = dot(da, probs.astype(BF16), 1, 1)
            inside = jnp.sum(probs * dprobs, axis=0, keepdims=True)
            dscores = (probs * (dprobs - inside)).astype(BF16)
            dquery = dot(key, dscores, 1, 0)
            dkey = dot(query, dscores, 1, 1)
            dquery = (dquery * cosine - rotate_rows(dquery * sine)) * scale
            dkey = dkey * cosine - rotate_rows(dkey * sine)
            qkv_f[rows, :] = dquery
            qkv_f[pl.ds(pl.multiple_of(head_cols + h * HD, 8), HD), :] = dkey
            qkv_f[pl.ds(pl.multiple_of(2 * head_cols + h * HD, 8), HD), :] = dvalue
            return carry

        lax.fori_loop(0, heads, head, 0, unroll=4)
        dqkv[image] = qkv_f[...].astype(BF16)

    heads_back(0)
    if plan["fused"]:
        p_up.add(0)
        p_down.add(1)
    for copy in go_dat:
        copy.wait_recv()
    heads_back(1)

    def dh1_strip(image):
        return lambda cols: dot(dqkv[image], wqkv[:, cols], 0, 0)

    for copy in go_b:
        copy.wait_send()
    strips_of(dh1_strip(1), send_a, go_d)
    strips_of(dh1_strip(0), keep=own)

    if plan["fused"]:
        p_gate.copies[0].wait_send()
        p_up.copies[0].wait_send()
        p_gate.add(1)
        turned(dat, p_out.order)
        p_out.compute(row_right(a_t, 0), 0)
        p_out.go()
        turned(h1, p_q.order)
        p_q.compute(row_right(dqkv, 0), 1)
        p_out.add(0)
        p_q.go()
        p_out.copies[0].wait_send()
        p_k.compute(row_right(dqkv, pad), 0)
        p_q.add(0)
        p_k.go()
        p_down.add(2)
        p_q.copies[0].wait_send()
        p_v.compute(row_right(dqkv, 2 * pad), 1)
        p_k.add(0)
        p_v.go()
        p_up.add(1)
        p_v.add(0)
    else:
        plain_grad_in(h1, row_right(dqkv, 0), 3 * head_cols, results[3])
        plain_grad_in(dat, row_right(a_t, 0), head_cols, results[4])

    pieces = [(n, min(LEN, width - n)) for n in range(0, width, LEN)]
    for n, size in pieces:
        p_s[n // LEN, :, 0:size] = dot(hid[0], wdown[:, n : n + size], 1, 0)
    for copy in go_c:
        copy.wait_recv()

    def finish(rows):
        mine_part = [p_s[n // LEN, rows, 0:size] for n, size in pieces]
        branch = jnp.concatenate(mine_part, axis=1) + recv_c[rows, :].astype(F32)
        out[rows, :] = (
            tok[rows, :].astype(F32) + gate_one * attn[rows, :] + gate_two * branch
        ).astype(BF16)
        sums[5] += fold(cot[rows, :].astype(F32) * branch)

    rows_loop(finish)
    if plan["fused"]:
        tail.fill(99)
        condition_back((3, 4))
    for copy in go_d:
        copy.wait_recv()

    def first_back(rows):
        grad = own[rows, :] + recv_a[rows, :].astype(F32)
        norm, inverse = normed(tok[rows, :].astype(F32))
        dtok[rows, :] = dx1[rows, :] + norm_back(grad * (1.0 + scale_one), norm, inverse)
        sums[0] += fold(grad)
        sums[1] += fold(grad * norm)

    rows_loop(first_back)

    if plan["fused"]:
        p_gate.add(2)
        p_up.add(2)
        condition_back((2, 5))
        p_down.add(3)
        p_out.add(1)
        condition_back((0, 1))
        share_out()
        p_q.add(1)
        p_out.add(2)
        p_gate.add(3)
        p_up.add(3)
        p_k.add(1)
        p_q.add(2)
        p_out.add(3)
        p_v.add(1)
        p_k.add(2)
        p_q.add(3)
        take_in()
        p_v.add(2)
        p_k.add(3)
        p_v.add(3)
        state["final"].wait()
        pl.semaphore_wait(credit, 1)
        for piece in (p_gate, p_up, p_down, *small):
            for level, copy in piece.copies.items():
                if level > 0 or piece in (p_k, p_v):
                    copy.wait_send()
    else:
        for n in range(6):
            results[5][n : n + 1, :] = jnp.sum(sums[n], axis=0, keepdims=True)
    for copy in (*go_h1, *go_cot, go_row, *go_h2, *go_dat, *go_c, *go_d):
        copy.wait_send()


def lay_out_kernel(cuts, whole, ada, tok, out, bias, *refs):
    (down, gate_up, qkv, wout, ada_to, tok_to, out_to, bias_to) = refs
    inner, head_cols, pad, own_cols = cuts
    ada_to[...] = ada[...]
    tok_to[...] = tok[...]
    out_to[...] = out[...]
    down[...] = whole[:, 0:inner]
    gate_up[:, 0, :] = whole[:, inner : 2 * inner]
    gate_up[:, 1, :] = whole[:, 2 * inner : 3 * inner]
    flat = whole[:, 3 * inner : 3 * inner + 3 * head_cols]
    for n in range(3):
        qkv[n] = flat[:, n * head_cols : (n + 1) * head_cols]
    start = whole.shape[1] - pad
    wout[...] = whole[:, start : start + head_cols]
    bias_to[...] = bias[0:1, 0:own_cols]


def lay_out(whole, ada, tok, out, bias, inner, head_cols, own_cols):
    rows = whole.shape[0]
    vmem = pl.BlockSpec(memory_space=pltpu.VMEM)
    pad = -(-head_cols // 128) * 128
    S = jax.ShapeDtypeStruct
    return pl.pallas_call(
        functools.partial(lay_out_kernel, (inner, head_cols, pad, own_cols)),
        out_shape=(
            S((rows, inner), F32), S((rows, 2, inner), F32), S((3, rows, head_cols), F32),
            S((rows, head_cols), F32), S(ada.shape, F32), S(tok.shape, F32), S(out.shape, BF16),
            S((1, own_cols), F32),
        ),
        in_specs=[vmem] * 5,
        out_specs=[vmem] * 8,
        compiler_params=pltpu.CompilerParams(vmem_limit_bytes=62 * 1024 * 1024),
    )(whole, ada, tok, out, bias)


def run_block(tok, cot, cond, grid, bias, wada, wqkv, wout, wgu, wdown):
    width = tok.shape[1]
    head_cols = wout.shape[0]
    heads = head_cols // HD
    inner = wdown.shape[0]
    strips = width // STRIP
    count = lax.axis_size("dp")
    sides = lax.axis_size("tensor")
    devices = count * sides
    own_cols = 6 * width // devices
    vmem = pl.BlockSpec(memory_space=pltpu.VMEM)
    hbm = pl.BlockSpec(memory_space=pl.ANY)
    V = pltpu.VMEM
    D = pltpu.SemaphoreType.DMA
    copies = 10 + 4 * strips
    fused = count == 16 and width % (8 * count) == 0 and 128 < own_cols <= 256 and own_cols % 8 == 0
    names = ["down", "gate", "up", "q", "k", "v", "out"]
    pad = -(-head_cols // 128) * 128
    if fused:
        rest_pad = -(-(3 * head_cols - 2 * pad) // 128) * 128
        results = [
            jax.ShapeDtypeStruct((width // count, 3 * inner + 3 * pad + rest_pad), F32),
            jax.ShapeDtypeStruct((own_cols, width), F32),
            jax.ShapeDtypeStruct((1, width), F32),
            jax.ShapeDtypeStruct((8, 256), F32),
        ]
        result_specs = [hbm, hbm, vmem, vmem]
        chunk = width // count
        widths = [inner, inner, inner, pad, pad, rest_pad, pad]
        extra = [
            V((width // 2, inner), BF16),
            V((width // 2, pad), BF16),
            V((width // 2, inner), BF16),
            V((chunk, inner), F32),
            D((len(names), 5)),
            D((len(names), 5)),
            D(()),
            pltpu.SemaphoreType.REGULAR,
            V((devices, 16, 128), BF16),
            V((devices, 16, 128), BF16),
            V((8, 6 * width + 128), F32),
            V((8, width // 2), F32),
            D((2,)),
            *[V((width // 4, w), BF16) for w in widths],
            *[V((width // 8, w), BF16) for w in widths],
            *[V((1, chunk, w), BF16) for w in widths],
            *[V((2, chunk, w), BF16) for w in widths],
        ]
        strides = [1, 2, 4, 8]
    else:
        wide = [inner, inner, inner, 3 * head_cols, head_cols]
        results = [jax.ShapeDtypeStruct((width, -(-w // TILE) * TILE), BF16) for w in wide]
        results += [jax.ShapeDtypeStruct((6, width), F32)]
        result_specs = [hbm] * 5 + [vmem]
        extra = [V((2, width, TILE), BF16), D((2,))]
        strides = []
    plan = {
        "fused": fused, "results": len(results), "count": count, "pieces": names,
        "devices": devices, "sides": sides, "own_cols": own_cols,
        "early": 8, "strides": strides, "orders": ((1, 2, 4, 8), (1, 4, 2, 8)),
    }
    return pl.pallas_call(
        functools.partial(block_kernel, plan),
        out_shape=(
            jax.ShapeDtypeStruct((LEN, width), BF16),
            jax.ShapeDtypeStruct((LEN, width), F32),
            *results,
        ),
        in_specs=[vmem] * 3 + [pl.BlockSpec(memory_space=pltpu.SMEM), vmem] + [hbm] * 5,
        out_specs=[vmem] * 2 + result_specs,
        scratch_shapes=[
            V((8, width), F32), V((2, 16, width // 2), BF16), V((2, HD, LEN), F32),
            V((2, HD, LEN), F32), V((3, 48, 2, inner), BF16),
                        V(wqkv.shape, BF16), V(wout.shape, BF16), V((width, inner), BF16),
            V((width, inner), BF16), V(wdown.shape, BF16),
            *[V((2, LEN, width), BF16)] * 4,
            *[V((2 * heads, HD, LEN), BF16)] * 3,
            V((2 * heads, LEN, LEN), F32),
            V((3 * head_cols, LEN), F32),
            V((head_cols, LEN), F32),
            V((2, head_cols, LEN), BF16),
            *[V((2, LEN, inner), BF16)] * 3,
            V((2, 3 * head_cols, LEN), BF16),
            *[V((LEN, width), F32)] * 3,
            *[V((LEN, width), BF16)] * 4,
            *[V((8, width), F32)] * 2,
            V((width, 2 * LEN), BF16),
            V((6, 8, width), F32),
            D((6,)),
            D((8,)),
            D((copies,)),
            D((copies,)),
            *extra,
        ],
        compiler_params=pltpu.CompilerParams(
            collective_id=0, has_side_effects=True, vmem_limit_bytes=62 * 1024 * 1024
        ),
    )(tok, cot, cond, grid, bias, wada, wqkv, wout, wgu, wdown)


def sum_over_images(partial):
    count = lax.axis_size("dp")
    me = lax.axis_index("dp")
    held = partial.reshape(count, partial.shape[0] // count, partial.shape[1])
    stride = 1
    left = count
    while left > 1:
        bit = (me // stride) % 2
        pairs = held.reshape(left // 2, 2, *held.shape[1:])
        keep = lax.dynamic_index_in_dim(pairs, bit, 1, keepdims=False)
        send = lax.dynamic_index_in_dim(pairs, 1 - bit, 1, keepdims=False)
        came = lax.ppermute(send, "dp", [(i, i ^ stride) for i in range(count)])
        held = keep.astype(F32) + came.astype(F32)
        left //= 2
        stride *= 2
        if left > 1:
            held = held.astype(BF16)
    return held[0]


def body(tokens, condition, grid_shape, w_ada, b_ada, w_qkv, w_out, w_gate_up, w_down, cotangent):
    width = tokens.shape[1]
    inner = w_down.shape[0]
    head_cols = w_out.shape[0]
    wqkv = w_qkv.transpose(1, 2, 0).reshape(3 * head_cols, width)
    layer_out, d_tokens, *grads = run_block(
        tokens, cotangent, condition, grid_shape, b_ada.reshape(-1, 128), w_ada, wqkv, w_out,
        w_gate_up, w_down,
    )
    devices_all = lax.axis_size("dp") * lax.axis_size("tensor")
    own_cols = 6 * width // devices_all
    if len(grads) == 4:
        whole, ada, d_condition, bias_rows = grads
        down, gate_up, qkv, g_out, ada, d_tokens, layer_out, bias_part = lay_out(
            whole, ada, d_tokens, layer_out, bias_rows, inner, head_cols, own_cols
        )
        grad_down, grad_gate_up = down.T, gate_up
        grad_qkv, grad_out = qkv.transpose(1, 0, 2), g_out.T
        weight_part, bias_part = ada.T, bias_part.reshape(own_cols)
    else:
        grad_down = sum_over_images(grads[0]).T
        grad_gate_up = jnp.stack([sum_over_images(grads[1]), sum_over_images(grads[2])], axis=1)
        grad_qkv = sum_over_images(grads[3][:, : 3 * head_cols]).reshape(-1, 3, head_cols)
        grad_out = sum_over_images(grads[4][:, :head_cols]).T
        cond = condition.astype(F32)
        cond_sigmoid = jax.nn.sigmoid(cond)
        silu_cond = (cond * cond_sigmoid).astype(BF16)
        d_mod = grads[5].reshape(1, 6 * width).astype(BF16)
        d_condition = (
            dot(d_mod, w_ada, 1, 1) * cond_sigmoid * (1.0 + cond * (1.0 - cond_sigmoid))
        )
        packed = jnp.concatenate(
            [
                d_mod.reshape(devices_all, own_cols),
                jnp.broadcast_to(silu_cond, (devices_all, width)),
            ],
            axis=1,
        )
        packed = jnp.pad(packed, ((0, 0), (0, -packed.shape[1] % 128)))
        packed = lax.all_to_all(
            packed.reshape(devices_all, -1, 128), ("dp", "tensor"), 0, 0, tiled=True
        ).reshape(devices_all, -1)
        columns = packed[:, :own_cols]
        silu_rows = packed[:, own_cols : own_cols + width]
        weight_part = dot(silu_rows, columns, 0, 0)
        bias_part = jnp.sum(columns.astype(F32), axis=0)
    return (
        layer_out, d_tokens, d_condition, weight_part, bias_part,
        grad_qkv, grad_out, grad_gate_up, grad_down,
    )


def solution(mesh):
    placed = (
        P(("dp", "tensor"), None),
        P(("dp", "tensor"), None),
        P("dp", None),
        P(),
        P(),
        P(None, None, "tensor"),
        P("tensor", None),
        P(None, None, "tensor"),
        P("tensor", None),
        P(("dp", "tensor"), None),
    )
    return jax.shard_map(
        body,
        mesh=mesh,
        in_specs=placed,
        out_specs=(
            P(("dp", "tensor"), None),
            P(("dp", "tensor"), None),
            P(("dp", "tensor"), None),
            P(None, ("dp", "tensor")),
            P(("dp", "tensor")),
            P("dp", None, "tensor"),
            P("tensor", "dp"),
            P("dp", None, "tensor"),
            P("tensor", "dp"),
        ),
        check_vma=False,
    )
```

```python
import functools

import jax
import jax.numpy as jnp
from jax import lax
from jax.experimental import pallas as pl
from jax.experimental.pallas import tpu as pltpu
from jax.sharding import PartitionSpec as P

HD = 72
LEN = 256
EPSILON = 1e-06
MESH = pl.DeviceIdType.MESH
F32 = jnp.float32
BF16 = jnp.bfloat16
ROWS = 32
STRIP = 384
TILE = 256


def dot(left, right, left_dim, right_dim):
    return lax.dot_general(
        left, right, (((left_dim,), (right_dim,)), ((), ())), preferred_element_type=F32
    )


def normed(values):
    centered = values - jnp.mean(values, axis=-1, keepdims=True)
    variance = jnp.mean(centered * centered, axis=-1, keepdims=True)
    inverse = lax.rsqrt(variance + EPSILON)
    return centered * inverse, inverse


def norm_back(upstream, norm, inverse):
    mean_grad = jnp.mean(upstream, axis=-1, keepdims=True)
    mean_cross = jnp.mean(upstream * norm, axis=-1, keepdims=True)
    return inverse * (upstream - mean_grad - norm * mean_cross)


def rotate_rows(values):
    quarter = HD // 4
    a, b = values[:quarter], values[quarter : 2 * quarter]
    c, d = values[2 * quarter : 3 * quarter], values[3 * quarter :]
    return jnp.concatenate([-b, a, -d, c], axis=0)


def fold(values):
    return jnp.sum(values.reshape(values.shape[0] // 8, 8, values.shape[1]), axis=0)


class Several:
    def __init__(self, copies):
        self.copies = copies

    def wait_send(self):
        for copy in self.copies:
            copy.wait_send()

    def wait_recv(self):
        for copy in self.copies:
            copy.wait_recv()


def block_kernel(
    plan, tok, cot, cond, grid, bias,
    wada_hbm, wqkv_hbm, wout_hbm, wgu_hbm, wdown_hbm,
    out, dtok, *rest,
):
    results, rest = rest[: plan["results"]], rest[plan["results"] :]
    (
        mod, silu_two, cos_t, sin_t, raw,
        wqkv, wout, wg, wu, wdown,
        h1, h2, dml, dat,
        q_s, k_s, v_s, p_s, qkv_f, a_f, a_t,
        hid, dgate, dup, dqkv,
        attn, dx1, own,
        send_a, send_c, recv_a, recv_c, row_out, row_in,
        flip, sums,
        wsem, asem, ssem, rsem, *extra,
    ) = rest
    width = tok.shape[1]
    heads = q_s.shape[0] // 2
    head_cols = heads * HD
    inner = wdown.shape[0]
    side = lax.axis_index("tensor")
    mate = {"tensor": 1 - side}
    scale = HD ** (-0.5)

    loads = [
        pltpu.make_async_copy(src, dst, wsem.at[i])
        for i, (src, dst) in enumerate(
            ((wqkv_hbm, wqkv), (wout_hbm, wout), (wdown_hbm, wdown))
        )
    ]
    half_rows = width // 2
    slots = [
        ref.at[pl.ds(n * half_rows, half_rows), pl.ds(0, width)] for ref in (wg, wu) for n in range(2)
    ]

    class Stream:
        def __init__(self, blocks, slots):
            self.chunks = [(b, h) for b in blocks for h in range(2)]
            self.slots = slots
            self.copies = []
            self.at = 0

        def fill(self, most):
            while len(self.copies) < min(most, len(self.chunks), self.at + len(self.slots)):
                n = len(self.copies)
                b, h = self.chunks[n]
                copy = pltpu.make_async_copy(
                    wada_hbm.at[pl.ds(h * half_rows, half_rows), pl.ds(b * width, width)],
                    self.slots[n % len(self.slots)], asem.at[n % len(self.slots)],
                )
                copy.start()
                self.copies.append(copy)

        def take(self):
            n = self.at
            self.copies[n].wait()
            b, h = self.chunks[n]
            self.at += 1
            return b, h, self.slots[n % len(self.slots)]

    stream = Stream((0, 1, 5, 2, 3, 4), slots)
    stream.fill(4)

    me = lax.axis_index("dp")

    def bit_of(stride):
        return lax.rem(lax.div(me, stride), 2)

    def partner(stride):
        return {"dp": me + stride - 2 * stride * bit_of(stride)}

    barrier = pltpu.get_barrier_semaphore()
    friends = [mate] + [partner(s) for s in plan["strides"]]
    for friend in friends:
        pl.semaphore_signal(barrier, inc=1, device_id=friend, device_id_type=MESH)

    def give(src, dst, slot):
        return pltpu.make_async_remote_copy(
            src_ref=src, dst_ref=dst, send_sem=ssem.at[slot], recv_sem=rsem.at[slot],
            device_id=mate, device_id_type=MESH,
        )

    def gather(buf, slot):
        half = LEN // 2
        return [
            give(buf.at[0, pl.ds(c * half, half)], buf.at[1, pl.ds(c * half, half)], slot + c)
            for c in range(2)
        ]

    strips = width // STRIP

    def scatter(send, recv, slot):
        return [
            give(
                send.at[:, pl.ds(c * STRIP, STRIP)], recv.at[:, pl.ds(c * STRIP, STRIP)], slot + c
            )
            for c in range(strips)
        ]

    go_h1, go_h2, go_dat = (gather(b, 2 * i) for i, b in enumerate((h1, h2, dat)))
    go_cot = [
        give(cot.at[pl.ds(at, size)], dml.at[1, pl.ds(at, size)], slot)
        for at, size, slot in ((0, 96, 6), (96, 96, 7), (192, 64, 9 + 4 * (width // STRIP)))
    ]
    go_row = give(row_out, row_in, 8 + 4 * (width // STRIP))
    go_a, go_b, go_c, go_d = (
        scatter(s, r, 8 + strips * i)
        for i, (s, r) in enumerate(
            ((send_a, recv_a), (send_a, recv_a), (send_c, recv_c), (send_a, recv_a))
        )
    )

    def rows_loop(step, copies=None):
        half = LEN // 2
        count = half // ROWS
        for c in range(2):
            def one(i, carry, c=c):
                step(pl.ds(pl.multiple_of(c * half + i * ROWS, ROWS), ROWS))
                return carry
            lax.fori_loop(0, count, one, 0)
            if copies is not None:
                copies[c].start()

    cond_f = cond[...].astype(F32)
    cond_sig = jax.nn.sigmoid(cond_f)
    silu = (cond_f * cond_sig).astype(BF16)
    silu_rows = jnp.broadcast_to(silu.astype(F32), (16, width))
    for h in range(2):
        silu_two[h] = silu_rows[:, h * half_rows : (h + 1) * half_rows].astype(BF16)

    bias_f = bias[...].astype(F32)
    tiles = width // bias.shape[1]

    def bias_row(b):
        return jnp.concatenate([bias_f[b * tiles + n : b * tiles + n + 1] for n in range(tiles)], axis=1)

    def modulate(count):
        for _ in range(count):
            row = None
            for _ in range(2):
                b, h, slot = stream.take()
                part = dot(silu_two[h], slot[...], 1, 0)[0:1]
                row = part if row is None else row + part
                stream.fill(99)
            mod[b : b + 1, :] = row + bias_row(b)

    def pre_norm(rows):
        norm, _ = normed(tok[rows, :].astype(F32))
        dx1[rows, :] = norm

    rows_loop(pre_norm)
    pl.semaphore_wait(barrier, len(friends))
    go_cot[0].start()
    modulate(2)
    for load in loads:
        load.start()
    shift_one, scale_one = mod[0:1], mod[1:2]

    def first_norm(rows):
        h1[0, rows, :] = (dx1[rows, :] * (1.0 + scale_one) + shift_one).astype(BF16)

    rows_loop(first_norm, go_h1)
    modulate(1)
    gate_two = mod[5:6]
    row_out[...] = jnp.broadcast_to(gate_two, row_out.shape)
    go_row.start()
    go_cot[1].start()
    sums[...] = jnp.zeros_like(sums)

    quarter = HD // 4
    limits = []
    for image in range(2):
        at = side if image == 0 else 1 - side
        tall, wide = grid[at, 0], grid[at, 1]
        limits.append(tall * wide)
        spot = lax.broadcasted_iota(jnp.int32, (1, LEN), 1).astype(F32)
        wide_f = jnp.full((1, LEN), wide, jnp.int32).astype(F32)
        row_at = jnp.floor((spot + 0.5) / wide_f)
        col_at = spot - row_at * wide_f
        step = lax.broadcasted_iota(jnp.int32, (quarter, LEN), 0).astype(F32)
        frequency = jnp.exp(step * (-9.210340371976184 / quarter))
        both = jnp.concatenate([row_at * frequency, col_at * frequency], axis=0)
        for table, turn in ((cos_t, jnp.cos), (sin_t, jnp.sin)):
            seen = turn(both)
            first, second = seen[:quarter], seen[quarter:]
            table[image] = jnp.concatenate([first, first, second, second], axis=0)

    depth = raw.shape[1]
    ring = raw.shape[0]
    parts = {"next": 0, "copies": []}
    r = lax.broadcasted_iota(jnp.int32, (2 * depth, 2 * depth), 0)
    c = lax.broadcasted_iota(jnp.int32, (2 * depth, 2 * depth), 1)
    sorter = jnp.where(c == jnp.where(r < depth, 2 * r, 2 * (r - depth) + 1), 1.0, 0.0).astype(BF16)

    def fetch(n):
        if n < width // depth:
            copy = pltpu.make_async_copy(
                wgu_hbm.at[pl.ds(n * depth, depth)], raw.at[n % ring], wsem.at[3 + n % ring]
            )
            copy.start()
            parts["copies"].append(copy)

    def pull_apart(until):
        while parts["next"] < until:
            n = parts["next"]
            parts["copies"][n].wait()
            parted = dot(sorter, raw[n % ring].reshape(2 * depth, inner), 1, 0).astype(BF16)
            wg[n * depth : (n + 1) * depth, :] = parted[:depth]
            wu[n * depth : (n + 1) * depth, :] = parted[depth:]
            fetch(n + ring)
            parts["next"] += 1

    def heads_forward(image):
        for part in range(3):
            qkv_f[part * head_cols : (part + 1) * head_cols, :] = dot(
                wqkv[part * head_cols : (part + 1) * head_cols, :], h1[image], 1, 1
            )
        cosine, sine = cos_t[image], sin_t[image]
        ok = lax.broadcasted_iota(jnp.int32, (LEN, LEN), 0) < limits[image]

        def head(h, carry):
            at = image * heads + h
            rows = pl.ds(pl.multiple_of(h * HD, 8), HD)
            query = qkv_f[rows, :]
            key = qkv_f[pl.ds(pl.multiple_of(head_cols + h * HD, 8), HD), :]
            value = qkv_f[pl.ds(pl.multiple_of(2 * head_cols + h * HD, 8), HD), :].astype(BF16)
            query = ((query * cosine + rotate_rows(query) * sine) * scale).astype(BF16)
            key = (key * cosine + rotate_rows(key) * sine).astype(BF16)
            q_s[at], k_s[at], v_s[at] = query, key, value
            scores = dot(key, query, 0, 0)
            scores = jnp.where(ok, scores, -1e30)
            top = jnp.max(scores, axis=0, keepdims=True)
            exps = jnp.exp(scores - top)
            probs = exps * (1.0 / jnp.sum(exps, axis=0, keepdims=True))
            p_s[at] = probs
            a_f[rows, :] = dot(value, probs.astype(BF16), 1, 0)
            return carry

        lax.fori_loop(0, heads, head, 0, unroll=4)
        a_t[image] = a_f[...].astype(BF16)

    def strips_of(make, send=None, copies=None, keep=None):
        for c in range(strips):
            cols = slice(c * STRIP, (c + 1) * STRIP)
            value = make(cols)
            if send is not None:
                send[:, cols] = value.astype(BF16)
                copies[c].start()
            else:
                keep[:, cols] = value

    for n in range(ring):
        fetch(n)
    loads[0].wait()
    heads_forward(0)
    modulate(3)
    pull_apart(plan["early"])
    gate_one, shift_two, scale_two = mod[2:3], mod[3:4], mod[4:5]
    for copy in go_h1:
        copy.wait_recv()
    heads_forward(1)
    loads[1].wait()
    strips_of(lambda cols: dot(a_t[1], wout[:, cols], 0, 0), send_a, go_a)
    go_cot[2].start()
    strips_of(lambda cols: dot(a_t[0], wout[:, cols], 0, 0), keep=own)

    gate_two_row = gate_two

    def mlp_grad(rows):
        dml[0, rows, :] = (gate_two_row * cot[rows, :].astype(F32)).astype(BF16)

    rows_loop(mlp_grad)
    pull_apart(width // depth)
    for copy in go_a:
        copy.wait_recv()

    def second_norm(rows):
        branch = own[rows, :] + recv_a[rows, :].astype(F32)
        attn[rows, :] = branch
        middle = tok[rows, :].astype(F32) + gate_one * branch
        norm, _ = normed(middle)
        h2[0, rows, :] = (norm * (1.0 + scale_two) + shift_two).astype(BF16)

    rows_loop(second_norm, go_h2)

    def turned(left, order):
        for image in range(2):
            flat = left[image].astype(F32).T
            chunk = width // plan["count"]
            for pair in range(plan["count"] // 2):
                place = [2 * pair, 2 * pair + 1]
                parts = []
                for spot in place:
                    which = 0
                    for level, stride in enumerate(order):
                        which += stride * ((spot >> (len(order) - 1 - level)) & 1)
                    parts.append(flat[which * chunk : (which + 1) * chunk])
                flip[2 * pair * chunk : 2 * (pair + 1) * chunk, image * LEN : (image + 1) * LEN] = (
                    jnp.concatenate(parts, axis=0).astype(BF16)
                )

    loads[2].wait()

    def feed_forward(image):
        def tile(j, carry):
            cols = pl.ds(pl.multiple_of(j * TILE, TILE), TILE)
            gate = dot(h2[image], wg[:, cols], 1, 0)
            up = dot(h2[image], wu[:, cols], 1, 0)
            grad = dot(dml[image], wdown[cols, :], 1, 1)
            sig = jax.nn.sigmoid(gate)
            act = gate * sig
            hid[image, :, cols] = (act * up).astype(BF16)
            dgate[image, :, cols] = (grad * up * sig * (1.0 + gate * (1.0 - sig))).astype(BF16)
            dup[image, :, cols] = (grad * act).astype(BF16)
            return carry

        lax.fori_loop(0, inner // TILE, tile, 0)

    def dh2_strip(image):
        return lambda cols: dot(dgate[image], wg[cols, :], 1, 1) + dot(dup[image], wu[cols, :], 1, 1)

    feed_forward(0)
    strips_of(dh2_strip(0), keep=own)
    for copy in go_cot:
        copy.wait_recv()
    go_row.wait_recv()
    gate_mate = row_in[0:1]

    def mate_grad(rows):
        dml[1, rows, :] = (gate_mate * dml[1, rows, :].astype(F32)).astype(BF16)

    rows_loop(mate_grad)
    if plan["fused"]:
        turned(dml, plan["orders"][0])
    for copy in go_h2:
        copy.wait_recv()
    feed_forward(1)

    def mlp_strip(image):
        return lambda cols: dot(hid[image], wdown[:, cols], 1, 0)

    for copy in go_a:
        copy.wait_send()
    strips_of(dh2_strip(1), send_a, go_b)

    if plan["fused"]:
        (
            give_one, keep_out, land0, final, gsend, grecv, osem, credit, packs, came, dflat, dcond, psem,
            *spots,
        ) = extra
        _, ada_out, cond_out, bias_out = results
        dflat[...] = jnp.zeros_like(dflat)
        dcond[...] = jnp.zeros_like(dcond)
        many = len(plan["pieces"])
        land1, land2, land3, held3 = (spots[n * many : (n + 1) * many] for n in range(4))
        half = width // 2
        gives = [wu.at[pl.ds(half, half)], give_one]
        core_bit = bit_of(1)
        state = {"gives": 0, "lands": 0}

        class Piece:
            def __init__(self, name, order, columns, padded, keep, offset, result, at):
                self.name, self.order, self.columns, self.padded = name, order, columns, padded
                self.keep, self.offset, self.result, self.at = keep, offset, result, at
                self.index = plan["pieces"].index(name)
                self.lanes = pl.ds(offset, padded)
                self.copies = {}

            def send(self, level, src, dst):
                copy = pltpu.make_async_remote_copy(
                    src_ref=src, dst_ref=dst, send_sem=gsend.at[self.index, level],
                    recv_sem=grecv.at[self.index, level], device_id=partner(self.order[level]),
                    device_id_type=MESH,
                )
                copy.start()
                self.copies[level] = copy

            def compute(self, right, give, cuts=0):
                self.give = gives[give]
                step = STRIP

                def tile(start, size, pad):
                    total = right(start, size)
                    low, high = total[:half], total[half:]
                    kept = jnp.where(core_bit == 0, low, high).astype(BF16)
                    gone = jnp.where(core_bit == 0, high, low).astype(BF16)
                    place = self.offset + start
                    if pad > size:
                        blank = jnp.zeros((half, pad - size), BF16)
                        kept = jnp.concatenate([kept, blank], axis=1)
                        gone = jnp.concatenate([gone, blank], axis=1)
                    if not isinstance(start, int):
                        place = pl.multiple_of(place, 128)
                        start = pl.multiple_of(start, 128)
                    self.keep[:, pl.ds(place, pad)] = kept
                    self.give[:, pl.ds(start, pad)] = gone

                whole = self.columns // step

                def one(n, carry):
                    tile(n * step, step, step)
                    return carry

                if cuts:
                    copies = []
                    for n in range(cuts):
                        part = whole // cuts
                        lax.fori_loop(n * part, (n + 1) * part, one, 0)
                        if n == 0:
                            pl.semaphore_wait(credit, 1)
                        lanes = pl.ds(n * part * step, part * step)
                        copy = pltpu.make_async_remote_copy(
                            src_ref=self.give.at[:, lanes], dst_ref=land0.at[:, lanes],
                            send_sem=gsend.at[self.index, 4 * n], recv_sem=grecv.at[self.index, 4 * n],
                            device_id=partner(1), device_id_type=MESH,
                        )
                        copy.start()
                        copies.append(copy)
                    self.copies[0] = Several(copies)
                    return
                lax.fori_loop(0, whole, one, 0)
                left = self.columns - whole * step
                if left:
                    tile(whole * step, left, self.padded - whole * step)

            def go(self):
                pl.semaphore_wait(credit, 1)
                self.send(0, self.give.at[:, pl.ds(0, self.padded)], land0.at[:, pl.ds(0, self.padded)])

            def add(self, level):
                rows = half >> level
                base = 0
                for before in range(1, level + 1):
                    base = base + bit_of(self.order[before]) * (half >> before)
                self.copies[level].wait_recv()
                cut = pl.ds(0, self.padded)
                if level == 0:
                    source = land0
                elif level == 1:
                    source = land1[self.index]
                elif level == 2:
                    source = land2[self.index]
                if level < 2:
                    block = 48

                    def one(n, carry):
                        there = pl.ds(pl.multiple_of(n * block, 16), block)
                        here = pl.ds(pl.multiple_of(base + n * block, 16), block)
                        self.keep[here, self.lanes] = (
                            self.keep[here, self.lanes].astype(F32) + source[there, cut].astype(F32)
                        ).astype(BF16)
                        return carry

                    lax.fori_loop(0, rows // block, one, 0)
                    if level == 0:
                        pl.semaphore_signal(
                            credit, inc=1, device_id=partner(1), device_id_type=MESH
                        )
                    quarter = rows // 2
                    off = pl.multiple_of(base + (1 - bit_of(self.order[level + 1])) * quarter, 16)
                    target = (land1, land2)[level][self.index]
                    self.send(level + 1, self.keep.at[pl.ds(off, quarter), self.lanes], target)
                elif level == 2:
                    here = pl.ds(pl.multiple_of(base, 16), rows)
                    total = self.keep[here, self.lanes].astype(F32) + source[:, cut].astype(F32)
                    held3[self.index][0] = total[: rows // 2].astype(BF16)
                    held3[self.index][1] = total[rows // 2 :].astype(BF16)
                    bit = bit_of(self.order[3])
                    self.send(3, held3[self.index].at[1 - bit], land3[self.index].at[0])
                else:
                    bit = bit_of(self.order[3])
                    if state.get("final") is not None:
                        state["final"].wait()
                    final[:, cut] = held3[self.index][bit].astype(F32) + land3[self.index][
                        0
                    ].astype(F32)
                    copy = pltpu.make_async_copy(
                        final.at[:, cut], self.result.at[:, pl.ds(self.at, self.padded)], osem
                    )
                    copy.start()
                    state["final"] = copy

            def close(self):
                for copy in self.copies.values():
                    copy.wait_send()

        pl.semaphore_signal(credit, inc=1, device_id=partner(1), device_id_type=MESH)
        y_first, z_first = plan["orders"]
        low, high = wg.at[pl.ds(0, half)], wg.at[pl.ds(half, half)]
        third = [wqkv.at[pl.ds(n * half, half)] for n in range(3)]
        p_down = Piece("down", y_first, inner, inner, low, 0, results[0], 0)
        p_gate = Piece("gate", z_first, inner, inner, high, 0, results[0], inner)
        p_up = Piece("up", y_first, inner, inner, wu.at[pl.ds(0, half)], 0, results[0], 2 * inner)
        pad = -(-head_cols // 128) * 128
        more = pad + 128
        rest = 3 * head_cols - more - pad
        rest_pad = -(-rest // 128) * 128
        small = [
            Piece(name, y_first, columns, padded, place, 0, results[0], 3 * inner + at)
            for name, columns, padded, place, at in (
                ("q", more, more, third[0], 0),
                ("k", pad, pad, third[1], more),
                ("v", rest, rest_pad, third[2], more + pad),
                ("out", head_cols, pad, keep_out, more + pad + rest_pad),
            )
        ]
        p_q, p_k, p_v, p_out = small

        tail = Stream(
            (3, 4, 2, 5, 0, 1), [wdown.at[pl.ds(n * half, half)] for n in range(2)] + [wout]
        )
        devices = plan["devices"]
        side_count = plan["sides"]
        mine = me * side_count + side
        own_cols = plan["own_cols"]

        def condition_back(blocks):
            for block in blocks:
                row = jnp.sum(sums[block], axis=0, keepdims=True)
                dflat[0:1, block * width : (block + 1) * width] = row
                rows = jnp.broadcast_to(row, (16, width)).astype(BF16)
                for _ in range(2):
                    b, h, slot = tail.take()
                    dcond[h : h + 1, :] += dot(rows, slot[...], 1, 1)[0:1]
                    tail.fill(99)

        def share_out():
            lanes = lax.broadcasted_iota(jnp.int32, (16, 128), 0)
            base = jnp.zeros((16, 128), F32)
            silu_f = silu.astype(F32)
            for n in range(width // 128):
                base = jnp.where(lanes == n, silu_f[:, n * 128 : (n + 1) * 128], base)
            row_a = width // 128
            for n in range(devices):
                first = dflat[0:1, n * own_cols : n * own_cols + 128]
                rest = own_cols - 128
                second = dflat[0:1, n * own_cols + 128 : n * own_cols + 256]
                packet = jnp.where(lanes == row_a, first, base)
                packet = jnp.where(lanes == row_a + 1, second, packet)
                packs[n] = packet.astype(BF16)

            def one(n, carry):
                other = lax.rem(mine + n, devices)
                pltpu.make_async_remote_copy(
                    src_ref=packs.at[other], dst_ref=came.at[mine], send_sem=psem.at[0],
                    recv_sem=psem.at[1],
                    device_id={
                        "dp": lax.div(other, side_count), "tensor": lax.rem(other, side_count)
                    },
                    device_id_type=MESH,
                ).start()
                return carry

            lax.fori_loop(1, devices, one, 0)
            came[mine] = packs[mine]

        def take_in():
            every = pl.ds(0, devices - 1)
            whole = pltpu.make_async_remote_copy(
                src_ref=packs.at[every], dst_ref=came.at[every], send_sem=psem.at[0],
                recv_sem=psem.at[1], device_id=mate, device_id_type=MESH,
            )
            whole.wait_send()
            whole.wait_recv()
            seen = came[...].astype(F32)
            row_a = width // 128
            silu_all = jnp.concatenate([seen[:, n, :] for n in range(row_a)], axis=1).astype(BF16)
            columns = jnp.concatenate([seen[:, row_a, :], seen[:, row_a + 1, :]], axis=1)
            bias_out[...] = jnp.broadcast_to(jnp.sum(columns, axis=0, keepdims=True), bias_out.shape)
            own[...] = dot(columns.astype(BF16), silu_all, 0, 0)
            copy = pltpu.make_async_copy(own.at[pl.ds(0, own_cols)], ada_out, asem.at[0])
            copy.start()
            copy.wait()
            slope = cond_sig * (1.0 + cond_f * (1.0 - cond_sig))
            whole_row = jnp.concatenate([dcond[0:1, :], dcond[1:2, :]], axis=1)
            cond_out[...] = whole_row * slope

    def lane_right(array):
        def right(start, size):
            if not isinstance(start, int):
                start = pl.multiple_of(start, 128)
            part = [array[i, :, pl.ds(start, size)] for i in range(2)]
            return dot(flip[:, 0:LEN], part[0], 1, 0) + dot(flip[:, LEN:], part[1], 1, 0)
        return right

    def row_right(array, base):
        def right(start, size):
            at = base + start
            if not isinstance(start, int):
                at = pl.multiple_of(at, 16)
            part = [array[i, pl.ds(at, size), :] for i in range(2)]
            return dot(flip[:, 0:LEN], part[0], 1, 1) + dot(flip[:, LEN:], part[1], 1, 1)
        return right

    def plain_grad(right, columns, target):
        (stage, gsem) = extra
        pend = {}
        for n, start in enumerate(range(0, columns, TILE)):
            size = min(TILE, columns - start)
            slot = n % 2
            if slot in pend:
                pend[slot].wait()
            stage[slot, :, 0:size] = right(start, size).astype(BF16)
            copy = pltpu.make_async_copy(
                stage.at[slot], target.at[:, pl.ds(start, TILE)], gsem.at[slot]
            )
            copy.start()
            pend[slot] = copy
        for copy in pend.values():
            copy.wait()

    def plain_grad_in(left, right, columns, target):
        for image in range(2):
            flip[:, image * LEN : (image + 1) * LEN] = left[image].astype(F32).T.astype(BF16)
        plain_grad(right, columns, target)

    if plan["fused"]:
        p_down.compute(lane_right(hid), 0, 2)
        turned(h2, p_gate.order)
        p_down.add(0)
        p_gate.compute(lane_right(dgate), 1, 2)
        p_gate.add(0)
    else:
        plain_grad_in(dml, lane_right(hid), inner, results[0])
        plain_grad_in(h2, lane_right(dgate), inner, results[1])
        plain_grad_in(h2, lane_right(dup), inner, results[2])

    for copy in go_b:
        copy.wait_recv()

    def second_back(rows):
        grad = own[rows, :] + recv_a[rows, :].astype(F32)
        norm, inverse = normed(tok[rows, :].astype(F32) + gate_one * attn[rows, :])
        middle = cot[rows, :].astype(F32) + norm_back(grad * (1.0 + scale_two), norm, inverse)
        dx1[rows, :] = middle
        dat[0, rows, :] = (gate_one * middle).astype(BF16)
        sums[2] += fold(middle * attn[rows, :])
        sums[3] += fold(grad)
        sums[4] += fold(grad * norm)

    rows_loop(second_back, go_dat)

    strips_of(mlp_strip(1), send_c, go_c)
    if plan["fused"]:
        p_down.copies[0].wait_send()
        turned(h2, p_up.order)
        p_up.compute(lane_right(dup), 0, 2)

    def heads_back(image):
        a_f[...] = dot(wout[...], dat[image], 1, 1)
        cosine, sine = cos_t[image], sin_t[image]

        def head(h, carry):
            at = image * heads + h
            rows = pl.ds(pl.multiple_of(h * HD, 8), HD)
            da = a_f[rows, :].astype(BF16)
            probs = p_s[at]
            query, key, value = q_s[at], k_s[at], v_s[at]
            dprobs = dot(value, da, 0, 0)
            dvalue = dot(da, probs.astype(BF16), 1, 1)
            inside = jnp.sum(probs * dprobs, axis=0, keepdims=True)
            dscores = (probs * (dprobs - inside)).astype(BF16)
            dquery = dot(key, dscores, 1, 0)
            dkey = dot(query, dscores, 1, 1)
            dquery = (dquery * cosine - rotate_rows(dquery * sine)) * scale
            dkey = dkey * cosine - rotate_rows(dkey * sine)
            qkv_f[rows, :] = dquery
            qkv_f[pl.ds(pl.multiple_of(head_cols + h * HD, 8), HD), :] = dkey
            qkv_f[pl.ds(pl.multiple_of(2 * head_cols + h * HD, 8), HD), :] = dvalue
            return carry

        lax.fori_loop(0, heads, head, 0, unroll=4)
        dqkv[image] = qkv_f[...].astype(BF16)

    heads_back(0)
    if plan["fused"]:
        p_up.add(0)
        p_down.add(1)
    for copy in go_dat:
        copy.wait_recv()
    heads_back(1)

    def dh1_strip(image):
        return lambda cols: dot(dqkv[image], wqkv[:, cols], 0, 0)

    for copy in go_b:
        copy.wait_send()
    strips_of(dh1_strip(1), send_a, go_d)
    strips_of(dh1_strip(0), keep=own)

    if plan["fused"]:
        p_gate.copies[0].wait_send()
        p_up.copies[0].wait_send()
        p_gate.add(1)
        turned(dat, p_out.order)
        p_out.compute(row_right(a_t, 0), 0)
        p_out.go()
        turned(h1, p_q.order)
        p_q.compute(row_right(dqkv, 0), 1)
        p_out.add(0)
        p_q.go()
        p_out.copies[0].wait_send()
        p_k.compute(row_right(dqkv, pad + 128), 0)
        p_q.add(0)
        p_k.go()
        p_down.add(2)
        p_q.copies[0].wait_send()
        p_v.compute(row_right(dqkv, 2 * pad + 128), 1)
        p_k.add(0)
        p_v.go()
        p_up.add(1)
        p_v.add(0)
    else:
        plain_grad_in(h1, row_right(dqkv, 0), 3 * head_cols, results[3])
        plain_grad_in(dat, row_right(a_t, 0), head_cols, results[4])

    pieces = [(n, min(LEN, width - n)) for n in range(0, width, LEN)]
    for n, size in pieces:
        p_s[n // LEN, :, 0:size] = dot(hid[0], wdown[:, n : n + size], 1, 0)
    for copy in go_c:
        copy.wait_recv()

    def finish(rows):
        mine_part = [p_s[n // LEN, rows, 0:size] for n, size in pieces]
        branch = jnp.concatenate(mine_part, axis=1) + recv_c[rows, :].astype(F32)
        out[rows, :] = (
            tok[rows, :].astype(F32) + gate_one * attn[rows, :] + gate_two * branch
        ).astype(BF16)
        sums[5] += fold(cot[rows, :].astype(F32) * branch)

    rows_loop(finish)
    if plan["fused"]:
        tail.fill(99)
        condition_back((3, 4))
    for copy in go_d:
        copy.wait_recv()

    def first_back(rows):
        grad = own[rows, :] + recv_a[rows, :].astype(F32)
        norm, inverse = normed(tok[rows, :].astype(F32))
        dtok[rows, :] = dx1[rows, :] + norm_back(grad * (1.0 + scale_one), norm, inverse)
        sums[0] += fold(grad)
        sums[1] += fold(grad * norm)

    rows_loop(first_back)

    if plan["fused"]:
        p_gate.add(2)
        p_up.add(2)
        condition_back((2, 5))
        p_down.add(3)
        p_out.add(1)
        condition_back((0, 1))
        share_out()
        p_q.add(1)
        p_out.add(2)
        p_gate.add(3)
        p_up.add(3)
        p_k.add(1)
        p_q.add(2)
        p_out.add(3)
        p_v.add(1)
        p_k.add(2)
        p_q.add(3)
        take_in()
        p_v.add(2)
        p_k.add(3)
        p_v.add(3)
        state["final"].wait()
        pl.semaphore_wait(credit, 1)
        for piece in (p_gate, p_up, p_down, *small):
            for level, copy in piece.copies.items():
                if level > 0 or piece in (p_k, p_v):
                    copy.wait_send()
    else:
        for n in range(6):
            results[5][n : n + 1, :] = jnp.sum(sums[n], axis=0, keepdims=True)
    for copy in (*go_h1, *go_cot, go_row, *go_h2, *go_dat, *go_c, *go_d):
        copy.wait_send()


def lay_out_kernel(cuts, whole, ada, tok, out, bias, *refs):
    (down, gate_up, qkv, wout, ada_to, tok_to, out_to, bias_to) = refs
    inner, head_cols, pad, own_cols = cuts
    ada_to[...] = ada[...]
    tok_to[...] = tok[...]
    out_to[...] = out[...]
    down[...] = whole[:, 0:inner]
    gate_up[:, 0, :] = whole[:, inner : 2 * inner]
    gate_up[:, 1, :] = whole[:, 2 * inner : 3 * inner]
    flat = whole[:, 3 * inner : 3 * inner + 3 * head_cols]
    for n in range(3):
        qkv[n] = flat[:, n * head_cols : (n + 1) * head_cols]
    start = whole.shape[1] - pad
    wout[...] = whole[:, start : start + head_cols]
    bias_to[...] = bias[0:1, 0:own_cols]


def lay_out(whole, ada, tok, out, bias, inner, head_cols, own_cols):
    rows = whole.shape[0]
    vmem = pl.BlockSpec(memory_space=pltpu.VMEM)
    pad = -(-head_cols // 128) * 128
    S = jax.ShapeDtypeStruct
    return pl.pallas_call(
        functools.partial(lay_out_kernel, (inner, head_cols, pad, own_cols)),
        out_shape=(
            S((rows, inner), F32), S((rows, 2, inner), F32), S((3, rows, head_cols), F32),
            S((rows, head_cols), F32), S(ada.shape, F32), S(tok.shape, F32), S(out.shape, BF16),
            S((1, own_cols), F32),
        ),
        in_specs=[vmem] * 5,
        out_specs=[vmem] * 8,
        compiler_params=pltpu.CompilerParams(vmem_limit_bytes=62 * 1024 * 1024),
    )(whole, ada, tok, out, bias)


def run_block(tok, cot, cond, grid, bias, wada, wqkv, wout, wgu, wdown):
    width = tok.shape[1]
    head_cols = wout.shape[0]
    heads = head_cols // HD
    inner = wdown.shape[0]
    strips = width // STRIP
    count = lax.axis_size("dp")
    sides = lax.axis_size("tensor")
    devices = count * sides
    own_cols = 6 * width // devices
    vmem = pl.BlockSpec(memory_space=pltpu.VMEM)
    hbm = pl.BlockSpec(memory_space=pl.ANY)
    V = pltpu.VMEM
    D = pltpu.SemaphoreType.DMA
    copies = 10 + 4 * strips
    fused = count == 16 and width % (8 * count) == 0 and 128 < own_cols <= 256 and own_cols % 8 == 0
    names = ["down", "gate", "up", "q", "k", "v", "out"]
    pad = -(-head_cols // 128) * 128
    if fused:
        rest_pad = -(-(3 * head_cols - 2 * pad - 128) // 128) * 128
        results = [
            jax.ShapeDtypeStruct((width // count, 3 * inner + 3 * pad + 128 + rest_pad), F32),
            jax.ShapeDtypeStruct((own_cols, width), F32),
            jax.ShapeDtypeStruct((1, width), F32),
            jax.ShapeDtypeStruct((8, 256), F32),
        ]
        result_specs = [hbm, hbm, vmem, vmem]
        chunk = width // count
        widths = [inner, inner, inner, pad + 128, pad, rest_pad, pad]
        extra = [
            V((width // 2, inner), BF16),
            V((width // 2, pad), BF16),
            V((width // 2, inner), BF16),
            V((chunk, inner), F32),
            D((len(names), 5)),
            D((len(names), 5)),
            D(()),
            pltpu.SemaphoreType.REGULAR,
            V((devices, 16, 128), BF16),
            V((devices, 16, 128), BF16),
            V((8, 6 * width + 128), F32),
            V((8, width // 2), F32),
            D((2,)),
            *[V((width // 4, w), BF16) for w in widths],
            *[V((width // 8, w), BF16) for w in widths],
            *[V((1, chunk, w), BF16) for w in widths],
            *[V((2, chunk, w), BF16) for w in widths],
        ]
        strides = [1, 2, 4, 8]
    else:
        wide = [inner, inner, inner, 3 * head_cols, head_cols]
        results = [jax.ShapeDtypeStruct((width, -(-w // TILE) * TILE), BF16) for w in wide]
        results += [jax.ShapeDtypeStruct((6, width), F32)]
        result_specs = [hbm] * 5 + [vmem]
        extra = [V((2, width, TILE), BF16), D((2,))]
        strides = []
    plan = {
        "fused": fused, "results": len(results), "count": count, "pieces": names,
        "devices": devices, "sides": sides, "own_cols": own_cols,
        "early": 8, "strides": strides, "orders": ((1, 2, 4, 8), (1, 4, 2, 8)),
    }
    return pl.pallas_call(
        functools.partial(block_kernel, plan),
        out_shape=(
            jax.ShapeDtypeStruct((LEN, width), BF16),
            jax.ShapeDtypeStruct((LEN, width), F32),
            *results,
        ),
        in_specs=[vmem] * 3 + [pl.BlockSpec(memory_space=pltpu.SMEM), vmem] + [hbm] * 5,
        out_specs=[vmem] * 2 + result_specs,
        scratch_shapes=[
            V((8, width), F32), V((2, 16, width // 2), BF16), V((2, HD, LEN), F32),
            V((2, HD, LEN), F32), V((3, 48, 2, inner), BF16),
                        V(wqkv.shape, BF16), V(wout.shape, BF16), V((width, inner), BF16),
            V((width, inner), BF16), V(wdown.shape, BF16),
            *[V((2, LEN, width), BF16)] * 4,
            *[V((2 * heads, HD, LEN), BF16)] * 3,
            V((2 * heads, LEN, LEN), F32),
            V((3 * head_cols, LEN), F32),
            V((head_cols, LEN), F32),
            V((2, head_cols, LEN), BF16),
            *[V((2, LEN, inner), BF16)] * 3,
            V((2, 3 * head_cols, LEN), BF16),
            *[V((LEN, width), F32)] * 3,
            *[V((LEN, width), BF16)] * 4,
            *[V((8, width), F32)] * 2,
            V((width, 2 * LEN), BF16),
            V((6, 8, width), F32),
            D((6,)),
            D((8,)),
            D((copies,)),
            D((copies,)),
            *extra,
        ],
        compiler_params=pltpu.CompilerParams(
            collective_id=0, has_side_effects=True, vmem_limit_bytes=62 * 1024 * 1024
        ),
    )(tok, cot, cond, grid, bias, wada, wqkv, wout, wgu, wdown)


def sum_over_images(partial):
    count = lax.axis_size("dp")
    me = lax.axis_index("dp")
    held = partial.reshape(count, partial.shape[0] // count, partial.shape[1])
    stride = 1
    left = count
    while left > 1:
        bit = (me // stride) % 2
        pairs = held.reshape(left // 2, 2, *held.shape[1:])
        keep = lax.dynamic_index_in_dim(pairs, bit, 1, keepdims=False)
        send = lax.dynamic_index_in_dim(pairs, 1 - bit, 1, keepdims=False)
        came = lax.ppermute(send, "dp", [(i, i ^ stride) for i in range(count)])
        held = keep.astype(F32) + came.astype(F32)
        left //= 2
        stride *= 2
        if left > 1:
            held = held.astype(BF16)
    return held[0]


def body(tokens, condition, grid_shape, w_ada, b_ada, w_qkv, w_out, w_gate_up, w_down, cotangent):
    width = tokens.shape[1]
    inner = w_down.shape[0]
    head_cols = w_out.shape[0]
    wqkv = w_qkv.transpose(1, 2, 0).reshape(3 * head_cols, width)
    layer_out, d_tokens, *grads = run_block(
        tokens, cotangent, condition, grid_shape, b_ada.reshape(-1, 128), w_ada, wqkv, w_out,
        w_gate_up, w_down,
    )
    devices_all = lax.axis_size("dp") * lax.axis_size("tensor")
    own_cols = 6 * width // devices_all
    if len(grads) == 4:
        whole, ada, d_condition, bias_rows = grads
        down, gate_up, qkv, g_out, ada, d_tokens, layer_out, bias_part = lay_out(
            whole, ada, d_tokens, layer_out, bias_rows, inner, head_cols, own_cols
        )
        grad_down, grad_gate_up = down.T, gate_up
        grad_qkv, grad_out = qkv.transpose(1, 0, 2), g_out.T
        weight_part, bias_part = ada.T, bias_part.reshape(own_cols)
    else:
        grad_down = sum_over_images(grads[0]).T
        grad_gate_up = jnp.stack([sum_over_images(grads[1]), sum_over_images(grads[2])], axis=1)
        grad_qkv = sum_over_images(grads[3][:, : 3 * head_cols]).reshape(-1, 3, head_cols)
        grad_out = sum_over_images(grads[4][:, :head_cols]).T
        cond = condition.astype(F32)
        cond_sigmoid = jax.nn.sigmoid(cond)
        silu_cond = (cond * cond_sigmoid).astype(BF16)
        d_mod = grads[5].reshape(1, 6 * width).astype(BF16)
        d_condition = (
            dot(d_mod, w_ada, 1, 1) * cond_sigmoid * (1.0 + cond * (1.0 - cond_sigmoid))
        )
        packed = jnp.concatenate(
            [
                d_mod.reshape(devices_all, own_cols),
                jnp.broadcast_to(silu_cond, (devices_all, width)),
            ],
            axis=1,
        )
        packed = jnp.pad(packed, ((0, 0), (0, -packed.shape[1] % 128)))
        packed = lax.all_to_all(
            packed.reshape(devices_all, -1, 128), ("dp", "tensor"), 0, 0, tiled=True
        ).reshape(devices_all, -1)
        columns = packed[:, :own_cols]
        silu_rows = packed[:, own_cols : own_cols + width]
        weight_part = dot(silu_rows, columns, 0, 0)
        bias_part = jnp.sum(columns.astype(F32), axis=0)
    return (
        layer_out, d_tokens, d_condition, weight_part, bias_part,
        grad_qkv, grad_out, grad_gate_up, grad_down,
    )


def solution(mesh):
    placed = (
        P(("dp", "tensor"), None),
        P(("dp", "tensor"), None),
        P("dp", None),
        P(),
        P(),
        P(None, None, "tensor"),
        P("tensor", None),
        P(None, None, "tensor"),
        P("tensor", None),
        P(("dp", "tensor"), None),
    )
    return jax.shard_map(
        body,
        mesh=mesh,
        in_specs=placed,
        out_specs=(
            P(("dp", "tensor"), None),
            P(("dp", "tensor"), None),
            P(("dp", "tensor"), None),
            P(None, ("dp", "tensor")),
            P(("dp", "tensor")),
            P("dp", None, "tensor"),
            P("tensor", "dp"),
            P("dp", None, "tensor"),
            P("tensor", "dp"),
        ),
        check_vma=False,
    )
```

```python
import functools

import jax
import jax.numpy as jnp
from jax import lax
from jax.experimental import pallas as pl
from jax.experimental.pallas import tpu as pltpu
from jax.sharding import PartitionSpec as P

HD = 72
LEN = 256
EPSILON = 1e-06
MESH = pl.DeviceIdType.MESH
F32 = jnp.float32
BF16 = jnp.bfloat16
ROWS = 32
STRIP = 384
TILE = 256


def dot(left, right, left_dim, right_dim):
    return lax.dot_general(
        left, right, (((left_dim,), (right_dim,)), ((), ())), preferred_element_type=F32
    )


def normed(values):
    centered = values - jnp.mean(values, axis=-1, keepdims=True)
    variance = jnp.mean(centered * centered, axis=-1, keepdims=True)
    inverse = lax.rsqrt(variance + EPSILON)
    return centered * inverse, inverse


def norm_back(upstream, norm, inverse):
    mean_grad = jnp.mean(upstream, axis=-1, keepdims=True)
    mean_cross = jnp.mean(upstream * norm, axis=-1, keepdims=True)
    return inverse * (upstream - mean_grad - norm * mean_cross)


def rotate_rows(values):
    quarter = HD // 4
    a, b = values[:quarter], values[quarter : 2 * quarter]
    c, d = values[2 * quarter : 3 * quarter], values[3 * quarter :]
    return jnp.concatenate([-b, a, -d, c], axis=0)


def fold(values):
    return jnp.sum(values.reshape(values.shape[0] // 8, 8, values.shape[1]), axis=0)


class Several:
    def __init__(self, copies):
        self.copies = copies

    def wait_send(self):
        for copy in self.copies:
            copy.wait_send()

    def wait_recv(self):
        for copy in self.copies:
            copy.wait_recv()


def block_kernel(
    plan, tok, cot, cond, grid, bias,
    wada_hbm, wqkv_hbm, wout_hbm, wgu_hbm, wdown_hbm,
    out, dtok, *rest,
):
    results, rest = rest[: plan["results"]], rest[plan["results"] :]
    (
        mod, silu_two, cos_t, sin_t, raw,
        wqkv, wout, wg, wu, wdown,
        h1, h2, dml, dat,
        q_s, k_s, v_s, p_s, qkv_f, a_f, a_t,
        hid, dgate, dup, dqkv,
        attn, dx1, own,
        send_a, send_c, recv_a, recv_c, row_out, row_in,
        flip, sums,
        wsem, asem, ssem, rsem, *extra,
    ) = rest
    width = tok.shape[1]
    heads = q_s.shape[0] // 2
    head_cols = heads * HD
    inner = wdown.shape[0]
    side = lax.axis_index("tensor")
    mate = {"tensor": 1 - side}
    scale = HD ** (-0.5)

    loads = [
        pltpu.make_async_copy(src, dst, wsem.at[i])
        for i, (src, dst) in enumerate(
            ((wqkv_hbm, wqkv), (wout_hbm, wout), (wdown_hbm, wdown))
        )
    ]
    half_rows = width // 2
    slots = [
        ref.at[pl.ds(n * half_rows, half_rows), pl.ds(0, width)] for ref in (wg, wu) for n in range(2)
    ]

    class Stream:
        def __init__(self, blocks, slots):
            self.chunks = [(b, h) for b in blocks for h in range(2)]
            self.slots = slots
            self.copies = []
            self.at = 0

        def fill(self, most):
            while len(self.copies) < min(most, len(self.chunks), self.at + len(self.slots)):
                n = len(self.copies)
                b, h = self.chunks[n]
                copy = pltpu.make_async_copy(
                    wada_hbm.at[pl.ds(h * half_rows, half_rows), pl.ds(b * width, width)],
                    self.slots[n % len(self.slots)], asem.at[n % len(self.slots)],
                )
                copy.start()
                self.copies.append(copy)

        def take(self):
            n = self.at
            self.copies[n].wait()
            b, h = self.chunks[n]
            self.at += 1
            return b, h, self.slots[n % len(self.slots)]

    stream = Stream((0, 1, 5, 2, 3, 4), slots)
    stream.fill(4)

    me = lax.axis_index("dp")

    def bit_of(stride):
        return lax.rem(lax.div(me, stride), 2)

    def partner(stride):
        return {"dp": me + stride - 2 * stride * bit_of(stride)}

    barrier = pltpu.get_barrier_semaphore()
    friends = [mate] + [partner(s) for s in plan["strides"]]
    for friend in friends:
        pl.semaphore_signal(barrier, inc=1, device_id=friend, device_id_type=MESH)

    def give(src, dst, slot):
        return pltpu.make_async_remote_copy(
            src_ref=src, dst_ref=dst, send_sem=ssem.at[slot], recv_sem=rsem.at[slot],
            device_id=mate, device_id_type=MESH,
        )

    def gather(buf, slot):
        half = LEN // 2
        return [
            give(buf.at[0, pl.ds(c * half, half)], buf.at[1, pl.ds(c * half, half)], slot + c)
            for c in range(2)
        ]

    strips = width // STRIP

    def scatter(send, recv, slot):
        return [
            give(
                send.at[:, pl.ds(c * STRIP, STRIP)], recv.at[:, pl.ds(c * STRIP, STRIP)], slot + c
            )
            for c in range(strips)
        ]

    go_h1, go_h2, go_dat = (gather(b, 2 * i) for i, b in enumerate((h1, h2, dat)))
    go_cot = [
        give(cot.at[pl.ds(at, size)], dml.at[1, pl.ds(at, size)], slot)
        for at, size, slot in ((0, 96, 6), (96, 96, 7), (192, 64, 9 + 4 * (width // STRIP)))
    ]
    go_row = give(row_out, row_in, 8 + 4 * (width // STRIP))
    go_a, go_b, go_c, go_d = (
        scatter(s, r, 8 + strips * i)
        for i, (s, r) in enumerate(
            ((send_a, recv_a), (send_a, recv_a), (send_c, recv_c), (send_a, recv_a))
        )
    )

    def rows_loop(step, copies=None):
        half = LEN // 2
        count = half // ROWS
        for c in range(2):
            def one(i, carry, c=c):
                step(pl.ds(pl.multiple_of(c * half + i * ROWS, ROWS), ROWS))
                return carry
            lax.fori_loop(0, count, one, 0)
            if copies is not None:
                copies[c].start()

    cond_f = cond[...].astype(F32)
    cond_sig = jax.nn.sigmoid(cond_f)
    silu = (cond_f * cond_sig).astype(BF16)
    silu_rows = jnp.broadcast_to(silu.astype(F32), (16, width))
    for h in range(2):
        silu_two[h] = silu_rows[:, h * half_rows : (h + 1) * half_rows].astype(BF16)

    bias_f = bias[...].astype(F32)
    tiles = width // bias.shape[1]

    def bias_row(b):
        return jnp.concatenate([bias_f[b * tiles + n : b * tiles + n + 1] for n in range(tiles)], axis=1)

    def modulate(count):
        for _ in range(count):
            row = None
            for _ in range(2):
                b, h, slot = stream.take()
                part = dot(silu_two[h], slot[...], 1, 0)[0:1]
                row = part if row is None else row + part
                stream.fill(99)
            mod[b : b + 1, :] = row + bias_row(b)

    def pre_norm(rows):
        norm, _ = normed(tok[rows, :].astype(F32))
        dx1[rows, :] = norm

    rows_loop(pre_norm)
    pl.semaphore_wait(barrier, len(friends))
    go_cot[0].start()
    modulate(2)
    for load in loads:
        load.start()
    shift_one, scale_one = mod[0:1], mod[1:2]

    def first_norm(rows):
        h1[0, rows, :] = (dx1[rows, :] * (1.0 + scale_one) + shift_one).astype(BF16)

    rows_loop(first_norm, go_h1)
    modulate(1)
    gate_two = mod[5:6]
    row_out[...] = jnp.broadcast_to(gate_two, row_out.shape)
    go_row.start()
    go_cot[1].start()
    sums[...] = jnp.zeros_like(sums)

    quarter = HD // 4
    limits = []
    for image in range(2):
        at = side if image == 0 else 1 - side
        tall, wide = grid[at, 0], grid[at, 1]
        limits.append(tall * wide)
        spot = lax.broadcasted_iota(jnp.int32, (1, LEN), 1).astype(F32)
        wide_f = jnp.full((1, LEN), wide, jnp.int32).astype(F32)
        row_at = jnp.floor((spot + 0.5) / wide_f)
        col_at = spot - row_at * wide_f
        step = lax.broadcasted_iota(jnp.int32, (quarter, LEN), 0).astype(F32)
        frequency = jnp.exp(step * (-9.210340371976184 / quarter))
        both = jnp.concatenate([row_at * frequency, col_at * frequency], axis=0)
        for table, turn in ((cos_t, jnp.cos), (sin_t, jnp.sin)):
            seen = turn(both)
            first, second = seen[:quarter], seen[quarter:]
            table[image] = jnp.concatenate([first, first, second, second], axis=0)

    depth = raw.shape[1]
    ring = raw.shape[0]
    parts = {"next": 0, "copies": []}
    r = lax.broadcasted_iota(jnp.int32, (2 * depth, 2 * depth), 0)
    c = lax.broadcasted_iota(jnp.int32, (2 * depth, 2 * depth), 1)
    sorter = jnp.where(c == jnp.where(r < depth, 2 * r, 2 * (r - depth) + 1), 1.0, 0.0).astype(BF16)

    def fetch(n):
        if n < width // depth:
            copy = pltpu.make_async_copy(
                wgu_hbm.at[pl.ds(n * depth, depth)], raw.at[n % ring], wsem.at[3 + n % ring]
            )
            copy.start()
            parts["copies"].append(copy)

    def pull_apart(until):
        while parts["next"] < until:
            n = parts["next"]
            parts["copies"][n].wait()
            parted = dot(sorter, raw[n % ring].reshape(2 * depth, inner), 1, 0).astype(BF16)
            wg[n * depth : (n + 1) * depth, :] = parted[:depth]
            wu[n * depth : (n + 1) * depth, :] = parted[depth:]
            fetch(n + ring)
            parts["next"] += 1

    def heads_forward(image):
        for part in range(3):
            qkv_f[part * head_cols : (part + 1) * head_cols, :] = dot(
                wqkv[part * head_cols : (part + 1) * head_cols, :], h1[image], 1, 1
            )
        cosine, sine = cos_t[image], sin_t[image]
        ok = lax.broadcasted_iota(jnp.int32, (LEN, LEN), 0) < limits[image]

        def head(h, carry):
            at = image * heads + h
            rows = pl.ds(pl.multiple_of(h * HD, 8), HD)
            query = qkv_f[rows, :]
            key = qkv_f[pl.ds(pl.multiple_of(head_cols + h * HD, 8), HD), :]
            value = qkv_f[pl.ds(pl.multiple_of(2 * head_cols + h * HD, 8), HD), :].astype(BF16)
            query = ((query * cosine + rotate_rows(query) * sine) * scale).astype(BF16)
            key = (key * cosine + rotate_rows(key) * sine).astype(BF16)
            q_s[at], k_s[at], v_s[at] = query, key, value
            scores = dot(key, query, 0, 0)
            scores = jnp.where(ok, scores, -1e30)
            top = jnp.max(scores, axis=0, keepdims=True)
            exps = jnp.exp(scores - top)
            probs = exps * (1.0 / jnp.sum(exps, axis=0, keepdims=True))
            p_s[at] = probs
            a_f[rows, :] = dot(value, probs.astype(BF16), 1, 0)
            return carry

        lax.fori_loop(0, heads, head, 0)
        a_t[image] = a_f[...].astype(BF16)

    def strips_of(make, send=None, copies=None, keep=None):
        for c in range(strips):
            cols = slice(c * STRIP, (c + 1) * STRIP)
            value = make(cols)
            if send is not None:
                send[:, cols] = value.astype(BF16)
                copies[c].start()
            else:
                keep[:, cols] = value

    for n in range(ring):
        fetch(n)
    loads[0].wait()
    heads_forward(0)
    modulate(3)
    pull_apart(plan["early"])
    gate_one, shift_two, scale_two = mod[2:3], mod[3:4], mod[4:5]
    for copy in go_h1:
        copy.wait_recv()
    heads_forward(1)
    loads[1].wait()
    strips_of(lambda cols: dot(a_t[1], wout[:, cols], 0, 0), send_a, go_a)
    go_cot[2].start()
    strips_of(lambda cols: dot(a_t[0], wout[:, cols], 0, 0), keep=own)

    gate_two_row = gate_two

    def mlp_grad(rows):
        dml[0, rows, :] = (gate_two_row * cot[rows, :].astype(F32)).astype(BF16)

    rows_loop(mlp_grad)
    pull_apart(width // depth)
    for copy in go_a:
        copy.wait_recv()

    def second_norm(rows):
        branch = own[rows, :] + recv_a[rows, :].astype(F32)
        attn[rows, :] = branch
        middle = tok[rows, :].astype(F32) + gate_one * branch
        norm, _ = normed(middle)
        h2[0, rows, :] = (norm * (1.0 + scale_two) + shift_two).astype(BF16)

    rows_loop(second_norm, go_h2)

    def turned(left, order):
        for image in range(2):
            flat = left[image].astype(F32).T
            chunk = width // plan["count"]
            for pair in range(plan["count"] // 2):
                place = [2 * pair, 2 * pair + 1]
                parts = []
                for spot in place:
                    which = 0
                    for level, stride in enumerate(order):
                        which += stride * ((spot >> (len(order) - 1 - level)) & 1)
                    parts.append(flat[which * chunk : (which + 1) * chunk])
                flip[2 * pair * chunk : 2 * (pair + 1) * chunk, image * LEN : (image + 1) * LEN] = (
                    jnp.concatenate(parts, axis=0).astype(BF16)
                )

    loads[2].wait()

    def feed_forward(image):
        def tile(j, carry):
            cols = pl.ds(pl.multiple_of(j * TILE, TILE), TILE)
            gate = dot(h2[image], wg[:, cols], 1, 0)
            up = dot(h2[image], wu[:, cols], 1, 0)
            grad = dot(dml[image], wdown[cols, :], 1, 1)
            sig = jax.nn.sigmoid(gate)
            act = gate * sig
            hid[image, :, cols] = (act * up).astype(BF16)
            dgate[image, :, cols] = (grad * up * sig * (1.0 + gate * (1.0 - sig))).astype(BF16)
            dup[image, :, cols] = (grad * act).astype(BF16)
            return carry

        lax.fori_loop(0, inner // TILE, tile, 0)

    def dh2_strip(image):
        return lambda cols: dot(dgate[image], wg[cols, :], 1, 1) + dot(dup[image], wu[cols, :], 1, 1)

    feed_forward(0)
    strips_of(dh2_strip(0), keep=own)
    for copy in go_cot:
        copy.wait_recv()
    go_row.wait_recv()
    gate_mate = row_in[0:1]

    def mate_grad(rows):
        dml[1, rows, :] = (gate_mate * dml[1, rows, :].astype(F32)).astype(BF16)

    rows_loop(mate_grad)
    if plan["fused"]:
        turned(dml, plan["orders"][0])
    for copy in go_h2:
        copy.wait_recv()
    feed_forward(1)

    def mlp_strip(image):
        return lambda cols: dot(hid[image], wdown[:, cols], 1, 0)

    for copy in go_a:
        copy.wait_send()
    strips_of(dh2_strip(1), send_a, go_b)

    if plan["fused"]:
        (
            give_one, keep_out, land0, final, gsend, grecv, osem, credit, packs, came, dflat, dcond, psem,
            *spots,
        ) = extra
        _, ada_out, cond_out, bias_out = results
        dflat[...] = jnp.zeros_like(dflat)
        dcond[...] = jnp.zeros_like(dcond)
        many = len(plan["pieces"])
        land1, land2, land3, held3 = (spots[n * many : (n + 1) * many] for n in range(4))
        half = width // 2
        gives = [wu.at[pl.ds(half, half)], give_one]
        core_bit = bit_of(1)
        state = {"gives": 0, "lands": 0}

        class Piece:
            def __init__(self, name, order, columns, padded, keep, offset, result, at):
                self.name, self.order, self.columns, self.padded = name, order, columns, padded
                self.keep, self.offset, self.result, self.at = keep, offset, result, at
                self.index = plan["pieces"].index(name)
                self.lanes = pl.ds(offset, padded)
                self.copies = {}

            def send(self, level, src, dst):
                copy = pltpu.make_async_remote_copy(
                    src_ref=src, dst_ref=dst, send_sem=gsend.at[self.index, level],
                    recv_sem=grecv.at[self.index, level], device_id=partner(self.order[level]),
                    device_id_type=MESH,
                )
                copy.start()
                self.copies[level] = copy

            def compute(self, right, give, cuts=0):
                self.give = gives[give]
                step = STRIP

                def tile(start, size, pad):
                    total = right(start, size)
                    low, high = total[:half], total[half:]
                    kept = jnp.where(core_bit == 0, low, high).astype(BF16)
                    gone = jnp.where(core_bit == 0, high, low).astype(BF16)
                    place = self.offset + start
                    if pad > size:
                        blank = jnp.zeros((half, pad - size), BF16)
                        kept = jnp.concatenate([kept, blank], axis=1)
                        gone = jnp.concatenate([gone, blank], axis=1)
                    if not isinstance(start, int):
                        place = pl.multiple_of(place, 128)
                        start = pl.multiple_of(start, 128)
                    self.keep[:, pl.ds(place, pad)] = kept
                    self.give[:, pl.ds(start, pad)] = gone

                whole = self.columns // step

                def one(n, carry):
                    tile(n * step, step, step)
                    return carry

                if cuts:
                    copies = []
                    for n in range(cuts):
                        part = whole // cuts
                        lax.fori_loop(n * part, (n + 1) * part, one, 0)
                        if n == 0:
                            pl.semaphore_wait(credit, 1)
                        lanes = pl.ds(n * part * step, part * step)
                        copy = pltpu.make_async_remote_copy(
                            src_ref=self.give.at[:, lanes], dst_ref=land0.at[:, lanes],
                            send_sem=gsend.at[self.index, 4 * n], recv_sem=grecv.at[self.index, 4 * n],
                            device_id=partner(1), device_id_type=MESH,
                        )
                        copy.start()
                        copies.append(copy)
                    self.copies[0] = Several(copies)
                    return
                lax.fori_loop(0, whole, one, 0)
                left = self.columns - whole * step
                if left:
                    tile(whole * step, left, self.padded - whole * step)

            def go(self):
                pl.semaphore_wait(credit, 1)
                self.send(0, self.give.at[:, pl.ds(0, self.padded)], land0.at[:, pl.ds(0, self.padded)])

            def add(self, level):
                rows = half >> level
                base = 0
                for before in range(1, level + 1):
                    base = base + bit_of(self.order[before]) * (half >> before)
                self.copies[level].wait_recv()
                cut = pl.ds(0, self.padded)
                if level == 0:
                    source = land0
                elif level == 1:
                    source = land1[self.index]
                elif level == 2:
                    source = land2[self.index]
                if level < 2:
                    block = 48

                    def one(n, carry):
                        there = pl.ds(pl.multiple_of(n * block, 16), block)
                        here = pl.ds(pl.multiple_of(base + n * block, 16), block)
                        self.keep[here, self.lanes] = (
                            self.keep[here, self.lanes].astype(F32) + source[there, cut].astype(F32)
                        ).astype(BF16)
                        return carry

                    lax.fori_loop(0, rows // block, one, 0)
                    if level == 0:
                        pl.semaphore_signal(
                            credit, inc=1, device_id=partner(1), device_id_type=MESH
                        )
                    quarter = rows // 2
                    off = pl.multiple_of(base + (1 - bit_of(self.order[level + 1])) * quarter, 16)
                    target = (land1, land2)[level][self.index]
                    self.send(level + 1, self.keep.at[pl.ds(off, quarter), self.lanes], target)
                elif level == 2:
                    here = pl.ds(pl.multiple_of(base, 16), rows)
                    total = self.keep[here, self.lanes].astype(F32) + source[:, cut].astype(F32)
                    held3[self.index][0] = total[: rows // 2].astype(BF16)
                    held3[self.index][1] = total[rows // 2 :].astype(BF16)
                    bit = bit_of(self.order[3])
                    self.send(3, held3[self.index].at[1 - bit], land3[self.index].at[0])
                else:
                    bit = bit_of(self.order[3])
                    if state.get("final") is not None:
                        state["final"].wait()
                    final[:, cut] = held3[self.index][bit].astype(F32) + land3[self.index][
                        0
                    ].astype(F32)
                    copy = pltpu.make_async_copy(
                        final.at[:, cut], self.result.at[:, pl.ds(self.at, self.padded)], osem
                    )
                    copy.start()
                    state["final"] = copy

            def close(self):
                for copy in self.copies.values():
                    copy.wait_send()

        pl.semaphore_signal(credit, inc=1, device_id=partner(1), device_id_type=MESH)
        y_first, z_first = plan["orders"]
        low, high = wg.at[pl.ds(0, half)], wg.at[pl.ds(half, half)]
        third = [wqkv.at[pl.ds(n * half, half)] for n in range(3)]
        p_down = Piece("down", y_first, inner, inner, low, 0, results[0], 0)
        p_gate = Piece("gate", z_first, inner, inner, high, 0, results[0], inner)
        p_up = Piece("up", y_first, inner, inner, wu.at[pl.ds(0, half)], 0, results[0], 2 * inner)
        pad = -(-head_cols // 128) * 128
        rest = 3 * head_cols - 2 * pad
        rest_pad = -(-rest // 128) * 128
        small = [
            Piece(name, y_first, columns, padded, place, 0, results[0], 3 * inner + at)
            for name, columns, padded, place, at in (
                ("q", pad, pad, third[0], 0),
                ("k", pad, pad, third[1], pad),
                ("v", rest, rest_pad, third[2], 2 * pad),
                ("out", head_cols, pad, keep_out, 2 * pad + rest_pad),
            )
        ]
        p_q, p_k, p_v, p_out = small

        tail = Stream(
            (3, 4, 2, 5, 0, 1), [wdown.at[pl.ds(n * half, half)] for n in range(2)] + [wout]
        )
        devices = plan["devices"]
        side_count = plan["sides"]
        mine = me * side_count + side
        own_cols = plan["own_cols"]

        def condition_back(blocks):
            for block in blocks:
                row = jnp.sum(sums[block], axis=0, keepdims=True)
                dflat[0:1, block * width : (block + 1) * width] = row
                rows = jnp.broadcast_to(row, (16, width)).astype(BF16)
                for _ in range(2):
                    b, h, slot = tail.take()
                    dcond[h : h + 1, :] += dot(rows, slot[...], 1, 1)[0:1]
                    tail.fill(99)

        def share_out():
            lanes = lax.broadcasted_iota(jnp.int32, (16, 128), 0)
            base = jnp.zeros((16, 128), F32)
            silu_f = silu.astype(F32)
            for n in range(width // 128):
                base = jnp.where(lanes == n, silu_f[:, n * 128 : (n + 1) * 128], base)
            row_a = width // 128
            for n in range(devices):
                first = dflat[0:1, n * own_cols : n * own_cols + 128]
                rest = own_cols - 128
                second = dflat[0:1, n * own_cols + 128 : n * own_cols + 256]
                packet = jnp.where(lanes == row_a, first, base)
                packet = jnp.where(lanes == row_a + 1, second, packet)
                packs[n] = packet.astype(BF16)

            def one(n, carry):
                other = lax.rem(mine + n, devices)
                pltpu.make_async_remote_copy(
                    src_ref=packs.at[other], dst_ref=came.at[mine], send_sem=psem.at[0],
                    recv_sem=psem.at[1],
                    device_id={
                        "dp": lax.div(other, side_count), "tensor": lax.rem(other, side_count)
                    },
                    device_id_type=MESH,
                ).start()
                return carry

            lax.fori_loop(1, devices, one, 0)
            came[mine] = packs[mine]

        def take_in():
            every = pl.ds(0, devices - 1)
            whole = pltpu.make_async_remote_copy(
                src_ref=packs.at[every], dst_ref=came.at[every], send_sem=psem.at[0],
                recv_sem=psem.at[1], device_id=mate, device_id_type=MESH,
            )
            whole.wait_send()
            whole.wait_recv()
            seen = came[...].astype(F32)
            row_a = width // 128
            silu_all = jnp.concatenate([seen[:, n, :] for n in range(row_a)], axis=1).astype(BF16)
            columns = jnp.concatenate([seen[:, row_a, :], seen[:, row_a + 1, :]], axis=1)
            bias_out[...] = jnp.broadcast_to(jnp.sum(columns, axis=0, keepdims=True), bias_out.shape)
            own[...] = dot(columns.astype(BF16), silu_all, 0, 0)
            copy = pltpu.make_async_copy(own.at[pl.ds(0, own_cols)], ada_out, asem.at[0])
            copy.start()
            copy.wait()
            slope = cond_sig * (1.0 + cond_f * (1.0 - cond_sig))
            whole_row = jnp.concatenate([dcond[0:1, :], dcond[1:2, :]], axis=1)
            cond_out[...] = whole_row * slope

    def lane_right(array):
        def right(start, size):
            if not isinstance(start, int):
                start = pl.multiple_of(start, 128)
            part = [array[i, :, pl.ds(start, size)] for i in range(2)]
            return dot(flip[:, 0:LEN], part[0], 1, 0) + dot(flip[:, LEN:], part[1], 1, 0)
        return right

    def row_right(array, base):
        def right(start, size):
            at = base + start
            if not isinstance(start, int):
                at = pl.multiple_of(at, 16)
            part = [array[i, pl.ds(at, size), :] for i in range(2)]
            return dot(flip[:, 0:LEN], part[0], 1, 1) + dot(flip[:, LEN:], part[1], 1, 1)
        return right

    def plain_grad(right, columns, target):
        (stage, gsem) = extra
        pend = {}
        for n, start in enumerate(range(0, columns, TILE)):
            size = min(TILE, columns - start)
            slot = n % 2
            if slot in pend:
                pend[slot].wait()
            stage[slot, :, 0:size] = right(start, size).astype(BF16)
            copy = pltpu.make_async_copy(
                stage.at[slot], target.at[:, pl.ds(start, TILE)], gsem.at[slot]
            )
            copy.start()
            pend[slot] = copy
        for copy in pend.values():
            copy.wait()

    def plain_grad_in(left, right, columns, target):
        for image in range(2):
            flip[:, image * LEN : (image + 1) * LEN] = left[image].astype(F32).T.astype(BF16)
        plain_grad(right, columns, target)

    if plan["fused"]:
        p_down.compute(lane_right(hid), 0, 2)
        turned(h2, p_gate.order)
        p_down.add(0)
        p_gate.compute(lane_right(dgate), 1, 1)
        p_gate.add(0)
    else:
        plain_grad_in(dml, lane_right(hid), inner, results[0])
        plain_grad_in(h2, lane_right(dgate), inner, results[1])
        plain_grad_in(h2, lane_right(dup), inner, results[2])

    for copy in go_b:
        copy.wait_recv()

    def second_back(rows):
        grad = own[rows, :] + recv_a[rows, :].astype(F32)
        norm, inverse = normed(tok[rows, :].astype(F32) + gate_one * attn[rows, :])
        middle = cot[rows, :].astype(F32) + norm_back(grad * (1.0 + scale_two), norm, inverse)
        dx1[rows, :] = middle
        dat[0, rows, :] = (gate_one * middle).astype(BF16)
        sums[2] += fold(middle * attn[rows, :])
        sums[3] += fold(grad)
        sums[4] += fold(grad * norm)

    rows_loop(second_back, go_dat)

    strips_of(mlp_strip(1), send_c, go_c)
    if plan["fused"]:
        p_down.copies[0].wait_send()
        turned(h2, p_up.order)
        p_up.compute(lane_right(dup), 0, 1)

    def heads_back(image):
        a_f[...] = dot(wout[...], dat[image], 1, 1)
        cosine, sine = cos_t[image], sin_t[image]

        def head(h, carry):
            at = image * heads + h
            rows = pl.ds(pl.multiple_of(h * HD, 8), HD)
            da = a_f[rows, :].astype(BF16)
            probs = p_s[at]
            query, key, value = q_s[at], k_s[at], v_s[at]
            dprobs = dot(value, da, 0, 0)
            dvalue = dot(da, probs.astype(BF16), 1, 1)
            inside = jnp.sum(probs * dprobs, axis=0, keepdims=True)
            dscores = (probs * (dprobs - inside)).astype(BF16)
            dquery = dot(key, dscores, 1, 0)
            dkey = dot(query, dscores, 1, 1)
            dquery = (dquery * cosine - rotate_rows(dquery * sine)) * scale
            dkey = dkey * cosine - rotate_rows(dkey * sine)
            qkv_f[rows, :] = dquery
            qkv_f[pl.ds(pl.multiple_of(head_cols + h * HD, 8), HD), :] = dkey
            qkv_f[pl.ds(pl.multiple_of(2 * head_cols + h * HD, 8), HD), :] = dvalue
            return carry

        lax.fori_loop(0, heads, head, 0)
        dqkv[image] = qkv_f[...].astype(BF16)

    heads_back(0)
    if plan["fused"]:
        p_up.add(0)
        p_down.add(1)
    for copy in go_dat:
        copy.wait_recv()
    heads_back(1)

    def dh1_strip(image):
        return lambda cols: dot(dqkv[image], wqkv[:, cols], 0, 0)

    for copy in go_b:
        copy.wait_send()
    strips_of(dh1_strip(1), send_a, go_d)
    strips_of(dh1_strip(0), keep=own)

    if plan["fused"]:
        p_gate.copies[0].wait_send()
        p_up.copies[0].wait_send()
        p_gate.add(1)
        turned(dat, p_out.order)
        p_out.compute(row_right(a_t, 0), 0)
        p_out.go()
        turned(h1, p_q.order)
        p_q.compute(row_right(dqkv, 0), 1)
        p_out.add(0)
        p_q.go()
        p_out.copies[0].wait_send()
        p_k.compute(row_right(dqkv, pad), 0)
        p_q.add(0)
        p_k.go()
        p_down.add(2)
        p_q.copies[0].wait_send()
        p_v.compute(row_right(dqkv, 2 * pad), 1)
        p_k.add(0)
        p_v.go()
        p_up.add(1)
        p_v.add(0)
    else:
        plain_grad_in(h1, row_right(dqkv, 0), 3 * head_cols, results[3])
        plain_grad_in(dat, row_right(a_t, 0), head_cols, results[4])

    pieces = [(n, min(LEN, width - n)) for n in range(0, width, LEN)]
    for n, size in pieces:
        p_s[n // LEN, :, 0:size] = dot(hid[0], wdown[:, n : n + size], 1, 0)
    for copy in go_c:
        copy.wait_recv()

    def finish(rows):
        mine_part = [p_s[n // LEN, rows, 0:size] for n, size in pieces]
        branch = jnp.concatenate(mine_part, axis=1) + recv_c[rows, :].astype(F32)
        out[rows, :] = (
            tok[rows, :].astype(F32) + gate_one * attn[rows, :] + gate_two * branch
        ).astype(BF16)
        sums[5] += fold(cot[rows, :].astype(F32) * branch)

    rows_loop(finish)
    if plan["fused"]:
        tail.fill(99)
        condition_back((3, 4))
    for copy in go_d:
        copy.wait_recv()

    def first_back(rows):
        grad = own[rows, :] + recv_a[rows, :].astype(F32)
        norm, inverse = normed(tok[rows, :].astype(F32))
        dtok[rows, :] = dx1[rows, :] + norm_back(grad * (1.0 + scale_one), norm, inverse)
        sums[0] += fold(grad)
        sums[1] += fold(grad * norm)

    rows_loop(first_back)

    if plan["fused"]:
        p_gate.add(2)
        p_up.add(2)
        condition_back((2, 5))
        p_down.add(3)
        p_out.add(1)
        condition_back((0, 1))
        share_out()
        p_q.add(1)
        p_out.add(2)
        p_gate.add(3)
        p_up.add(3)
        p_k.add(1)
        p_q.add(2)
        p_out.add(3)
        p_v.add(1)
        p_k.add(2)
        p_q.add(3)
        take_in()
        p_v.add(2)
        p_k.add(3)
        p_v.add(3)
        state["final"].wait()
        pl.semaphore_wait(credit, 1)
        for piece in (p_gate, p_up, p_down, *small):
            for level, copy in piece.copies.items():
                if level > 0 or piece in (p_k, p_v):
                    copy.wait_send()
    else:
        for n in range(6):
            results[5][n : n + 1, :] = jnp.sum(sums[n], axis=0, keepdims=True)
    for copy in (*go_h1, *go_cot, go_row, *go_h2, *go_dat, *go_c, *go_d):
        copy.wait_send()


def lay_out_kernel(cuts, whole, ada, tok, out, bias, *refs):
    (down, gate_up, qkv, wout, ada_to, tok_to, out_to, bias_to) = refs
    inner, head_cols, pad, own_cols = cuts
    ada_to[...] = ada[...]
    tok_to[...] = tok[...]
    out_to[...] = out[...]
    down[...] = whole[:, 0:inner]
    gate_up[:, 0, :] = whole[:, inner : 2 * inner]
    gate_up[:, 1, :] = whole[:, 2 * inner : 3 * inner]
    flat = whole[:, 3 * inner : 3 * inner + 3 * head_cols]
    for n in range(3):
        qkv[n] = flat[:, n * head_cols : (n + 1) * head_cols]
    start = whole.shape[1] - pad
    wout[...] = whole[:, start : start + head_cols]
    bias_to[...] = bias[0:1, 0:own_cols]


def lay_out(whole, ada, tok, out, bias, inner, head_cols, own_cols):
    rows = whole.shape[0]
    vmem = pl.BlockSpec(memory_space=pltpu.VMEM)
    pad = -(-head_cols // 128) * 128
    S = jax.ShapeDtypeStruct
    return pl.pallas_call(
        functools.partial(lay_out_kernel, (inner, head_cols, pad, own_cols)),
        out_shape=(
            S((rows, inner), F32), S((rows, 2, inner), F32), S((3, rows, head_cols), F32),
            S((rows, head_cols), F32), S(ada.shape, F32), S(tok.shape, F32), S(out.shape, BF16),
            S((1, own_cols), F32),
        ),
        in_specs=[vmem] * 5,
        out_specs=[vmem] * 8,
        compiler_params=pltpu.CompilerParams(vmem_limit_bytes=62 * 1024 * 1024),
    )(whole, ada, tok, out, bias)


def run_block(tok, cot, cond, grid, bias, wada, wqkv, wout, wgu, wdown):
    width = tok.shape[1]
    head_cols = wout.shape[0]
    heads = head_cols // HD
    inner = wdown.shape[0]
    strips = width // STRIP
    count = lax.axis_size("dp")
    sides = lax.axis_size("tensor")
    devices = count * sides
    own_cols = 6 * width // devices
    vmem = pl.BlockSpec(memory_space=pltpu.VMEM)
    hbm = pl.BlockSpec(memory_space=pl.ANY)
    V = pltpu.VMEM
    D = pltpu.SemaphoreType.DMA
    copies = 10 + 4 * strips
    fused = count == 16 and width % (8 * count) == 0 and 128 < own_cols <= 256 and own_cols % 8 == 0
    names = ["down", "gate", "up", "q", "k", "v", "out"]
    pad = -(-head_cols // 128) * 128
    if fused:
        rest_pad = -(-(3 * head_cols - 2 * pad) // 128) * 128
        results = [
            jax.ShapeDtypeStruct((width // count, 3 * inner + 3 * pad + rest_pad), F32),
            jax.ShapeDtypeStruct((own_cols, width), F32),
            jax.ShapeDtypeStruct((1, width), F32),
            jax.ShapeDtypeStruct((8, 256), F32),
        ]
        result_specs = [hbm, hbm, vmem, vmem]
        chunk = width // count
        widths = [inner, inner, inner, pad, pad, rest_pad, pad]
        extra = [
            V((width // 2, inner), BF16),
            V((width // 2, pad), BF16),
            V((width // 2, inner), BF16),
            V((chunk, inner), F32),
            D((len(names), 5)),
            D((len(names), 5)),
            D(()),
            pltpu.SemaphoreType.REGULAR,
            V((devices, 16, 128), BF16),
            V((devices, 16, 128), BF16),
            V((8, 6 * width + 128), F32),
            V((8, width // 2), F32),
            D((2,)),
            *[V((width // 4, w), BF16) for w in widths],
            *[V((width // 8, w), BF16) for w in widths],
            *[V((1, chunk, w), BF16) for w in widths],
            *[V((2, chunk, w), BF16) for w in widths],
        ]
        strides = [1, 2, 4, 8]
    else:
        wide = [inner, inner, inner, 3 * head_cols, head_cols]
        results = [jax.ShapeDtypeStruct((width, -(-w // TILE) * TILE), BF16) for w in wide]
        results += [jax.ShapeDtypeStruct((6, width), F32)]
        result_specs = [hbm] * 5 + [vmem]
        extra = [V((2, width, TILE), BF16), D((2,))]
        strides = []
    plan = {
        "fused": fused, "results": len(results), "count": count, "pieces": names,
        "devices": devices, "sides": sides, "own_cols": own_cols,
        "early": 8, "strides": strides, "orders": ((1, 2, 4, 8), (1, 4, 2, 8)),
    }
    return pl.pallas_call(
        functools.partial(block_kernel, plan),
        out_shape=(
            jax.ShapeDtypeStruct((LEN, width), BF16),
            jax.ShapeDtypeStruct((LEN, width), F32),
            *results,
        ),
        in_specs=[vmem] * 3 + [pl.BlockSpec(memory_space=pltpu.SMEM), vmem] + [hbm] * 5,
        out_specs=[vmem] * 2 + result_specs,
        scratch_shapes=[
            V((8, width), F32), V((2, 16, width // 2), BF16), V((2, HD, LEN), F32),
            V((2, HD, LEN), F32), V((3, 48, 2, inner), BF16),
                        V(wqkv.shape, BF16), V(wout.shape, BF16), V((width, inner), BF16),
            V((width, inner), BF16), V(wdown.shape, BF16),
            *[V((2, LEN, width), BF16)] * 4,
            *[V((2 * heads, HD, LEN), BF16)] * 3,
            V((2 * heads, LEN, LEN), F32),
            V((3 * head_cols, LEN), F32),
            V((head_cols, LEN), F32),
            V((2, head_cols, LEN), BF16),
            *[V((2, LEN, inner), BF16)] * 3,
            V((2, 3 * head_cols, LEN), BF16),
            *[V((LEN, width), F32)] * 3,
            *[V((LEN, width), BF16)] * 4,
            *[V((8, width), F32)] * 2,
            V((width, 2 * LEN), BF16),
            V((6, 8, width), F32),
            D((6,)),
            D((8,)),
            D((copies,)),
            D((copies,)),
            *extra,
        ],
        compiler_params=pltpu.CompilerParams(
            collective_id=0, has_side_effects=True, vmem_limit_bytes=62 * 1024 * 1024
        ),
    )(tok, cot, cond, grid, bias, wada, wqkv, wout, wgu, wdown)


def sum_over_images(partial):
    count = lax.axis_size("dp")
    me = lax.axis_index("dp")
    held = partial.reshape(count, partial.shape[0] // count, partial.shape[1])
    stride = 1
    left = count
    while left > 1:
        bit = (me // stride) % 2
        pairs = held.reshape(left // 2, 2, *held.shape[1:])
        keep = lax.dynamic_index_in_dim(pairs, bit, 1, keepdims=False)
        send = lax.dynamic_index_in_dim(pairs, 1 - bit, 1, keepdims=False)
        came = lax.ppermute(send, "dp", [(i, i ^ stride) for i in range(count)])
        held = keep.astype(F32) + came.astype(F32)
        left //= 2
        stride *= 2
        if left > 1:
            held = held.astype(BF16)
    return held[0]


def body(tokens, condition, grid_shape, w_ada, b_ada, w_qkv, w_out, w_gate_up, w_down, cotangent):
    width = tokens.shape[1]
    inner = w_down.shape[0]
    head_cols = w_out.shape[0]
    wqkv = w_qkv.transpose(1, 2, 0).reshape(3 * head_cols, width)
    layer_out, d_tokens, *grads = run_block(
        tokens, cotangent, condition, grid_shape, b_ada.reshape(-1, 128), w_ada, wqkv, w_out,
        w_gate_up, w_down,
    )
    devices_all = lax.axis_size("dp") * lax.axis_size("tensor")
    own_cols = 6 * width // devices_all
    if len(grads) == 4:
        whole, ada, d_condition, bias_rows = grads
        down, gate_up, qkv, g_out, ada, d_tokens, layer_out, bias_part = lay_out(
            whole, ada, d_tokens, layer_out, bias_rows, inner, head_cols, own_cols
        )
        grad_down, grad_gate_up = down.T, gate_up
        grad_qkv, grad_out = qkv.transpose(1, 0, 2), g_out.T
        weight_part, bias_part = ada.T, bias_part.reshape(own_cols)
    else:
        grad_down = sum_over_images(grads[0]).T
        grad_gate_up = jnp.stack([sum_over_images(grads[1]), sum_over_images(grads[2])], axis=1)
        grad_qkv = sum_over_images(grads[3][:, : 3 * head_cols]).reshape(-1, 3, head_cols)
        grad_out = sum_over_images(grads[4][:, :head_cols]).T
        cond = condition.astype(F32)
        cond_sigmoid = jax.nn.sigmoid(cond)
        silu_cond = (cond * cond_sigmoid).astype(BF16)
        d_mod = grads[5].reshape(1, 6 * width).astype(BF16)
        d_condition = (
            dot(d_mod, w_ada, 1, 1) * cond_sigmoid * (1.0 + cond * (1.0 - cond_sigmoid))
        )
        packed = jnp.concatenate(
            [
                d_mod.reshape(devices_all, own_cols),
                jnp.broadcast_to(silu_cond, (devices_all, width)),
            ],
            axis=1,
        )
        packed = jnp.pad(packed, ((0, 0), (0, -packed.shape[1] % 128)))
        packed = lax.all_to_all(
            packed.reshape(devices_all, -1, 128), ("dp", "tensor"), 0, 0, tiled=True
        ).reshape(devices_all, -1)
        columns = packed[:, :own_cols]
        silu_rows = packed[:, own_cols : own_cols + width]
        weight_part = dot(silu_rows, columns, 0, 0)
        bias_part = jnp.sum(columns.astype(F32), axis=0)
    return (
        layer_out, d_tokens, d_condition, weight_part, bias_part,
        grad_qkv, grad_out, grad_gate_up, grad_down,
    )


def solution(mesh):
    placed = (
        P(("dp", "tensor"), None),
        P(("dp", "tensor"), None),
        P("dp", None),
        P(),
        P(),
        P(None, None, "tensor"),
        P("tensor", None),
        P(None, None, "tensor"),
        P("tensor", None),
        P(("dp", "tensor"), None),
    )
    return jax.shard_map(
        body,
        mesh=mesh,
        in_specs=placed,
        out_specs=(
            P(("dp", "tensor"), None),
            P(("dp", "tensor"), None),
            P(("dp", "tensor"), None),
            P(None, ("dp", "tensor")),
            P(("dp", "tensor")),
            P("dp", None, "tensor"),
            P("tensor", "dp"),
            P("dp", None, "tensor"),
            P("tensor", "dp"),
        ),
        check_vma=False,
    )
```
